512 devices in a mesh: row: 16 (over z, core), col: 32 (over y, x).
Axes of the slice: x: 4, y: 8, z: 8, core: 2. Of those that a mesh axis runs over, the one named last changes fastest.
Arguments:
- rhs: bfloat16 [57344, 256], P('row', 'col'), may hold values from -6 to 6
- dinv: bfloat16 [224, 256, 256], P('row'), may hold values from -1 to 2.5, as said below
- blocks: bfloat16 [16, 448, 256, 256], P('row', 'col'), may hold values from -0.046875 to 0.046875
- block_row: int32 [16, 448], P('row', 'col'), may hold values from 0 to 14, as said below
- block_col: int32 [16, 448], P('row', 'col'), may hold values from 0 to 223, as said below
Outputs:
- solution: bfloat16 [57344, 256], P('row', 'col')
The draws below stay inside these ranges and needn't reach their ends.
Inputs may be any that keep to these rules, and one draw needn't show every extreme that they name: `dinv`: lower triangular with positive diagonal. `block_row`: slots at positions below 8 of a device hold level-1 row supernodes, the others level-2 ones; 14 marks an empty slot. Some device fills all its slots. `block_col`: A live slot's column supernode is congruent to the device's col index modulo 32 and has a lower level than its row supernode; no pair of supernodes is held twice. An empty slot holds the device's col index.
All inputs are finite; a program needn't handle non-finite values.
Results may differ from the reference program's by a relative error of at most 0.028.
Values may be sent and summed in bfloat16 or wider, within the bound.
No kernel may reach another device: no remote copies, remote signals or barrier semaphores. Data moves between devices by JAX's collectives and lax.ppermute only.
A program may use at most 64 MiB of HBM per device.

```python
import math
import jax
import jax.numpy as jnp
from jax import lax

SN = 256
RHS = 256
L0 = 8
L1 = 4
L2 = 2
SLOTS1 = 8
SLOTS2 = 6
OWN = 14
SLOTS = 14
NSUP = 224
N_ROW = 16
N_COL = 32


def slot_lists(key):
    key = jax.random.fold_in(key, 17)
    owned = L0 + L1 + L2
    total_sup = owned * N_ROW
    devices = N_ROW * N_COL
    ident = jnp.arange(total_sup, dtype=jnp.int32)
    local = ident % owned
    level = (local >= L0).astype(jnp.int32) + (local >= L0 + L1).astype(jnp.int32)
    klass = ident % N_COL
    device = jnp.arange(devices, dtype=jnp.int32)
    device_col = device % N_COL
    key_one, key_two = jax.random.split(key)

    def choose(subkey, first, count, slots):
        noise_key, want_key = jax.random.split(subkey)
        pairs = jnp.arange(count * total_sup, dtype=jnp.int32)
        row_local = first + pairs // total_sup
        column = pairs % total_sup
        row_level = (row_local >= L0).astype(jnp.int32) + (row_local >= L0 + L1).astype(jnp.int32)
        valid = (klass[column][None, :] == device_col[:, None]) & (level[column] < row_level)[None, :]
        noise = jax.random.randint(noise_key, (devices, count * total_sup), 0, 1024)
        score = valid.astype(jnp.int32) * 16777216 + noise * 8192 + pairs[None, :]
        picked = lax.top_k(score, slots)[1]
        picked_valid = jnp.take_along_axis(valid, picked, axis=1)
        wanted = jax.random.randint(want_key, (devices,), slots // 2, slots + 1)
        wanted = jnp.where(device % 3 == 0, slots, wanted)
        live = picked_valid & (jnp.arange(slots, dtype=jnp.int32)[None, :] < wanted[:, None])
        row_ids = jnp.where(live, first + picked // total_sup, owned)
        col_ids = jnp.where(live, picked % total_sup, device_col[:, None])
        return (row_ids.astype(jnp.int32), col_ids.astype(jnp.int32))
    rows_one, cols_one = choose(key_one, L0, L1, SLOTS1)
    rows_two, cols_two = choose(key_two, L0 + L1, L2, SLOTS2)
    row_all = jnp.concatenate([rows_one, rows_two], axis=1).reshape(N_ROW, N_COL * (SLOTS1 + SLOTS2))
    col_all = jnp.concatenate([cols_one, cols_two], axis=1).reshape(N_ROW, N_COL * (SLOTS1 + SLOTS2))
    return (row_all, col_all)


def draw_block_row(key, part):
    lists = slot_lists(key)
    return lists[0]


def draw_block_col(key, part):
    lists = slot_lists(key)
    return lists[1]


def draw_dinv(key, part):
    key = jax.random.fold_in(key, 3)
    key_diag, key_off = jax.random.split(key)
    total_sup = (L0 + L1 + L2) * N_ROW
    row_grid = lax.broadcasted_iota(jnp.int32, (SN, SN), 0)
    col_grid = lax.broadcasted_iota(jnp.int32, (SN, SN), 1)
    strict = (row_grid > col_grid).astype(jnp.float32)
    unit = (row_grid == col_grid).astype(jnp.float32)
    diagonal = jax.random.uniform(key_diag, (total_sup, SN, 1), minval=0.5, maxval=1.5)
    offdiag = jax.random.normal(key_off, (total_sup, SN, SN)) * (0.6 / math.sqrt(SN))
    return (unit * diagonal + strict * offdiag).astype(jnp.bfloat16)


def shard_levels(rng, extent, shards, least, top_value):
    gain, own = 1.0, jax.random.fold_in(rng, 6)
    for position, shards_of in shards:
        heights = jnp.exp(jax.random.uniform(jax.random.fold_in(own, position), (shards_of,), jnp.float32, least / len(shards), top_value / len(shards)))
        gain = gain * jnp.repeat(heights, extent[position] // shards_of).reshape([-1 if axis == position else 1 for axis in range(len(extent))])
    return gain


def normal_values(key, shape, deviation, bound, cuts=(), kind=jnp.bfloat16):
    entries = deviation * jax.random.normal(key, shape, jnp.float32)
    if cuts:
        entries = entries * shard_levels(key, shape, cuts, -0.22, 0.18)
    return jnp.clip(entries, -bound, bound).astype(kind)


def setup_inputs(seed: int = 0) -> dict:
    key_of = jax.random.split(jax.random.key(seed), 6)
    rhs = normal_values(key_of[0], (NSUP * SN, RHS), 1.0, 6.0, ((0, 16), (1, 32)))
    dinv = draw_dinv(jax.random.fold_in(key_of[5], 71), 0)
    blocks = normal_values(key_of[2], (N_ROW, N_COL * SLOTS, SN, SN), (SN * N_COL * 2) ** -0.5, 0.046875, ((0, 16), (1, 32)))
    block_row = draw_block_row(jax.random.fold_in(key_of[5], 71), 0)
    block_col = draw_block_col(jax.random.fold_in(key_of[5], 71), 0)
    return {"rhs": rhs, "dinv": dinv, "blocks": blocks, "block_row": block_row, "block_col": block_col}


def solve_rows(factor, vector):
    rounded = lax.optimization_barrier(vector.astype(jnp.bfloat16)).astype(jnp.float32)
    return jnp.einsum("rkab,rkbn->rkan", factor.astype(jnp.float32), rounded).astype(jnp.bfloat16)


def solve_cols(factor, vector):
    rounded = lax.optimization_barrier(vector.astype(jnp.bfloat16)).astype(jnp.float32)
    return jnp.einsum("rkab,rkan->rkbn", factor.astype(jnp.float32), rounded).astype(jnp.bfloat16)


def split_slots(blocks, block_row, block_col, first, final):
    tiles = blocks.reshape(N_ROW, N_COL, SLOTS, SN, SN)[:, :, first:final]
    row_list = block_row.reshape(N_ROW, N_COL, SLOTS)[:, :, first:final]
    col_list = block_col.reshape(N_ROW, N_COL, SLOTS)[:, :, first:final]
    return tiles.reshape(N_ROW, -1, SN, SN), row_list.reshape(N_ROW, -1), col_list.reshape(N_ROW, -1)


def level_sums(tiles, row_list, col_list, solved):
    def one_row(items):
        tile_part, row_part, col_part = items
        source = jnp.take(solved, col_part, axis=0).astype(jnp.float32)
        product = jnp.einsum("sab,sbn->san", tile_part.astype(jnp.float32), source)
        return jax.ops.segment_sum(product, row_part, num_segments=OWN + 1)[:OWN]
    return lax.map(one_row, (tiles, row_list, col_list))


def carry_sums(tiles, row_list, col_list, known):
    padded = jnp.concatenate([known, jnp.zeros((N_ROW, 1, SN, RHS), jnp.bfloat16)], axis=1)

    def one_row(total, items):
        tile_part, row_part, col_part, known_part = items
        chosen = jnp.take(known_part, row_part, axis=0).astype(jnp.float32)
        product = jnp.einsum("sab,san->sbn", tile_part.astype(jnp.float32), chosen)
        partial_sum = jax.ops.segment_sum(product, col_part, num_segments=NSUP)
        rounded = lax.optimization_barrier(partial_sum.astype(jnp.bfloat16)).astype(jnp.float32)
        return total + rounded, None

    total, ignored = lax.scan(one_row, jnp.zeros((NSUP, SN, RHS), jnp.float32), (tiles, row_list, col_list, padded))
    return total.reshape(N_ROW, OWN, SN, RHS)


def reference(rhs, dinv, blocks, block_row, block_col):
    middle = L0 + L1
    target = rhs.astype(jnp.float32).reshape(N_ROW, OWN, SN, RHS)
    factor = dinv.reshape(N_ROW, OWN, SN, SN)
    lower_set = split_slots(blocks, block_row, block_col, 0, SLOTS1)
    upper_set = split_slots(blocks, block_row, block_col, SLOTS1, SLOTS)
    all_set = tuple(jnp.concatenate([lower_set[i], upper_set[i]], axis=1) for i in range(3))
    zeros_low = jnp.zeros((N_ROW, L0, SN, RHS), jnp.bfloat16)
    zeros_mid = jnp.zeros((N_ROW, L1, SN, RHS), jnp.bfloat16)
    zeros_top = jnp.zeros((N_ROW, L2, SN, RHS), jnp.bfloat16)
    y_low = solve_rows(factor[:, :L0], target[:, :L0])
    solved = jnp.concatenate([y_low, zeros_mid, zeros_top], axis=1).reshape(NSUP, SN, RHS)
    sums_mid = level_sums(lower_set[0], lower_set[1], lower_set[2], solved)
    y_mid = solve_rows(factor[:, L0:middle], target[:, L0:middle] - sums_mid[:, L0:middle])
    solved = jnp.concatenate([y_low, y_mid, zeros_top], axis=1).reshape(NSUP, SN, RHS)
    sums_top = level_sums(upper_set[0], upper_set[1], upper_set[2], solved)
    y_top = solve_rows(factor[:, middle:], target[:, middle:] - sums_top[:, middle:])
    x_top = solve_cols(factor[:, middle:], y_top.astype(jnp.float32))
    known = jnp.concatenate([zeros_low, zeros_mid, x_top], axis=1)
    carry_top = carry_sums(upper_set[0], upper_set[1], upper_set[2], known)
    x_mid = solve_cols(factor[:, L0:middle], y_mid.astype(jnp.float32) - carry_top[:, L0:middle])
    known = jnp.concatenate([zeros_low, x_mid, x_top], axis=1)
    carry_low = carry_sums(all_set[0], all_set[1], all_set[2], known)
    x_low = solve_cols(factor[:, :L0], y_low.astype(jnp.float32) - carry_low[:, :L0])
    return jnp.concatenate([x_low, x_mid, x_top], axis=1).reshape(NSUP * SN, RHS)
```

```python
import jax
import jax.numpy as jnp
from jax import lax
from jax.experimental import pallas as pl
from jax.experimental.pallas import tpu as pltpu
from jax.sharding import PartitionSpec as P

SN = 256
L0 = 8
L1 = 4
L2 = 2
MID = L0 + L1
OWN = L0 + L1 + L2
SLOTS1 = 8
SLOTS = 14
R = 16
C = 32
Z = 8
W = 8
F32 = jnp.float32
BF16 = jnp.bfloat16
Z_GROUPS = [[2 * z + core for z in range(Z)] for core in range(2)]
CORE_GROUPS = [[2 * z, 2 * z + 1] for z in range(Z)]


def dot_nt(left, right):
    return lax.dot_general(left, right, (((1,), (1,)), ((), ())), preferred_element_type=F32)


def dot_nn(left, right):
    return lax.dot_general(left, right, (((1,), (0,)), ((), ())), preferred_element_type=F32)


def panel_of(column):
    k = column % OWN
    parity = column % (2 * OWN) // OWN
    return jnp.where(k < L0, 2 * parity + k // 4, 4 + parity)


def join(ref_value, index):
    rows = ref_value.shape[1]
    wide = ref_value.astype(F32).reshape(C, rows // W, W, SN)
    return wide[:, index].reshape(C * W, SN).astype(BF16)


def cut(panels):
    parts = [p.reshape(C, W, SN) for p in panels]
    return jnp.stack(parts, axis=1).reshape(C, W * len(parts), SN).astype(BF16)


def low_forward(rhs_ref, dinv_ref, y_ref, spread_ref):
    rows = []
    for k in range(L0):
        rows.append(dot_nt(rhs_ref[:, k * SN : (k + 1) * SN], dinv_ref[k]))
    y = jnp.concatenate(rows, axis=0).astype(BF16)
    y_ref[...] = y
    for z in range(Z):
        spread_ref[z] = y


def low_by_class(core_ref, in_ref, out_ref):
    core = core_ref[0]
    for c in range(C):
        halves = []
        for o in range(2):
            a = (c + 2 * core) % 4
            z = (7 * ((c - 14 * core - a - 4 * o + 64) // 4)) % Z
            tile = in_ref[z, 32 * o : 32 * o + 32].astype(F32)
            piece = jnp.where(a == 0, tile[0:8], tile[8:16])
            other = jnp.where(a == 2, tile[16:24], tile[24:32])
            halves.append(jnp.where(a < 2, piece, other))
        out_ref[c] = jnp.concatenate(halves, axis=0).astype(BF16)


def mid_sums(row_ref, col_ref, low_ref, blocks_ref, out_ref, panels, acc):
    for p in range(2):
        half = low_ref[p].astype(F32).reshape(C, 2, W, SN)
        for o in range(2):
            panels[2 * p + o] = half[:, o].reshape(C * W, SN).astype(BF16)
    acc[...] = jnp.zeros_like(acc)
    for q in range(SLOTS1):
        row = row_ref[0, q]
        slot = jnp.where(row < OWN, row - L0, L1)
        source = jnp.minimum(panel_of(col_ref[0, q]), 3)
        acc[slot] += dot_nt(panels[source], blocks_ref[0, q])
    out_ref[...] = cut([acc[i] for i in range(L1)])


def mid_forward(in_ref, rhs_ref, dinv_ref, y_ref, spread_ref):
    sums = jnp.sum(in_ref[...].astype(F32), axis=0)
    rows = []
    for i in range(L1):
        k = L0 + i
        right = rhs_ref[:, k * SN : (k + 1) * SN].astype(F32) - sums[i * W : (i + 1) * W]
        rows.append(dot_nt(right.astype(BF16), dinv_ref[k]))
    y = jnp.concatenate(rows, axis=0).astype(BF16)
    y_ref[...] = y
    for r in range(R):
        spread_ref[r] = y


def mid_by_class(in_ref, out_ref):
    for c in range(C):
        halves = [None, None]
        for r in range(R):
            for i in range(L1):
                if (r * OWN + L0 + i) % C == c:
                    halves[r % 2] = in_ref[r].astype(F32)[i * W : (i + 1) * W]
        out_ref[c] = jnp.concatenate(halves, axis=0).astype(BF16)


def top_sums(row_ref, col_ref, low_ref, mid_ref, blocks_ref, out_ref, panels, acc):
    for p in range(2):
        half = low_ref[p].astype(F32).reshape(C, 2, W, SN)
        for o in range(2):
            panels[2 * p + o] = half[:, o].reshape(C * W, SN).astype(BF16)
    for p in range(2):
        panels[4 + p] = join(mid_ref[...], p)
    acc[...] = jnp.zeros_like(acc)
    for q in range(SLOTS1, SLOTS):
        row = row_ref[0, q]
        slot = jnp.where(row < OWN, row - MID, L2)
        source = panel_of(col_ref[0, q])
        acc[slot] += dot_nt(panels[source], blocks_ref[0, q])
    out_ref[...] = cut([acc[i] for i in range(L2)])


def top_solve(in_ref, rhs_ref, dinv_ref, x_ref, spread_ref):
    sums = jnp.sum(in_ref[...].astype(F32), axis=0)
    rows = []
    for i in range(L2):
        k = MID + i
        right = rhs_ref[:, k * SN : (k + 1) * SN].astype(F32) - sums[i * W : (i + 1) * W]
        y = dot_nt(right.astype(BF16), dinv_ref[k]).astype(BF16)
        rows.append(dot_nn(y, dinv_ref[k]))
    x = jnp.concatenate(rows, axis=0).astype(BF16)
    x_ref[...] = x
    for c in range(C):
        spread_ref[c] = x


def top_carries(row_ref, col_ref, in_ref, blocks_ref, low_ref, out_ref, known, acc):
    for i in range(L2):
        known[i] = join(in_ref[...], i)
    acc[...] = jnp.zeros_like(acc)
    for q in range(SLOTS1, SLOTS):
        row = row_ref[0, q]
        source = jnp.clip(row - MID, 0, L2 - 1)
        slot = jnp.where(row < OWN, panel_of(col_ref[0, q]), 6)
        acc[slot] += dot_nn(known[source], blocks_ref[0, q])
    for p in range(4):
        low_ref[p] = acc[p]
    out_ref[...] = cut([acc[4], acc[5]])


def mid_by_row(in_ref, out_ref):
    for r in range(R):
        parts = []
        for i in range(L1):
            c = (r * OWN + L0 + i) % C
            parts.append(in_ref[c].astype(F32)[(r % 2) * W : (r % 2 + 1) * W])
        out_ref[r] = jnp.concatenate(parts, axis=0).astype(BF16)


def mid_backward(in_ref, y_ref, dinv_ref, x_ref, spread_ref):
    carry = jnp.sum(in_ref[...].astype(F32), axis=0)
    left = (y_ref[...].astype(F32) - carry).reshape(L1, W, SN)
    rows = [dot_nn(left[i].astype(BF16), dinv_ref[L0 + i]) for i in range(L1)]
    x = jnp.concatenate(rows, axis=0).astype(BF16)
    x_ref[...] = x
    for c in range(C):
        spread_ref[c] = x


def low_carries(row_ref, col_ref, in_ref, part_ref, blocks_ref, out_ref, known, acc):
    for i in range(L1):
        known[i] = join(in_ref[...], i)
    for p in range(4):
        acc[p] = part_ref[p]
    acc[4] = jnp.zeros((SN, SN), F32)
    for q in range(SLOTS1):
        row = row_ref[0, q]
        source = jnp.clip(row - L0, 0, L1 - 1)
        slot = jnp.where(row < OWN, jnp.minimum(panel_of(col_ref[0, q]), 3), 4)
        acc[slot] += dot_nn(known[source], blocks_ref[0, q])
    for p in range(2):
        out_ref[p] = cut([acc[2 * p], acc[2 * p + 1]])


def pair_sum(in_ref, out_ref):
    out_ref[...] = (in_ref[0].astype(F32) + in_ref[1].astype(F32)).astype(BF16)


def low_by_row(core_ref, in_ref, out_ref):
    core = core_ref[0]
    for z in range(Z):
        parts = []
        for k in range(L0):
            c = (28 * z + 14 * core + k) % C
            o = k // 4
            parts.append(in_ref[c].astype(F32)[o * W : (o + 1) * W])
        out_ref[z] = jnp.concatenate(parts, axis=0).astype(BF16)


def low_backward(in_ref, y_ref, dinv_ref, mid_ref, top_ref, out_ref):
    carry = jnp.sum(in_ref[...].astype(F32), axis=0)
    left = (y_ref[...].astype(F32) - carry).reshape(L0, W, SN)
    for k in range(L0):
        out_ref[:, k * SN : (k + 1) * SN] = dot_nn(left[k].astype(BF16), dinv_ref[k]).astype(BF16)
    mid = mid_ref[...].astype(F32)
    for i in range(L1):
        out_ref[:, (L0 + i) * SN : (L0 + i + 1) * SN] = mid[i * W : (i + 1) * W].astype(BF16)
    top = top_ref[...].astype(F32)
    for i in range(L2):
        out_ref[:, (MID + i) * SN : (MID + i + 1) * SN] = top[i * W : (i + 1) * W].astype(BF16)


VM = pl.BlockSpec(memory_space=pltpu.VMEM)
SM = pl.BlockSpec(memory_space=pltpu.SMEM)


def call(kernel, outs, *args, scratch=()):
    single = len(outs) == 1
    shapes = [jax.ShapeDtypeStruct(shape, kind) for shape, kind in outs]
    return pl.pallas_call(
        kernel,
        out_shape=shapes[0] if single else shapes,
        in_specs=[SM if a.dtype == jnp.int32 else VM for a in args],
        out_specs=VM if single else [VM] * len(outs),
        scratch_shapes=list(scratch),
        compiler_params=pltpu.CompilerParams(vmem_limit_bytes=24 * 1024 * 1024),
    )(*args)


def over_col(pieces):
    return lax.all_to_all(pieces, "col", 0, 0, tiled=True)


def over_row(pieces):
    return lax.all_to_all(pieces, "row", 0, 0, tiled=True)


def over_z(pieces):
    return lax.all_to_all(pieces, "row", 0, 0, tiled=True, axis_index_groups=Z_GROUPS)


def on_device(rhs, dinv, blocks, block_row, block_col):
    core = (lax.axis_index("row") % 2).astype(jnp.int32).reshape(1)
    right = rhs.T
    panel = pltpu.VMEM((7, SN, SN), BF16)
    sums = pltpu.VMEM((7, SN, SN), F32)
    work = (panel, sums)
    y_low, spread = call(low_forward, [((64, SN), BF16), ((Z, 64, SN), BF16)], right, dinv)
    sent = call(low_by_class, [((C, 16, SN), BF16)], core, over_z(spread))
    low = lax.all_gather(over_col(sent), "row", axis=0, axis_index_groups=CORE_GROUPS)
    part = call(mid_sums, [((C, 32, SN), BF16)], block_row, block_col, low, blocks, scratch=work)
    y_mid, spread = call(
        mid_forward, [((32, SN), BF16), ((R, 32, SN), BF16)], over_col(part), right, dinv
    )
    sent = call(mid_by_class, [((C, 16, SN), BF16)], over_row(spread))
    part = call(
        top_sums, [((C, 16, SN), BF16)], block_row, block_col, low, over_col(sent), blocks, scratch=work
    )
    x_top, spread = call(
        top_solve, [((16, SN), BF16), ((C, 16, SN), BF16)], over_col(part), right, dinv
    )
    low_part, sent = call(
        top_carries,
        [((4, SN, SN), F32), ((C, 16, SN), BF16)],
        block_row,
        block_col,
        over_col(spread),
        blocks,
        scratch=work,
    )
    sent = call(mid_by_row, [((R, 32, SN), BF16)], over_col(sent))
    x_mid, spread = call(
        mid_backward, [((32, SN), BF16), ((C, 32, SN), BF16)], over_row(sent), y_mid, dinv
    )
    part = call(
        low_carries,
        [((2, C, 16, SN), BF16)],
        block_row,
        block_col,
        over_col(spread),
        low_part,
        blocks,
        scratch=work,
    )
    both = lax.all_to_all(part, "row", 0, 0, tiled=True, axis_index_groups=CORE_GROUPS)
    sent = call(pair_sum, [((C, 16, SN), BF16)], both)
    sent = call(low_by_row, [((Z, 64, SN), BF16)], core, over_col(sent))
    out = call(low_backward, [((W, OWN * SN), BF16)], over_z(sent), y_low, dinv, x_mid, x_top)
    return out.T


def solution(mesh):
    placed = (
        P("row", "col"),
        P("row", None, None),
        P("row", "col", None, None),
        P("row", "col"),
        P("row", "col"),
    )
    return jax.shard_map(
        on_device, mesh=mesh, in_specs=placed, out_specs=P("row", "col"), check_vma=False
    )
```

```python
import jax
import jax.numpy as jnp
from jax import lax
from jax.experimental import pallas as pl
from jax.experimental.pallas import tpu as pltpu
from jax.sharding import PartitionSpec as P

SN = 256
L0 = 8
L1 = 4
L2 = 2
MID = L0 + L1
OWN = L0 + L1 + L2
SLOTS1 = 8
SLOTS = 14
R = 16
C = 32
Z = 8
W = 8
F32 = jnp.float32
BF16 = jnp.bfloat16
Z_GROUPS = [[2 * z + core for z in range(Z)] for core in range(2)]
CORE_GROUPS = [[2 * z, 2 * z + 1] for z in range(Z)]
SWAP = [(r, r ^ 1) for r in range(R)]
X = 4
Y = 8
STRIP = 32
Y_GROUPS = [[X * y + x for y in range(Y)] for x in range(X)]


def mid_groups():
    groups = []
    for core in range(2):
        for c in range(C):
            by_y = [0] * Y
            for z in range(Z):
                r = 2 * z + core
                column = [s % C for s in range(r * OWN + L0, r * OWN + MID) if s % X == c % X][0]
                by_y[column // X] = r * C + c
            groups.append(by_y)
    return groups


MID_GROUPS = mid_groups()


def dot_nt(left, right):
    return lax.dot_general(left, right, (((1,), (1,)), ((), ())), preferred_element_type=F32)


def dot_nn(left, right):
    return lax.dot_general(left, right, (((1,), (0,)), ((), ())), preferred_element_type=F32)


def panel_of(column):
    k = column % OWN
    parity = column % (2 * OWN) // OWN
    return jnp.where(k < L0, 2 * parity + k // 4, 4 + parity)


def join(ref_value, index):
    rows = ref_value.shape[1]
    wide = ref_value.astype(F32).reshape(C, rows // W, W, SN)
    return wide[:, index].reshape(C * W, SN).astype(BF16)


def cut(panels, kind=BF16):
    parts = [p.reshape(C, W, SN) for p in panels]
    return jnp.stack(parts, axis=1).reshape(C, W * len(parts), SN).astype(kind)


def low_forward(rhs_ref, dinv_ref, y_ref, spread_ref):
    rows = []
    for k in range(L0):
        rows.append(dot_nt(rhs_ref[:, k * SN : (k + 1) * SN], dinv_ref[k]))
    y = jnp.concatenate(rows, axis=0).astype(BF16)
    y_ref[...] = y
    for z in range(Z):
        spread_ref[z] = y


def low_by_class(place_ref, in_ref, out_ref):
    core = place_ref[0] % 2
    for c in range(C):
        halves = []
        for o in range(2):
            a = (c + 2 * core) % 4
            z = (7 * ((c - 14 * core - a - 4 * o + 64) // 4)) % Z
            tile = in_ref[z, 32 * o : 32 * o + 32].astype(F32)
            piece = jnp.where(a == 0, tile[0:8], tile[8:16])
            other = jnp.where(a == 2, tile[16:24], tile[24:32])
            halves.append(jnp.where(a < 2, piece, other))
        out_ref[c] = jnp.concatenate(halves, axis=0).astype(BF16)


def mid_sums(place_ref, row_ref, col_ref, low_ref, blocks_ref, rhs_ref, out_ref, panels, acc):
    r = place_ref[0]
    c = pl.multiple_of(place_ref[1] * W, W)
    for p in range(2):
        half = low_ref[p].astype(F32).reshape(C, 2, W, SN)
        for o in range(2):
            panels[2 * p + o] = half[:, o].reshape(C * W, SN).astype(BF16)
    acc[...] = jnp.zeros_like(acc)
    for i in range(L1):
        x = (r * OWN + L0 + i) % X
        acc[x, pl.ds(c, W)] = -rhs_ref[:, (L0 + i) * SN : (L0 + i + 1) * SN].astype(F32)
    for q in range(SLOTS1):
        row = row_ref[0, q]
        slot = jnp.where(row < OWN, (r * OWN + row) % X, X)
        source = jnp.minimum(panel_of(col_ref[0, q]), 3)
        acc[slot] += dot_nt(panels[source], blocks_ref[0, q])
    for x in range(X):
        strips = acc[x].astype(BF16)
        for y in range(Y):
            out_ref[X * y + x] = strips[y * STRIP : (y + 1) * STRIP]


def mid_forward(place_ref, in_ref, dinv_ref, y_ref, spread_ref):
    k = L0 + (place_ref[1] + 2 * place_ref[0]) % X
    right = -jnp.sum(in_ref[...].astype(F32), axis=0)
    y = dot_nt(right.astype(BF16), dinv_ref[k]).astype(BF16)
    y_ref[...] = y
    for z in range(Z):
        spread_ref[z] = y


def top_sums(row_ref, col_ref, low_ref, mid_ref, blocks_ref, out_ref, panels, acc):
    for p in range(2):
        half = low_ref[p].astype(F32).reshape(C, 2, W, SN)
        for o in range(2):
            panels[2 * p + o] = half[:, o].reshape(C * W, SN).astype(BF16)
    for p in range(2):
        panels[4 + p] = mid_ref[p].reshape(SN, SN)
    acc[...] = jnp.zeros_like(acc)
    for q in range(SLOTS1, SLOTS):
        row = row_ref[0, q]
        slot = jnp.where(row < OWN, row - MID, L2)
        source = panel_of(col_ref[0, q])
        acc[slot] += dot_nt(panels[source], blocks_ref[0, q])
    out_ref[...] = cut([acc[i] for i in range(L2)])


def top_solve(in_ref, rhs_ref, dinv_ref, x_ref, spread_ref):
    sums = jnp.sum(in_ref[...].astype(F32), axis=0)
    rows = []
    for i in range(L2):
        k = MID + i
        right = rhs_ref[:, k * SN : (k + 1) * SN].astype(F32) - sums[i * W : (i + 1) * W]
        y = dot_nt(right.astype(BF16), dinv_ref[k]).astype(BF16)
        rows.append(dot_nn(y, dinv_ref[k]))
    x = jnp.concatenate(rows, axis=0).astype(BF16)
    x_ref[...] = x
    for c in range(C):
        spread_ref[c] = x


def top_carries(place_ref, row_ref, col_ref, in_ref, blocks_ref, low_ref, keep_ref, out_ref, known, acc):
    core = place_ref[0] % 2
    for i in range(L2):
        known[i] = join(in_ref[...], i)
    acc[...] = jnp.zeros_like(acc)
    for q in range(SLOTS1, SLOTS):
        row = row_ref[0, q]
        source = jnp.clip(row - MID, 0, L2 - 1)
        slot = jnp.where(row < OWN, panel_of(col_ref[0, q]), 6)
        acc[slot] += dot_nn(known[source], blocks_ref[0, q])
    for p in range(4):
        low_ref[p] = acc[p]
    keep_ref[...] = acc[4 + core]
    out_ref[...] = acc[5 - core].astype(BF16)


def mid_backward(place_ref, in_ref, y_ref, dinv_ref, spread_ref):
    k = L0 + (place_ref[1] + 2 * place_ref[0]) % X
    left = y_ref[...].astype(F32) - jnp.sum(in_ref[...].astype(F32), axis=0)
    x = dot_nn(left.astype(BF16), dinv_ref[k]).astype(BF16)
    for c in range(C):
        spread_ref[c] = x


def low_carries(
    place_ref, row_ref, col_ref, in_ref, part_ref, blocks_ref, x_ref, keep_ref, out_ref, known, acc
):
    r = place_ref[0]
    c = place_ref[1]
    core = r % 2
    for x in range(X):
        for y in range(Y):
            known[x, y * STRIP : (y + 1) * STRIP] = in_ref[X * y + x]
    own = []
    for i in range(L1):
        strip = in_ref[c // X * X + (r * OWN + L0 + i) % X].astype(F32)
        octet = strip[:W]
        for part in range(1, X):
            octet = jnp.where(c % X == part, strip[part * W : (part + 1) * W], octet)
        own.append(octet)
    x_ref[...] = jnp.concatenate(own, axis=0).astype(BF16)
    for p in range(4):
        acc[p] = part_ref[p]
    acc[4] = jnp.zeros((SN, SN), F32)
    for q in range(SLOTS1):
        row = row_ref[0, q]
        source = (r * OWN + row) % X
        slot = jnp.where(row < OWN, jnp.minimum(panel_of(col_ref[0, q]), 3), 4)
        acc[slot] += dot_nn(known[source], blocks_ref[0, q])
    keep_ref[...] = cut([acc[2 * core], acc[2 * core + 1]], F32)
    out_ref[...] = cut([acc[2 - 2 * core], acc[3 - 2 * core]], BF16)


def pair_sum(keep_ref, in_ref, out_ref):
    out_ref[...] = (keep_ref[...] + in_ref[...].astype(F32)).astype(BF16)


def low_by_row(place_ref, in_ref, out_ref):
    core = place_ref[0] % 2
    for z in range(Z):
        parts = []
        for k in range(L0):
            c = (28 * z + 14 * core + k) % C
            o = k // 4
            parts.append(in_ref[c].astype(F32)[o * W : (o + 1) * W])
        out_ref[z] = jnp.concatenate(parts, axis=0).astype(BF16)


def low_backward(in_ref, y_ref, dinv_ref, mid_ref, top_ref, out_ref):
    carry = jnp.sum(in_ref[...].astype(F32), axis=0)
    left = (y_ref[...].astype(F32) - carry).reshape(L0, W, SN)
    for k in range(L0):
        out_ref[:, k * SN : (k + 1) * SN] = dot_nn(left[k].astype(BF16), dinv_ref[k]).astype(BF16)
    mid = mid_ref[...].astype(F32)
    for i in range(L1):
        out_ref[:, (L0 + i) * SN : (L0 + i + 1) * SN] = mid[i * W : (i + 1) * W].astype(BF16)
    top = top_ref[...].astype(F32)
    for i in range(L2):
        out_ref[:, (MID + i) * SN : (MID + i + 1) * SN] = top[i * W : (i + 1) * W].astype(BF16)


VM = pl.BlockSpec(memory_space=pltpu.VMEM)
SM = pl.BlockSpec(memory_space=pltpu.SMEM)


def call(kernel, outs, *args, scratch=()):
    single = len(outs) == 1
    shapes = [jax.ShapeDtypeStruct(shape, kind) for shape, kind in outs]
    return pl.pallas_call(
        kernel,
        out_shape=shapes[0] if single else shapes,
        in_specs=[SM if a.dtype == jnp.int32 else VM for a in args],
        out_specs=VM if single else [VM] * len(outs),
        scratch_shapes=list(scratch),
        compiler_params=pltpu.CompilerParams(vmem_limit_bytes=24 * 1024 * 1024),
    )(*args)


def over_col(pieces):
    return lax.all_to_all(pieces, "col", 0, 0, tiled=True)


def over_y(pieces):
    return lax.all_to_all(pieces, "col", 0, 0, tiled=True, axis_index_groups=Y_GROUPS)


def over_z_by_y(pieces):
    return lax.all_to_all(pieces, ("row", "col"), 0, 0, tiled=True, axis_index_groups=MID_GROUPS)


def swap(half):
    return lax.ppermute(half, "row", SWAP)


def over_z(pieces):
    return lax.all_to_all(pieces, "row", 0, 0, tiled=True, axis_index_groups=Z_GROUPS)


def on_device(rhs, dinv, blocks, block_row, block_col):
    place = jnp.stack([lax.axis_index("row"), lax.axis_index("col")]).astype(jnp.int32)
    right = rhs.T
    panel = pltpu.VMEM((7, SN, SN), BF16)
    sums = pltpu.VMEM((7, SN, SN), F32)
    work = (panel, sums)
    y_low, spread = call(low_forward, [((64, SN), BF16), ((Z, 64, SN), BF16)], right, dinv)
    sent = call(low_by_class, [((C, 16, SN), BF16)], place, over_z(spread))
    low = lax.all_gather(over_col(sent), "row", axis=0, axis_index_groups=CORE_GROUPS)
    part = call(
        mid_sums,
        [((C, STRIP, SN), BF16)],
        place,
        block_row,
        block_col,
        low,
        blocks,
        right,
        scratch=work,
    )
    y_mid, spread = call(
        mid_forward, [((STRIP, SN), BF16), ((Z, STRIP, SN), BF16)], place, over_col(part), dinv
    )
    mid = lax.all_gather(over_y(over_z_by_y(spread)), "row", axis=0, axis_index_groups=CORE_GROUPS)
    part = call(
        top_sums, [((C, 16, SN), BF16)], block_row, block_col, low, mid, blocks, scratch=work
    )
    x_top, spread = call(
        top_solve, [((16, SN), BF16), ((C, 16, SN), BF16)], over_col(part), right, dinv
    )
    low_part, keep, sent = call(
        top_carries,
        [((4, SN, SN), F32), ((SN, SN), F32), ((SN, SN), BF16)],
        place,
        block_row,
        block_col,
        over_col(spread),
        blocks,
        scratch=work,
    )
    both = call(pair_sum, [((SN, SN), BF16)], keep, swap(sent))
    carry = over_z_by_y(over_y(both.reshape(Y, STRIP, SN)))
    spread = call(mid_backward, [((C, STRIP, SN), BF16)], place, carry, y_mid, dinv)
    x_mid, keep, sent = call(
        low_carries,
        [((32, SN), BF16), ((C, 16, SN), F32), ((C, 16, SN), BF16)],
        place,
        block_row,
        block_col,
        over_col(spread),
        low_part,
        blocks,
        scratch=work,
    )
    sent = call(pair_sum, [((C, 16, SN), BF16)], keep, swap(sent))
    sent = call(low_by_row, [((Z, 64, SN), BF16)], place, over_col(sent))
    out = call(low_backward, [((W, OWN * SN), BF16)], over_z(sent), y_low, dinv, x_mid, x_top)
    return out.T


def solution(mesh):
    placed = (
        P("row", "col"),
        P("row", None, None),
        P("row", "col", None, None),
        P("row", "col"),
        P("row", "col"),
    )
    return jax.shard_map(
        on_device, mesh=mesh, in_specs=placed, out_specs=P("row", "col"), check_vma=False
    )
```

```python
import jax
import jax.numpy as jnp
from jax import lax
from jax.experimental import pallas as pl
from jax.experimental.pallas import tpu as pltpu
from jax.sharding import PartitionSpec as P

SN = 256
L0 = 8
L1 = 4
L2 = 2
MID = L0 + L1
OWN = L0 + L1 + L2
SLOTS1 = 8
SLOTS2 = 6
SLOTS = 14
R = 16
C = 32
X = 4
Y = 8
Z = 8
W = 8
N = W * Y
LOWS = 4 * X
MIDS = 2 * X
F32 = jnp.float32
BF16 = jnp.bfloat16
Z_GROUPS = [[2 * z + core for z in range(Z)] for core in range(2)]
CORE_GROUPS = [[2 * z, 2 * z + 1] for z in range(Z)]
Y_GROUPS = [[X * y + x for y in range(Y)] for x in range(X)]
X_GROUPS = [[X * y + x for x in range(X)] for y in range(Y)]
X_PAIRS = [[X * y + x, X * y + x + 2] for y in range(Y) for x in range(2)]
SWAP = [(r, r ^ 1) for r in range(R)]


def dot_nt(left, right):
    return lax.dot_general(left, right, (((1,), (1,)), ((), ())), preferred_element_type=F32)


def dot_nn(left, right):
    return lax.dot_general(left, right, (((1,), (0,)), ((), ())), preferred_element_type=F32)


def low_panel(column):
    return column % (2 * OWN) // OWN * MIDS + column % X * 2 + column % OWN // 4


def mid_panel(column):
    return column % (2 * OWN) // OWN * X + column % X


def panel_of(column):
    return jnp.where(column % OWN < L0, low_panel(column), LOWS + mid_panel(column))


def join(pieces, out_ref, first=0):
    count = pieces.shape[1] // W
    wide = pieces.astype(F32).reshape(Y, count, W, SN)
    for i in range(count):
        out_ref[first + i] = wide[:, i].reshape(N, SN).astype(BF16)


def cut(panels, kind=BF16):
    parts = [p.reshape(Y, W, SN) for p in panels]
    return jnp.stack(parts, axis=1).reshape(Y, W * len(parts), SN).astype(kind)


def each(pair_ref, left_ref, right_ref):
    return enumerate((pair_ref.at[0], pair_ref.at[1], left_ref, right_ref))


def low_forward(rhs_ref, dinv_ref, y_ref, spread_ref):
    rows = []
    for k in range(L0):
        rows.append(dot_nt(rhs_ref[:, k * SN : (k + 1) * SN], dinv_ref[k]))
    y = jnp.concatenate(rows, axis=0).astype(BF16)
    y_ref[...] = y
    for z in range(Z):
        spread_ref[z] = y


def low_by_class(place_ref, in_ref, out_ref):
    core = place_ref[0] % 2
    for c in range(C):
        halves = []
        for o in range(2):
            a = (c + 2 * core) % 4
            z = (7 * ((c - 14 * core - a - 4 * o + 64) // 4)) % Z
            tile = in_ref[z, 32 * o : 32 * o + 32].astype(F32)
            piece = jnp.where(a == 0, tile[0:8], tile[8:16])
            other = jnp.where(a == 2, tile[16:24], tile[24:32])
            halves.append(jnp.where(a < 2, piece, other))
        x = c % X * 2 * W
        out_ref[c // X, x : x + 2 * W] = jnp.concatenate(halves, axis=0).astype(BF16)


def mid_sums(code_ref, low_ref, pair_ref, left_ref, right_ref, out_ref, panels, acc):
    for p in range(2):
        join(low_ref[p], panels, p * MIDS)
    acc[...] = jnp.zeros_like(acc)
    for place, tiles in each(pair_ref, left_ref, right_ref):
        for q in range(SLOTS1):
            row = code_ref[place, q]
            slot = jnp.where(row < OWN, row - L0, L1)
            source = jnp.minimum(panel_of(code_ref[place, SLOTS + q]), LOWS - 1)
            acc[slot] += dot_nt(panels[source], tiles[q * SN : (q + 1) * SN])
    out_ref[...] = cut([acc[i] for i in range(L1)])


def mid_forward(in_ref, rhs_ref, dinv_ref, y_ref, spread_ref):
    sums = jnp.sum(in_ref[...].astype(F32), axis=0)
    rows = []
    for i in range(L1):
        k = L0 + i
        right = rhs_ref[:, k * SN : (k + 1) * SN].astype(F32) - sums[i * W : (i + 1) * W]
        rows.append(dot_nt(right.astype(BF16), dinv_ref[k]))
    y = jnp.concatenate(rows, axis=0).astype(BF16)
    y_ref[...] = y
    for z in range(Z):
        spread_ref[z] = y


def mid_by_class(place_ref, in_ref, out_ref):
    core = place_ref[0] % 2
    for y in range(Y):
        octets = []
        for x in range(X):
            i = (x + 2 * core) % 4
            z = (7 * ((X * y + x - 14 * core - L0 - i + 64) // 4)) % Z
            tile = in_ref[z].astype(F32)
            octets.append(jnp.where(core == 0, tile[x * W :][:W], tile[(x + 2) % 4 * W :][:W]))
        out_ref[y] = jnp.concatenate(octets, axis=0).astype(BF16)


def top_sums(code_ref, low_ref, mid_ref, tiles_ref, out_ref, panels, acc):
    for p in range(2):
        join(low_ref[p], panels, p * MIDS)
        join(mid_ref[p], panels, LOWS + p * X)
    acc[...] = jnp.zeros_like(acc)
    for place in range(X):
        for q in range(SLOTS2):
            row = code_ref[place, SLOTS1 + q]
            slot = jnp.where(row < OWN, row - MID, L2)
            source = panel_of(code_ref[place, SLOTS + SLOTS1 + q])
            acc[slot] += dot_nt(panels[source], tiles_ref[place, q * SN : (q + 1) * SN])
    out_ref[...] = cut([acc[i] for i in range(L2)])


def top_solve(in_ref, rhs_ref, dinv_ref, x_ref, spread_ref):
    sums = jnp.sum(in_ref[...].astype(F32), axis=0)
    rows = []
    for i in range(L2):
        k = MID + i
        right = rhs_ref[:, k * SN : (k + 1) * SN].astype(F32) - sums[i * W : (i + 1) * W]
        y = dot_nt(right.astype(BF16), dinv_ref[k]).astype(BF16)
        rows.append(dot_nn(y, dinv_ref[k]))
    x = jnp.concatenate(rows, axis=0).astype(BF16)
    x_ref[...] = x
    for y in range(Y):
        spread_ref[y] = x


def top_carries(place_ref, code_ref, in_ref, tiles_ref, low_ref, keep_ref, out_ref, known, acc):
    core = place_ref[0] % 2
    join(in_ref[...], known)
    acc[...] = jnp.zeros_like(acc)
    for place in range(X):
        for q in range(SLOTS2):
            row = code_ref[place, SLOTS1 + q]
            source = jnp.clip(row - MID, 0, L2 - 1)
            slot = jnp.where(row < OWN, panel_of(code_ref[place, SLOTS + SLOTS1 + q]), LOWS + MIDS)
            acc[slot] += dot_nn(known[source], tiles_ref[place, q * SN : (q + 1) * SN])
    for p in range(LOWS):
        low_ref[p] = acc[p]
    keep_ref[...] = cut([acc[LOWS + core * X + x] for x in range(X)], F32)
    out_ref[...] = cut([acc[LOWS + (1 - core) * X + x] for x in range(X)])


def mid_by_row(place_ref, in_ref, out_ref):
    core = place_ref[0] % 2
    for z in range(Z):
        octets = []
        for i in range(L1):
            y = (28 * z + 14 * core + L0 + i) % C // X
            tile = in_ref[y].astype(F32)
            octets.append(jnp.where(core == 0, tile[i * W :][:W], tile[(i + 2) % 4 * W :][:W]))
        out_ref[z] = jnp.concatenate(octets, axis=0).astype(BF16)


def mid_backward(in_ref, y_ref, dinv_ref, x_ref, spread_ref):
    carry = jnp.sum(in_ref[...].astype(F32), axis=0)
    left = (y_ref[...].astype(F32) - carry).reshape(L1, W, SN)
    rows = [dot_nn(left[i].astype(BF16), dinv_ref[L0 + i]) for i in range(L1)]
    x = jnp.concatenate(rows, axis=0).astype(BF16)
    x_ref[...] = x
    for y in range(Y):
        spread_ref[y] = x


def low_carries(
    place_ref, code_ref, in_ref, part_ref, pair_ref, left_ref, right_ref, keep_ref, out_ref, known, acc
):
    core = place_ref[0] % 2
    join(in_ref[...], known)
    for p in range(LOWS):
        acc[p] = part_ref[p]
    acc[LOWS] = jnp.zeros((N, SN), F32)
    for place, tiles in each(pair_ref, left_ref, right_ref):
        for q in range(SLOTS1):
            row = code_ref[place, q]
            source = jnp.clip(row - L0, 0, L1 - 1)
            panel = jnp.minimum(panel_of(code_ref[place, SLOTS + q]), LOWS - 1)
            slot = jnp.where(row < OWN, panel, LOWS)
            acc[slot] += dot_nn(known[source], tiles[q * SN : (q + 1) * SN])
    keep_ref[...] = cut([acc[core * MIDS + i] for i in range(MIDS)], F32)
    out_ref[...] = cut([acc[(1 - core) * MIDS + i] for i in range(MIDS)])


def pair_sum(keep_ref, in_ref, out_ref):
    out_ref[...] = (keep_ref[...] + in_ref[...].astype(F32)).astype(BF16)


def low_by_row(place_ref, in_ref, out_ref):
    core = place_ref[0] % 2
    for z in range(Z):
        parts = []
        for k in range(L0):
            c = (28 * z + 14 * core + k) % C
            o = k // 4
            tile = in_ref[c // X].astype(F32)
            even = tile[(k % X * 2 + o) * W :][:W]
            odd = tile[((k + 2) % X * 2 + o) * W :][:W]
            parts.append(jnp.where(core == 0, even, odd))
        out_ref[z] = jnp.concatenate(parts, axis=0).astype(BF16)


def low_backward(in_ref, y_ref, dinv_ref, mid_ref, top_ref, out_ref):
    carry = jnp.sum(in_ref[...].astype(F32), axis=0)
    left = (y_ref[...].astype(F32) - carry).reshape(L0, W, SN)
    for k in range(L0):
        out_ref[:, k * SN : (k + 1) * SN] = dot_nn(left[k].astype(BF16), dinv_ref[k]).astype(BF16)
    mid = mid_ref[...].astype(F32)
    for i in range(L1):
        out_ref[:, (L0 + i) * SN : (L0 + i + 1) * SN] = mid[i * W : (i + 1) * W].astype(BF16)
    top = top_ref[...].astype(F32)
    for i in range(L2):
        out_ref[:, (MID + i) * SN : (MID + i + 1) * SN] = top[i * W : (i + 1) * W].astype(BF16)


VM = pl.BlockSpec(memory_space=pltpu.VMEM)
SM = pl.BlockSpec(memory_space=pltpu.SMEM)


def call(kernel, outs, *args, scratch=()):
    single = len(outs) == 1
    shapes = [jax.ShapeDtypeStruct(shape, kind) for shape, kind in outs]
    return pl.pallas_call(
        kernel,
        out_shape=shapes[0] if single else shapes,
        in_specs=[SM if a.dtype == jnp.int32 else VM for a in args],
        out_specs=VM if single else [VM] * len(outs),
        scratch_shapes=list(scratch),
        compiler_params=pltpu.CompilerParams(vmem_limit_bytes=40 * 1024 * 1024),
    )(*args)


def over_y(pieces):
    return lax.all_to_all(pieces, "col", 0, 0, tiled=True, axis_index_groups=Y_GROUPS)


def over_z(pieces):
    return lax.all_to_all(pieces, "row", 0, 0, tiled=True, axis_index_groups=Z_GROUPS)


def over_core(pieces):
    return lax.all_gather(pieces, "row", axis=0, axis_index_groups=CORE_GROUPS)


def swap(half):
    return lax.ppermute(half, "row", SWAP)


def along_x(array, step):
    return lax.ppermute(array, "col", [(c, c // X * X + (c + step) % X) for c in range(C)])


def on_device(rhs, dinv, blocks, block_row, block_col):
    place = jnp.stack([lax.axis_index("row"), lax.axis_index("col")]).astype(jnp.int32)
    right = rhs.T
    panels = pltpu.VMEM((LOWS + MIDS, N, SN), BF16)
    sums = pltpu.VMEM((LOWS + MIDS + 1, N, SN), F32)
    work = (panels, sums)

    codes = jnp.concatenate([block_row, block_col], axis=1).astype(BF16)
    codes = jnp.pad(codes, ((0, 15), (0, SN - 2 * SLOTS)))
    tiles = jnp.concatenate([blocks[0, :SLOTS1].reshape(SLOTS1 * SN, SN), codes])
    before = along_x(tiles, 1)
    after = along_x(tiles, -1)
    pair = lax.all_gather(tiles, "col", axis=0, axis_index_groups=X_PAIRS)
    upper = jnp.concatenate([blocks[0, SLOTS1:].reshape(SLOTS2 * SN, SN), codes])
    upper = lax.all_gather(upper, "col", axis=0, axis_index_groups=X_GROUPS)

    y_low, spread = call(low_forward, [((64, SN), BF16), ((Z, 64, SN), BF16)], right, dinv)
    sent = call(low_by_class, [((Y, 64, SN), BF16)], place, over_z(spread))
    low = over_core(over_y(sent))
    rows = jnp.stack([pair[0, -16], pair[1, -16], before[-16], after[-16]]).astype(jnp.int32)
    code = rows[:, : 2 * SLOTS]
    upper_code = upper[:, -16, : 2 * SLOTS].astype(jnp.int32)
    part = call(mid_sums, [((Y, 32, SN), BF16)], code, low, pair, before, after, scratch=work)
    y_mid, spread = call(
        mid_forward, [((32, SN), BF16), ((Z, 32, SN), BF16)], over_y(part), right, dinv
    )
    sent = call(mid_by_class, [((Y, 32, SN), BF16)], place, over_z(spread))
    mid = over_core(over_y(sent))
    part = call(top_sums, [((Y, 16, SN), BF16)], upper_code, low, mid, upper, scratch=work)
    x_top, spread = call(
        top_solve, [((16, SN), BF16), ((Y, 16, SN), BF16)], over_y(part), right, dinv
    )
    low_part, keep, sent = call(
        top_carries,
        [((LOWS, N, SN), F32), ((Y, 32, SN), F32), ((Y, 32, SN), BF16)],
        place,
        upper_code,
        over_y(spread),
        upper,
        scratch=work,
    )
    both = call(pair_sum, [((Y, 32, SN), BF16)], keep, swap(sent))
    sent = call(mid_by_row, [((Z, 32, SN), BF16)], place, over_y(both))
    x_mid, spread = call(
        mid_backward, [((32, SN), BF16), ((Y, 32, SN), BF16)], over_z(sent), y_mid, dinv
    )
    keep, sent = call(
        low_carries,
        [((Y, 64, SN), F32), ((Y, 64, SN), BF16)],
        place,
        code,
        over_y(spread),
        low_part,
        pair,
        before,
        after,
        scratch=work,
    )
    both = call(pair_sum, [((Y, 64, SN), BF16)], keep, swap(sent))
    sent = call(low_by_row, [((Z, 64, SN), BF16)], place, over_y(both))
    out = call(low_backward, [((W, OWN * SN), BF16)], over_z(sent), y_low, dinv, x_mid, x_top)
    return out.T


def solution(mesh):
    placed = (
        P("row", "col"),
        P("row", None, None),
        P("row", "col", None, None),
        P("row", "col"),
        P("row", "col"),
    )
    return jax.shard_map(
        on_device, mesh=mesh, in_specs=placed, out_specs=P("row", "col"), check_vma=False
    )
```

```python
import jax
import jax.numpy as jnp
from jax import lax
from jax.experimental import pallas as pl
from jax.experimental.pallas import tpu as pltpu
from jax.sharding import PartitionSpec as P

SN = 256
L0 = 8
L1 = 4
L2 = 2
MID = L0 + L1
OWN = L0 + L1 + L2
SLOTS1 = 8
SLOTS = 14
R = 16
C = 32
X = 4
Y = 8
Z = 8
HALVES = 2
PEERS = Y * HALVES
W = 8
STRIP = W * HALVES
N = W * PEERS
LOWS = 8
MIDS = 4
F32 = jnp.float32
BF16 = jnp.bfloat16
Z_GROUPS = [[2 * z + core for z in range(Z)] for core in range(2)]
CORE_GROUPS = [[2 * z, 2 * z + 1] for z in range(Z)]
Y_GROUPS = [[X * y + x for y in range(Y)] for x in range(X)]
PEER_GROUPS = [[2 * peer + low for peer in range(PEERS)] for low in range(2)]
SWAP = [(r, r ^ 1) for r in range(R)]
NEIGHBOURS = [(c, c ^ 1) for c in range(C)]


def mid_groups():
    groups = []
    for core in range(2):
        for c in range(C):
            by_y = [0] * Y
            for z in range(Z):
                r = 2 * z + core
                column = [s % C for s in range(r * OWN + L0, r * OWN + MID) if s % X == c % X][0]
                by_y[column // X] = r * C + c
            groups.append(by_y)
    return groups


MID_GROUPS = mid_groups()


def dot_nt(left, right):
    return lax.dot_general(left, right, (((1,), (1,)), ((), ())), preferred_element_type=F32)


def dot_nn(left, right):
    return lax.dot_general(left, right, (((1,), (0,)), ((), ())), preferred_element_type=F32)


def low_panel(column):
    return column % (2 * OWN) // OWN * 4 + column % 2 * 2 + column % OWN // 4


def mid_panel(column):
    return column % (2 * OWN) // OWN * 2 + column % 2


def panel_of(column):
    return jnp.where(column % OWN < L0, low_panel(column), LOWS + mid_panel(column))


def join(pieces, out_ref, first=0):
    count = pieces.shape[1] // W
    wide = pieces.astype(F32).reshape(PEERS, count, W, SN)
    for i in range(count):
        out_ref[first + i] = wide[:, i].reshape(N, SN).astype(BF16)


def cut(panels, kind=BF16):
    parts = [p.reshape(PEERS, W, SN) for p in panels]
    return jnp.stack(parts, axis=1).reshape(PEERS, W * len(parts), SN).astype(kind)


def low_forward(rhs_ref, dinv_ref, y_ref, spread_ref):
    rows = []
    for k in range(L0):
        rows.append(dot_nt(rhs_ref[:, k * SN : (k + 1) * SN], dinv_ref[k]))
    y = jnp.concatenate(rows, axis=0).astype(BF16)
    y_ref[...] = y
    for z in range(Z):
        spread_ref[z] = y


def low_by_class(place_ref, in_ref, out_ref):
    core = place_ref[0] % 2
    for c in range(C):
        halves = []
        for o in range(2):
            a = (c + 2 * core) % 4
            z = (7 * ((c - 14 * core - a - 4 * o + 64) // 4)) % Z
            tile = in_ref[z, 32 * o : 32 * o + 32].astype(F32)
            piece = jnp.where(a == 0, tile[0:8], tile[8:16])
            other = jnp.where(a == 2, tile[16:24], tile[24:32])
            halves.append(jnp.where(a < 2, piece, other))
        out_ref[c // 2, c % 2 * 16 : c % 2 * 16 + 16] = jnp.concatenate(halves, axis=0).astype(BF16)


def mid_sums(place_ref, code_ref, low_ref, mine_ref, other_ref, rhs_ref, out_ref, panels, acc):
    r = place_ref[0]
    own = pl.multiple_of(place_ref[1] // 2 * W, W)
    for p in range(2):
        join(low_ref[p], panels, 4 * p)
    acc[...] = jnp.zeros_like(acc)
    for i in range(L1):
        x = (r * OWN + L0 + i) % X
        acc[x, pl.ds(own, W)] = -rhs_ref[:, (L0 + i) * SN : (L0 + i + 1) * SN].astype(F32)
    for side, tiles in enumerate((mine_ref, other_ref)):
        for q in range(SLOTS1):
            row = code_ref[side, q]
            slot = jnp.where(row < OWN, (r * OWN + row) % X, X)
            source = jnp.minimum(panel_of(code_ref[side, SLOTS + q]), LOWS - 1)
            acc[slot] += dot_nt(panels[source], tiles[0, q])
    for x in range(X):
        strips = acc[x].astype(BF16)
        for y in range(Y):
            out_ref[2 * y + x // 2, x % 2 * STRIP : x % 2 * STRIP + STRIP] = strips[y * STRIP :][:STRIP]


def mid_forward(place_ref, in_ref, dinv_ref, y_ref, spread_ref):
    right = -jnp.sum(in_ref[...].astype(F32), axis=0)
    rows = []
    for b in range(2):
        k = L0 + (place_ref[1] // 2 * 2 + b + 2 * place_ref[0]) % X
        rows.append(dot_nt(right[b * STRIP :][:STRIP].astype(BF16), dinv_ref[k]))
    y = jnp.concatenate(rows, axis=0).astype(BF16)
    y_ref[...] = y
    for z in range(Z):
        spread_ref[z] = y


def top_sums(code_ref, low_ref, mid_ref, mine_ref, other_ref, out_ref, panels, acc):
    for p in range(2):
        join(low_ref[p], panels, 4 * p)
        for b in range(2):
            for y in range(Y):
                strip = mid_ref[p, y, b * STRIP : (b + 1) * STRIP]
                panels[LOWS + 2 * p + b, y * STRIP : (y + 1) * STRIP] = strip
    acc[...] = jnp.zeros_like(acc)
    for side, tiles in enumerate((mine_ref, other_ref)):
        for q in range(SLOTS1, SLOTS):
            row = code_ref[side, q]
            slot = jnp.where(row < OWN, row - MID, L2)
            source = panel_of(code_ref[side, SLOTS + q])
            acc[slot] += dot_nt(panels[source], tiles[0, q])
    out_ref[...] = cut([acc[i] for i in range(L2)])


def top_solve(in_ref, rhs_ref, dinv_ref, x_ref, spread_ref):
    sums = jnp.sum(in_ref[...].astype(F32), axis=0)
    rows = []
    for i in range(L2):
        k = MID + i
        right = rhs_ref[:, k * SN : (k + 1) * SN].astype(F32) - sums[i * W : (i + 1) * W]
        y = dot_nt(right.astype(BF16), dinv_ref[k]).astype(BF16)
        rows.append(dot_nn(y, dinv_ref[k]))
    x = jnp.concatenate(rows, axis=0).astype(BF16)
    x_ref[...] = x
    for peer in range(PEERS):
        spread_ref[peer] = x


def top_carries(
    place_ref, code_ref, in_ref, mine_ref, other_ref, low_ref, keep_ref, out_ref, known, acc
):
    core = place_ref[0] % 2
    join(in_ref[...], known)
    acc[...] = jnp.zeros_like(acc)
    for side, tiles in enumerate((mine_ref, other_ref)):
        for q in range(SLOTS1, SLOTS):
            row = code_ref[side, q]
            source = jnp.clip(row - MID, 0, L2 - 1)
            slot = jnp.where(row < OWN, panel_of(code_ref[side, SLOTS + q]), LOWS + MIDS)
            acc[slot] += dot_nn(known[source], tiles[0, q])
    for p in range(LOWS):
        low_ref[p] = acc[p]
    for b in range(2):
        keep = acc[LOWS + 2 * core + b]
        sent = acc[LOWS + 2 * (1 - core) + b].astype(BF16)
        for y in range(Y):
            keep_ref[y, b * STRIP : (b + 1) * STRIP] = keep[y * STRIP : (y + 1) * STRIP]
            out_ref[y, b * STRIP : (b + 1) * STRIP] = sent[y * STRIP : (y + 1) * STRIP]


def mid_backward(place_ref, in_ref, y_ref, dinv_ref, spread_ref):
    left = y_ref[...].astype(F32) - jnp.sum(in_ref[...].astype(F32), axis=0)
    rows = []
    for b in range(2):
        k = L0 + (place_ref[1] // 2 * 2 + b + 2 * place_ref[0]) % X
        rows.append(dot_nn(left[b * STRIP :][:STRIP].astype(BF16), dinv_ref[k]))
    x = jnp.concatenate(rows, axis=0).astype(BF16)
    for peer in range(PEERS):
        spread_ref[peer] = x


def low_carries(
    place_ref,
    code_ref,
    in_ref,
    part_ref,
    mine_ref,
    other_ref,
    x_ref,
    keep_ref,
    out_ref,
    known,
    acc,
):
    r = place_ref[0]
    peer = place_ref[1] // 2
    core = r % 2
    for x in range(X):
        for y in range(Y):
            strip = in_ref[2 * y + x // 2, x % 2 * STRIP : x % 2 * STRIP + STRIP]
            known[x, y * STRIP : (y + 1) * STRIP] = strip
    own = []
    for i in range(L1):
        x = (r * OWN + L0 + i) % X
        strips = in_ref[peer // 2 * 2 + x // 2].astype(F32)
        octet = jnp.where(x % 2 == 0, strips[:STRIP], strips[STRIP:])
        own.append(jnp.where(peer % 2 == 0, octet[:W], octet[W:]))
    x_ref[...] = jnp.concatenate(own, axis=0).astype(BF16)
    for p in range(LOWS):
        acc[p] = part_ref[p]
    acc[LOWS] = jnp.zeros((N, SN), F32)
    for side, tiles in enumerate((mine_ref, other_ref)):
        for q in range(SLOTS1):
            row = code_ref[side, q]
            source = (r * OWN + row) % X
            panel = jnp.minimum(panel_of(code_ref[side, SLOTS + q]), LOWS - 1)
            slot = jnp.where(row < OWN, panel, LOWS)
            acc[slot] += dot_nn(known[source], tiles[0, q])
    keep_ref[...] = cut([acc[4 * core + i] for i in range(4)], F32)
    out_ref[...] = cut([acc[4 * (1 - core) + i] for i in range(4)])


def pair_sum(keep_ref, in_ref, out_ref):
    out_ref[...] = (keep_ref[...] + in_ref[...].astype(F32)).astype(BF16)


def low_by_row(place_ref, in_ref, out_ref):
    core = place_ref[0] % 2
    for z in range(Z):
        parts = []
        for k in range(L0):
            c = (28 * z + 14 * core + k) % C
            o = k // 4
            tile = in_ref[c // 2].astype(F32)
            parts.append(tile[(k % 2 * 2 + o) * W :][:W])
        out_ref[z] = jnp.concatenate(parts, axis=0).astype(BF16)


def low_backward(in_ref, y_ref, dinv_ref, mid_ref, top_ref, out_ref):
    carry = jnp.sum(in_ref[...].astype(F32), axis=0)
    left = (y_ref[...].astype(F32) - carry).reshape(L0, W, SN)
    for k in range(L0):
        out_ref[:, k * SN : (k + 1) * SN] = dot_nn(left[k].astype(BF16), dinv_ref[k]).astype(BF16)
    mid = mid_ref[...].astype(F32)
    for i in range(L1):
        out_ref[:, (L0 + i) * SN : (L0 + i + 1) * SN] = mid[i * W : (i + 1) * W].astype(BF16)
    top = top_ref[...].astype(F32)
    for i in range(L2):
        out_ref[:, (MID + i) * SN : (MID + i + 1) * SN] = top[i * W : (i + 1) * W].astype(BF16)


VM = pl.BlockSpec(memory_space=pltpu.VMEM)
SM = pl.BlockSpec(memory_space=pltpu.SMEM)


def call(kernel, outs, *args, scratch=()):
    single = len(outs) == 1
    shapes = [jax.ShapeDtypeStruct(shape, kind) for shape, kind in outs]
    return pl.pallas_call(
        kernel,
        out_shape=shapes[0] if single else shapes,
        in_specs=[SM if a.dtype == jnp.int32 else VM for a in args],
        out_specs=VM if single else [VM] * len(outs),
        scratch_shapes=list(scratch),
        compiler_params=pltpu.CompilerParams(vmem_limit_bytes=24 * 1024 * 1024),
    )(*args)


def over_peers(pieces):
    return lax.all_to_all(pieces, "col", 0, 0, tiled=True, axis_index_groups=PEER_GROUPS)


def over_y(pieces):
    return lax.all_to_all(pieces, "col", 0, 0, tiled=True, axis_index_groups=Y_GROUPS)


def over_z_by_y(pieces):
    return lax.all_to_all(pieces, ("row", "col"), 0, 0, tiled=True, axis_index_groups=MID_GROUPS)


def over_core(pieces):
    return lax.all_gather(pieces, "row", axis=0, axis_index_groups=CORE_GROUPS)


def swap(half):
    return lax.ppermute(half, "row", SWAP)


def over_z(pieces):
    return lax.all_to_all(pieces, "row", 0, 0, tiled=True, axis_index_groups=Z_GROUPS)


def on_device(rhs, dinv, blocks, block_row, block_col):
    place = jnp.stack([lax.axis_index("row"), lax.axis_index("col")]).astype(jnp.int32)
    right = rhs.T
    panels = pltpu.VMEM((LOWS + MIDS, N, SN), BF16)
    sums = pltpu.VMEM((LOWS + MIDS + 1, N, SN), F32)
    work = (panels, sums)
    others = lax.ppermute(blocks, "col", NEIGHBOURS)
    codes = jnp.concatenate([block_row, block_col], axis=1)
    code = jnp.concatenate([codes, lax.ppermute(codes, "col", NEIGHBOURS)])

    y_low, spread = call(low_forward, [((64, SN), BF16), ((Z, 64, SN), BF16)], right, dinv)
    sent = call(low_by_class, [((PEERS, 32, SN), BF16)], place, over_z(spread))
    low = over_core(over_peers(sent))
    part = call(
        mid_sums,
        [((PEERS, 2 * STRIP, SN), BF16)],
        place,
        code,
        low,
        blocks,
        others,
        right,
        scratch=work,
    )
    y_mid, spread = call(
        mid_forward,
        [((2 * STRIP, SN), BF16), ((Z, 2 * STRIP, SN), BF16)],
        place,
        over_peers(part),
        dinv,
    )
    mid = over_core(over_y(over_z_by_y(spread)))
    part = call(
        top_sums, [((PEERS, 16, SN), BF16)], code, low, mid, blocks, others, scratch=work
    )
    x_top, spread = call(
        top_solve, [((16, SN), BF16), ((PEERS, 16, SN), BF16)], over_peers(part), right, dinv
    )
    low_part, keep, sent = call(
        top_carries,
        [
            ((LOWS, N, SN), F32),
            ((Y, 2 * STRIP, SN), F32),
            ((Y, 2 * STRIP, SN), BF16),
        ],
        place,
        code,
        over_peers(spread),
        blocks,
        others,
        scratch=work,
    )
    both = call(pair_sum, [((Y, 2 * STRIP, SN), BF16)], keep, swap(sent))
    carry = over_z_by_y(over_y(both))
    spread = call(mid_backward, [((PEERS, 2 * STRIP, SN), BF16)], place, carry, y_mid, dinv)
    x_mid, keep, sent = call(
        low_carries,
        [((32, SN), BF16), ((PEERS, 32, SN), F32), ((PEERS, 32, SN), BF16)],
        place,
        code,
        over_peers(spread),
        low_part,
        blocks,
        others,
        scratch=work,
    )
    both = call(pair_sum, [((PEERS, 32, SN), BF16)], keep, swap(sent))
    sent = call(low_by_row, [((Z, 64, SN), BF16)], place, over_peers(both))
    out = call(low_backward, [((W, OWN * SN), BF16)], over_z(sent), y_low, dinv, x_mid, x_top)
    return out.T


def solution(mesh):
    placed = (
        P("row", "col"),
        P("row", None, None),
        P("row", "col", None, None),
        P("row", "col"),
        P("row", "col"),
    )
    return jax.shard_map(
        on_device, mesh=mesh, in_specs=placed, out_specs=P("row", "col"), check_vma=False
    )
```

```python
import jax
import jax.numpy as jnp
from jax import lax
from jax.experimental import pallas as pl
from jax.experimental.pallas import tpu as pltpu
from jax.sharding import PartitionSpec as P

SN = 256
L0 = 8
L1 = 4
L2 = 2
MID = L0 + L1
OWN = L0 + L1 + L2
SLOTS1 = 8
SLOTS = 14
R = 16
C = 32
X = 4
Y = 8
Z = 8
HALVES = 2
PEERS = Y * HALVES
W = 8
STRIP = W * HALVES
N = W * PEERS
LOWS = 8
MIDS = 4
F32 = jnp.float32
BF16 = jnp.bfloat16
Z_GROUPS = [[2 * z + core for z in range(Z)] for core in range(2)]
CORE_GROUPS = [[2 * z, 2 * z + 1] for z in range(Z)]
Y_GROUPS = [[X * y + x for y in range(Y)] for x in range(X)]
PEER_GROUPS = [[2 * peer + (side + peer) % 2 for peer in range(PEERS)] for side in range(2)]
SWAP = [(r, r ^ 1) for r in range(R)]
NEIGHBOURS = [(c, c ^ 1) for c in range(C)]


def mid_groups():
    groups = []
    for c in range(C):
        order = [0] * R
        for r in range(R):
            column = [s % C for s in range(r * OWN + L0, r * OWN + MID) if s % X == c % X][0]
            order[column // X * 2 + r % 2] = r * C + c
        groups.append(order)
    return groups


MID_GROUPS = mid_groups()


def dot_nt(left, right):
    return lax.dot_general(left, right, (((1,), (1,)), ((), ())), preferred_element_type=F32)


def dot_nn(left, right):
    return lax.dot_general(left, right, (((1,), (0,)), ((), ())), preferred_element_type=F32)


def low_panel(column):
    return column % (2 * OWN) // OWN * 4 + column % 2 * 2 + column % OWN // 4


def mid_panel(column):
    return column % (2 * OWN) // OWN * 2 + column % 2


def panel_of(column):
    return jnp.where(column % OWN < L0, low_panel(column), LOWS + mid_panel(column))


def join(pieces, out_ref, first=0):
    count = pieces.shape[1] // W
    wide = pieces.astype(F32).reshape(PEERS, count, W, SN)
    for i in range(count):
        out_ref[first + i] = wide[:, i].reshape(N, SN).astype(BF16)


def cut(panels, kind=BF16):
    parts = [p.reshape(PEERS, W, SN) for p in panels]
    return jnp.stack(parts, axis=1).reshape(PEERS, W * len(parts), SN).astype(kind)


def low_forward(rhs_ref, dinv_ref, y_ref, spread_ref):
    rows = []
    for k in range(L0):
        rows.append(dot_nt(rhs_ref[:, k * SN : (k + 1) * SN], dinv_ref[k]))
    y = jnp.concatenate(rows, axis=0).astype(BF16)
    y_ref[...] = y
    for z in range(Z):
        spread_ref[z] = y


def low_by_class(place_ref, in_ref, out_ref):
    core = place_ref[0] % 2
    for c in range(C):
        halves = []
        for o in range(2):
            a = (c + 2 * core) % 4
            z = (7 * ((c - 14 * core - a - 4 * o + 64) // 4)) % Z
            tile = in_ref[z, 32 * o : 32 * o + 32].astype(F32)
            piece = jnp.where(a == 0, tile[0:8], tile[8:16])
            other = jnp.where(a == 2, tile[16:24], tile[24:32])
            halves.append(jnp.where(a < 2, piece, other))
        out_ref[c // 2, c % 2 * 16 : c % 2 * 16 + 16] = jnp.concatenate(halves, axis=0).astype(BF16)


def mid_sums(place_ref, code_ref, low_ref, mine_ref, other_ref, rhs_ref, out_ref, panels, acc):
    r = place_ref[0]
    own = pl.multiple_of(place_ref[1] // 2 * W, W)
    for p in range(2):
        join(low_ref[p], panels, 4 * p)
    acc[...] = jnp.zeros_like(acc)
    for i in range(L1):
        x = (r * OWN + L0 + i) % X
        acc[x, pl.ds(own, W)] = -rhs_ref[:, (L0 + i) * SN : (L0 + i + 1) * SN].astype(F32)
    for side, tiles in enumerate((mine_ref, other_ref)):
        for q in range(SLOTS1):
            row = code_ref[side, q]
            slot = jnp.where(row < OWN, (r * OWN + row) % X, X)
            source = jnp.minimum(panel_of(code_ref[side, SLOTS + q]), LOWS - 1)
            acc[slot] += dot_nt(panels[source], tiles[0, q])
    for x in range(X):
        strips = acc[x].astype(BF16)
        for y in range(Y):
            out_ref[2 * y + x // 2, x % 2 * STRIP : x % 2 * STRIP + STRIP] = strips[y * STRIP :][:STRIP]


def mid_forward(place_ref, in_ref, dinv_ref, y_ref, spread_ref):
    right = -jnp.sum(in_ref[...].astype(F32), axis=0)
    rows = []
    for b in range(2):
        k = L0 + (place_ref[1] // 2 * 2 + b + 2 * place_ref[0]) % X
        rows.append(dot_nt(right[b * STRIP :][:STRIP].astype(BF16), dinv_ref[k]))
    y = jnp.concatenate(rows, axis=0).astype(BF16)
    y_ref[...] = y
    for r in range(R):
        spread_ref[r] = y


def top_sums(code_ref, low_ref, mid_ref, mine_ref, other_ref, out_ref, panels, acc):
    for p in range(2):
        join(low_ref[p], panels, 4 * p)
    for m in range(MIDS):
        for y in range(Y):
            strip = mid_ref[y, m * STRIP : (m + 1) * STRIP]
            panels[LOWS + m, y * STRIP : (y + 1) * STRIP] = strip
    acc[...] = jnp.zeros_like(acc)
    for side, tiles in enumerate((mine_ref, other_ref)):
        for q in range(SLOTS1, SLOTS):
            row = code_ref[side, q]
            slot = jnp.where(row < OWN, row - MID, L2)
            source = panel_of(code_ref[side, SLOTS + q])
            acc[slot] += dot_nt(panels[source], tiles[0, q - side * SLOTS1])
    out_ref[...] = cut([acc[i] for i in range(L2)])


def top_solve(in_ref, rhs_ref, dinv_ref, x_ref, spread_ref):
    sums = jnp.sum(in_ref[...].astype(F32), axis=0)
    rows = []
    for i in range(L2):
        k = MID + i
        right = rhs_ref[:, k * SN : (k + 1) * SN].astype(F32) - sums[i * W : (i + 1) * W]
        y = dot_nt(right.astype(BF16), dinv_ref[k]).astype(BF16)
        rows.append(dot_nn(y, dinv_ref[k]))
    x = jnp.concatenate(rows, axis=0).astype(BF16)
    x_ref[...] = x
    for peer in range(PEERS):
        spread_ref[peer] = x


def top_carries(
    code_ref, in_ref, mine_ref, other_ref, low_ref, out_ref, known, acc
):
    join(in_ref[...], known)
    acc[...] = jnp.zeros_like(acc)
    for side, tiles in enumerate((mine_ref, other_ref)):
        for q in range(SLOTS1, SLOTS):
            row = code_ref[side, q]
            source = jnp.clip(row - MID, 0, L2 - 1)
            slot = jnp.where(row < OWN, panel_of(code_ref[side, SLOTS + q]), LOWS + MIDS)
            acc[slot] += dot_nn(known[source], tiles[0, q - side * SLOTS1])
    for p in range(LOWS):
        low_ref[p] = acc[p]
    for m in range(MIDS):
        strips = acc[LOWS + m].astype(BF16)
        for y in range(Y):
            out_ref[y, m * STRIP : (m + 1) * STRIP] = strips[y * STRIP : (y + 1) * STRIP]


def mid_backward(place_ref, in_ref, y_ref, dinv_ref, spread_ref):
    left = y_ref[...].astype(F32) - jnp.sum(in_ref[...].astype(F32), axis=0)
    rows = []
    for b in range(2):
        k = L0 + (place_ref[1] // 2 * 2 + b + 2 * place_ref[0]) % X
        rows.append(dot_nn(left[b * STRIP :][:STRIP].astype(BF16), dinv_ref[k]))
    x = jnp.concatenate(rows, axis=0).astype(BF16)
    for peer in range(PEERS):
        spread_ref[peer] = x


def low_carries(
    place_ref,
    code_ref,
    in_ref,
    part_ref,
    mine_ref,
    other_ref,
    x_ref,
    keep_ref,
    out_ref,
    known,
    acc,
):
    r = place_ref[0]
    peer = place_ref[1] // 2
    core = r % 2
    for x in range(X):
        for y in range(Y):
            strip = in_ref[2 * y + x // 2, x % 2 * STRIP : x % 2 * STRIP + STRIP]
            known[x, y * STRIP : (y + 1) * STRIP] = strip
    own = []
    for i in range(L1):
        x = (r * OWN + L0 + i) % X
        strips = in_ref[peer // 2 * 2 + x // 2].astype(F32)
        octet = jnp.where(x % 2 == 0, strips[:STRIP], strips[STRIP:])
        own.append(jnp.where(peer % 2 == 0, octet[:W], octet[W:]))
    x_ref[...] = jnp.concatenate(own, axis=0).astype(BF16)
    for p in range(LOWS):
        acc[p] = part_ref[p]
    acc[LOWS] = jnp.zeros((N, SN), F32)
    for side, tiles in enumerate((mine_ref, other_ref)):
        for q in range(SLOTS1):
            row = code_ref[side, q]
            source = (r * OWN + row) % X
            panel = jnp.minimum(panel_of(code_ref[side, SLOTS + q]), LOWS - 1)
            slot = jnp.where(row < OWN, panel, LOWS)
            acc[slot] += dot_nn(known[source], tiles[0, q])
    keep_ref[...] = cut([acc[4 * core + i] for i in range(4)], F32)
    out_ref[...] = cut([acc[4 * (1 - core) + i] for i in range(4)])


def pair_sum(keep_ref, in_ref, out_ref):
    out_ref[...] = (keep_ref[...] + in_ref[...].astype(F32)).astype(BF16)


def low_by_row(place_ref, in_ref, out_ref):
    core = place_ref[0] % 2
    for z in range(Z):
        parts = []
        for k in range(L0):
            c = (28 * z + 14 * core + k) % C
            o = k // 4
            tile = in_ref[c // 2].astype(F32)
            parts.append(tile[(k % 2 * 2 + o) * W :][:W])
        out_ref[z] = jnp.concatenate(parts, axis=0).astype(BF16)


def low_backward(in_ref, y_ref, dinv_ref, mid_ref, top_ref, out_ref):
    carry = jnp.sum(in_ref[...].astype(F32), axis=0)
    left = (y_ref[...].astype(F32) - carry).reshape(L0, W, SN)
    for k in range(L0):
        out_ref[:, k * SN : (k + 1) * SN] = dot_nn(left[k].astype(BF16), dinv_ref[k]).astype(BF16)
    mid = mid_ref[...].astype(F32)
    for i in range(L1):
        out_ref[:, (L0 + i) * SN : (L0 + i + 1) * SN] = mid[i * W : (i + 1) * W].astype(BF16)
    top = top_ref[...].astype(F32)
    for i in range(L2):
        out_ref[:, (MID + i) * SN : (MID + i + 1) * SN] = top[i * W : (i + 1) * W].astype(BF16)


VM = pl.BlockSpec(memory_space=pltpu.VMEM)
SM = pl.BlockSpec(memory_space=pltpu.SMEM)


def call(kernel, outs, *args, scratch=()):
    single = len(outs) == 1
    shapes = [jax.ShapeDtypeStruct(shape, kind) for shape, kind in outs]
    return pl.pallas_call(
        kernel,
        out_shape=shapes[0] if single else shapes,
        in_specs=[SM if a.dtype == jnp.int32 else VM for a in args],
        out_specs=VM if single else [VM] * len(outs),
        scratch_shapes=list(scratch),
        compiler_params=pltpu.CompilerParams(vmem_limit_bytes=24 * 1024 * 1024),
    )(*args)


def over_peers(pieces):
    return lax.all_to_all(pieces, "col", 0, 0, tiled=True, axis_index_groups=PEER_GROUPS)


def over_y(pieces):
    return lax.all_to_all(pieces, "col", 0, 0, tiled=True, axis_index_groups=Y_GROUPS)


def over_row_by_y(pieces):
    return lax.all_to_all(pieces, ("row", "col"), 0, 0, tiled=True, axis_index_groups=MID_GROUPS)


def over_core(pieces):
    return lax.all_gather(pieces, "row", axis=0, axis_index_groups=CORE_GROUPS)


def swap(half):
    return lax.ppermute(half, "row", SWAP)


def over_z(pieces):
    return lax.all_to_all(pieces, "row", 0, 0, tiled=True, axis_index_groups=Z_GROUPS)


def on_device(rhs, dinv, blocks, block_row, block_col):
    place = jnp.stack([lax.axis_index("row"), lax.axis_index("col")]).astype(jnp.int32)
    right = rhs.T
    panels = pltpu.VMEM((LOWS + MIDS, N, SN), BF16)
    sums = pltpu.VMEM((LOWS + MIDS + 1, N, SN), F32)
    work = (panels, sums)
    codes = jnp.concatenate([block_row, block_col], axis=1)
    others = lax.ppermute(blocks[:, :SLOTS1], "col", NEIGHBOURS)
    code = jnp.concatenate([codes, lax.ppermute(codes, "col", NEIGHBOURS)])
    right, code = lax.optimization_barrier((right, code))

    y_low, spread = call(low_forward, [((64, SN), BF16), ((Z, 64, SN), BF16)], right, dinv)
    sent = call(low_by_class, [((PEERS, 32, SN), BF16)], place, over_z(spread))
    low = over_core(over_peers(sent))
    part = call(
        mid_sums,
        [((PEERS, 2 * STRIP, SN), BF16)],
        place,
        code,
        low,
        blocks,
        others,
        right,
        scratch=work,
    )
    rest, part = lax.optimization_barrier((blocks[:, SLOTS1:], part))
    rest = lax.ppermute(rest, "col", NEIGHBOURS)
    y_mid, spread = call(
        mid_forward,
        [((2 * STRIP, SN), BF16), ((R, 2 * STRIP, SN), BF16)],
        place,
        over_peers(part),
        dinv,
    )
    mid = over_y(over_row_by_y(spread).reshape(Y, 4 * STRIP, SN))
    part = call(top_sums, [((PEERS, 16, SN), BF16)], code, low, mid, blocks, rest, scratch=work)
    x_top, spread = call(
        top_solve, [((16, SN), BF16), ((PEERS, 16, SN), BF16)], over_peers(part), right, dinv
    )
    low_part, sent = call(
        top_carries,
        [((LOWS, N, SN), F32), ((Y, 4 * STRIP, SN), BF16)],
        code,
        over_peers(spread),
        blocks,
        rest,
        scratch=work,
    )
    carry = over_row_by_y(over_y(sent).reshape(R, 2 * STRIP, SN))
    spread = call(mid_backward, [((PEERS, 2 * STRIP, SN), BF16)], place, carry, y_mid, dinv)
    x_mid, keep, sent = call(
        low_carries,
        [((32, SN), BF16), ((PEERS, 32, SN), F32), ((PEERS, 32, SN), BF16)],
        place,
        code,
        over_peers(spread),
        low_part,
        blocks,
        others,
        scratch=work,
    )
    both = call(pair_sum, [((PEERS, 32, SN), BF16)], keep, swap(sent))
    sent = call(low_by_row, [((Z, 64, SN), BF16)], place, over_peers(both))
    out = call(low_backward, [((W, OWN * SN), BF16)], over_z(sent), y_low, dinv, x_mid, x_top)
    return out.T


def solution(mesh):
    placed = (
        P("row", "col"),
        P("row", None, None),
        P("row", "col", None, None),
        P("row", "col"),
        P("row", "col"),
    )
    return jax.shard_map(
        on_device, mesh=mesh, in_specs=placed, out_specs=P("row", "col"), check_vma=False
    )
```

```python
import jax
import jax.numpy as jnp
from jax import lax
from jax.experimental import pallas as pl
from jax.experimental.pallas import tpu as pltpu
from jax.sharding import PartitionSpec as P

SN = 256
L0 = 8
L1 = 4
L2 = 2
MID = L0 + L1
OWN = L0 + L1 + L2
SLOTS1 = 8
SLOTS = 14
R = 16
C = 32
X = 4
Y = 8
Z = 8
HALVES = 2
PEERS = Y * HALVES
W = 8
STRIP = W * HALVES
N = W * PEERS
LOWS = 8
MIDS = 4
F32 = jnp.float32
BF16 = jnp.bfloat16
Z_GROUPS = [[2 * z + core for z in range(Z)] for core in range(2)]
CORE_GROUPS = [[2 * z, 2 * z + 1] for z in range(Z)]
Y_GROUPS = [[X * y + x for y in range(Y)] for x in range(X)]
PEER_GROUPS = [[2 * peer + (side + peer) % 2 for peer in range(PEERS)] for side in range(2)]
SWAP = [(r, r ^ 1) for r in range(R)]
NEIGHBOURS = [(c, c ^ 1) for c in range(C)]


def mid_groups():
    groups = []
    for core in range(2):
        for c in range(C):
            by_y = [0] * Y
            for z in range(Z):
                r = 2 * z + core
                column = [s % C for s in range(r * OWN + L0, r * OWN + MID) if s % X == c % X][0]
                by_y[column // X] = r * C + c
            groups.append(by_y)
    return groups


MID_GROUPS = mid_groups()


def dot_nt(left, right):
    return lax.dot_general(left, right, (((1,), (1,)), ((), ())), preferred_element_type=F32)


def dot_nn(left, right):
    return lax.dot_general(left, right, (((1,), (0,)), ((), ())), preferred_element_type=F32)


def low_panel(column):
    return column % (2 * OWN) // OWN * 4 + column % 2 * 2 + column % OWN // 4


def mid_panel(column):
    return column % (2 * OWN) // OWN * 2 + column % 2


def panel_of(column):
    return jnp.where(column % OWN < L0, low_panel(column), LOWS + mid_panel(column))


def join(pieces, out_ref, first=0):
    count = pieces.shape[1] // W
    wide = pieces.astype(F32).reshape(PEERS, count, W, SN)
    for i in range(count):
        out_ref[first + i] = wide[:, i].reshape(N, SN).astype(BF16)


def cut(panels, kind=BF16):
    parts = [p.reshape(PEERS, W, SN) for p in panels]
    return jnp.stack(parts, axis=1).reshape(PEERS, W * len(parts), SN).astype(kind)


def slots(row_ref, col_ref, far_ref, mine_ref, other_ref, first, final):
    for q in range(first, final):
        yield row_ref[0, q], col_ref[0, q], mine_ref[0, q]
    for q in range(first, final):
        tile = other_ref[(q - first) * SN : (q - first + 1) * SN]
        yield far_ref[0, q], far_ref[0, 128 + q], tile


def low_forward(
    rhs_ref, row_ref, col_ref, dinv_ref, blocks_ref, y_ref, spread_ref, sent_ref, factors, tail, sems
):
    fetch = [pltpu.make_async_copy(dinv_ref.at[k], factors.at[k], sems.at[k]) for k in range(L0)]
    for copy in fetch:
        copy.start()
    pack = []
    for q in range(SLOTS1):
        target = sent_ref.at[pl.ds(q * SN, SN)]
        pack.append(pltpu.make_async_copy(blocks_ref.at[0, q], target, sems.at[L0 + q]))
    tail[...] = jnp.zeros_like(tail)
    tail[:, :SLOTS] = jnp.broadcast_to(row_ref[...].astype(F32), (16, SLOTS)).astype(BF16)
    tail[:, 128 : 128 + SLOTS] = jnp.broadcast_to(col_ref[...].astype(F32), (16, SLOTS)).astype(BF16)
    pack.append(
        pltpu.make_async_copy(tail, sent_ref.at[pl.ds(SLOTS1 * SN, 16)], sems.at[L0 + SLOTS1])
    )
    for copy in pack:
        copy.start()
    rows = []
    for k in range(L0):
        fetch[k].wait()
        rows.append(dot_nt(rhs_ref[:, k * SN : (k + 1) * SN], factors[k]))
    y = jnp.concatenate(rows, axis=0).astype(BF16)
    y_ref[...] = y
    for z in range(Z):
        spread_ref[z] = y
    for copy in pack:
        copy.wait()


def low_by_class(place_ref, in_ref, out_ref):
    core = place_ref[0] % 2
    for c in range(C):
        halves = []
        for o in range(2):
            a = (c + 2 * core) % 4
            z = (7 * ((c - 14 * core - a - 4 * o + 64) // 4)) % Z
            tile = in_ref[z, 32 * o : 32 * o + 32].astype(F32)
            piece = jnp.where(a == 0, tile[0:8], tile[8:16])
            other = jnp.where(a == 2, tile[16:24], tile[24:32])
            halves.append(jnp.where(a < 2, piece, other))
        out_ref[c // 2, c % 2 * 16 : c % 2 * 16 + 16] = jnp.concatenate(halves, axis=0).astype(BF16)


def mid_sums(place_ref, row_ref, col_ref, far_ref, low_ref, mine_ref, other_ref, rhs_ref, out_ref, panels, acc):
    r = place_ref[0]
    own = pl.multiple_of(place_ref[1] // 2 * W, W)
    for p in range(2):
        join(low_ref[p], panels, 4 * p)
    acc[...] = jnp.zeros_like(acc)
    for i in range(L1):
        x = (r * OWN + L0 + i) % X
        acc[x, pl.ds(own, W)] = -rhs_ref[:, (L0 + i) * SN : (L0 + i + 1) * SN].astype(F32)
    for row, column, tile in slots(row_ref, col_ref, far_ref, mine_ref, other_ref, 0, SLOTS1):
        slot = jnp.where(row < OWN, (r * OWN + row) % X, X)
        source = jnp.minimum(panel_of(column), LOWS - 1)
        acc[slot] += dot_nt(panels[source], tile)
    for x in range(X):
        strips = acc[x].astype(BF16)
        for y in range(Y):
            out_ref[2 * y + x // 2, x % 2 * STRIP : x % 2 * STRIP + STRIP] = strips[y * STRIP :][:STRIP]


def mid_forward(place_ref, in_ref, dinv_ref, y_ref, spread_ref):
    right = -jnp.sum(in_ref[...].astype(F32), axis=0)
    rows = []
    for b in range(2):
        k = L0 + (place_ref[1] // 2 * 2 + b + 2 * place_ref[0]) % X
        rows.append(dot_nt(right[b * STRIP :][:STRIP].astype(BF16), dinv_ref[k]))
    y = jnp.concatenate(rows, axis=0).astype(BF16)
    y_ref[...] = y
    for z in range(Z):
        spread_ref[z] = y


def top_sums(row_ref, col_ref, far_ref, low_ref, mid_ref, mine_ref, other_ref, out_ref, panels, acc):
    for p in range(2):
        join(low_ref[p], panels, 4 * p)
        for b in range(2):
            for y in range(Y):
                strip = mid_ref[p, y, b * STRIP : (b + 1) * STRIP]
                panels[LOWS + 2 * p + b, y * STRIP : (y + 1) * STRIP] = strip
    acc[...] = jnp.zeros_like(acc)
    for row, column, tile in slots(row_ref, col_ref, far_ref, mine_ref, other_ref, SLOTS1, SLOTS):
        slot = jnp.where(row < OWN, row - MID, L2)
        source = panel_of(column)
        acc[slot] += dot_nt(panels[source], tile)
    out_ref[...] = cut([acc[i] for i in range(L2)])


def top_solve(in_ref, rhs_ref, dinv_ref, x_ref, spread_ref):
    sums = jnp.sum(in_ref[...].astype(F32), axis=0)
    rows = []
    for i in range(L2):
        k = MID + i
        right = rhs_ref[:, k * SN : (k + 1) * SN].astype(F32) - sums[i * W : (i + 1) * W]
        y = dot_nt(right.astype(BF16), dinv_ref[k]).astype(BF16)
        rows.append(dot_nn(y, dinv_ref[k]))
    x = jnp.concatenate(rows, axis=0).astype(BF16)
    x_ref[...] = x
    for peer in range(PEERS):
        spread_ref[peer] = x


def top_carries(
    place_ref, row_ref, col_ref, far_ref, in_ref, mine_ref, other_ref, low_ref, keep_ref, out_ref, known, acc
):
    core = place_ref[0] % 2
    join(in_ref[...], known)
    acc[...] = jnp.zeros_like(acc)
    for row, column, tile in slots(row_ref, col_ref, far_ref, mine_ref, other_ref, SLOTS1, SLOTS):
        source = jnp.clip(row - MID, 0, L2 - 1)
        slot = jnp.where(row < OWN, panel_of(column), LOWS + MIDS)
        acc[slot] += dot_nn(known[source], tile)
    for p in range(LOWS):
        low_ref[p] = acc[p]
    for b in range(2):
        keep = acc[LOWS + 2 * core + b]
        sent = acc[LOWS + 2 * (1 - core) + b].astype(BF16)
        for y in range(Y):
            keep_ref[y, b * STRIP : (b + 1) * STRIP] = keep[y * STRIP : (y + 1) * STRIP]
            out_ref[y, b * STRIP : (b + 1) * STRIP] = sent[y * STRIP : (y + 1) * STRIP]


def mid_backward(place_ref, in_ref, y_ref, dinv_ref, spread_ref):
    left = y_ref[...].astype(F32) - jnp.sum(in_ref[...].astype(F32), axis=0)
    rows = []
    for b in range(2):
        k = L0 + (place_ref[1] // 2 * 2 + b + 2 * place_ref[0]) % X
        rows.append(dot_nn(left[b * STRIP :][:STRIP].astype(BF16), dinv_ref[k]))
    x = jnp.concatenate(rows, axis=0).astype(BF16)
    for peer in range(PEERS):
        spread_ref[peer] = x


def low_carries(
    place_ref,
    row_ref,
    col_ref,
    far_ref,
    in_ref,
    part_ref,
    mine_ref,
    other_ref,
    x_ref,
    keep_ref,
    out_ref,
    known,
    acc,
):
    r = place_ref[0]
    peer = place_ref[1] // 2
    core = r % 2
    for x in range(X):
        for y in range(Y):
            strip = in_ref[2 * y + x // 2, x % 2 * STRIP : x % 2 * STRIP + STRIP]
            known[x, y * STRIP : (y + 1) * STRIP] = strip
    own = []
    for i in range(L1):
        x = (r * OWN + L0 + i) % X
        strips = in_ref[peer // 2 * 2 + x // 2].astype(F32)
        octet = jnp.where(x % 2 == 0, strips[:STRIP], strips[STRIP:])
        own.append(jnp.where(peer % 2 == 0, octet[:W], octet[W:]))
    x_ref[...] = jnp.concatenate(own, axis=0).astype(BF16)
    for p in range(LOWS):
        acc[p] = part_ref[p]
    acc[LOWS] = jnp.zeros((N, SN), F32)
    for row, column, tile in slots(row_ref, col_ref, far_ref, mine_ref, other_ref, 0, SLOTS1):
        source = (r * OWN + row) % X
        panel = jnp.minimum(panel_of(column), LOWS - 1)
        slot = jnp.where(row < OWN, panel, LOWS)
        acc[slot] += dot_nn(known[source], tile)
    keep_ref[...] = cut([acc[4 * core + i] for i in range(4)], F32)
    out_ref[...] = cut([acc[4 * (1 - core) + i] for i in range(4)])


def pair_sum(keep_ref, in_ref, out_ref):
    out_ref[...] = (keep_ref[...] + in_ref[...].astype(F32)).astype(BF16)


def low_by_row(place_ref, in_ref, out_ref):
    core = place_ref[0] % 2
    for z in range(Z):
        parts = []
        for k in range(L0):
            c = (28 * z + 14 * core + k) % C
            o = k // 4
            tile = in_ref[c // 2].astype(F32)
            parts.append(tile[(k % 2 * 2 + o) * W :][:W])
        out_ref[z] = jnp.concatenate(parts, axis=0).astype(BF16)


def low_backward(in_ref, y_ref, dinv_ref, mid_ref, top_ref, out_ref):
    carry = jnp.sum(in_ref[...].astype(F32), axis=0)
    left = (y_ref[...].astype(F32) - carry).reshape(L0, W, SN)
    for k in range(L0):
        out_ref[:, k * SN : (k + 1) * SN] = dot_nn(left[k].astype(BF16), dinv_ref[k]).astype(BF16)
    mid = mid_ref[...].astype(F32)
    for i in range(L1):
        out_ref[:, (L0 + i) * SN : (L0 + i + 1) * SN] = mid[i * W : (i + 1) * W].astype(BF16)
    top = top_ref[...].astype(F32)
    for i in range(L2):
        out_ref[:, (MID + i) * SN : (MID + i + 1) * SN] = top[i * W : (i + 1) * W].astype(BF16)


VM = pl.BlockSpec(memory_space=pltpu.VMEM)
SM = pl.BlockSpec(memory_space=pltpu.SMEM)


def call(kernel, outs, *args, scratch=()):
    single = len(outs) == 1
    shapes = [jax.ShapeDtypeStruct(shape, kind) for shape, kind in outs]
    return pl.pallas_call(
        kernel,
        out_shape=shapes[0] if single else shapes,
        in_specs=[SM if a.dtype == jnp.int32 else VM for a in args],
        out_specs=VM if single else [VM] * len(outs),
        scratch_shapes=list(scratch),
        compiler_params=pltpu.CompilerParams(vmem_limit_bytes=24 * 1024 * 1024),
    )(*args)


def over_peers(pieces):
    return lax.all_to_all(pieces, "col", 0, 0, tiled=True, axis_index_groups=PEER_GROUPS)


def over_y(pieces):
    return lax.all_to_all(pieces, "col", 0, 0, tiled=True, axis_index_groups=Y_GROUPS)


def over_z_by_y(pieces):
    return lax.all_to_all(pieces, ("row", "col"), 0, 0, tiled=True, axis_index_groups=MID_GROUPS)


def over_core(pieces):
    return lax.all_gather(pieces, "row", axis=0, axis_index_groups=CORE_GROUPS)


def swap(half):
    return lax.ppermute(half, "row", SWAP)


def over_z(pieces):
    return lax.all_to_all(pieces, "row", 0, 0, tiled=True, axis_index_groups=Z_GROUPS)


def on_device(rhs, dinv, blocks, block_row, block_col):
    place = jnp.stack([lax.axis_index("row"), lax.axis_index("col")]).astype(jnp.int32)
    right = rhs.T
    panels = pltpu.VMEM((LOWS + MIDS, N, SN), BF16)
    sums = pltpu.VMEM((LOWS + MIDS + 1, N, SN), F32)
    work = (panels, sums)
    whole = pl.BlockSpec(memory_space=pl.ANY)
    y_low, spread, packed = pl.pallas_call(
        low_forward,
        out_shape=[
            jax.ShapeDtypeStruct((64, SN), BF16),
            jax.ShapeDtypeStruct((Z, 64, SN), BF16),
            jax.ShapeDtypeStruct((SLOTS1 * SN + 16, SN), BF16),
        ],
        in_specs=[VM, VM, VM, whole, whole],
        out_specs=[VM, VM, whole],
        scratch_shapes=[
            pltpu.VMEM((L0, SN, SN), BF16),
            pltpu.VMEM((16, SN), BF16),
            pltpu.SemaphoreType.DMA((L0 + SLOTS1 + 1,)),
        ],
        compiler_params=pltpu.CompilerParams(vmem_limit_bytes=62 * 1062 * 1062),
    )(right, block_row, block_col, dinv, blocks)
    lower = lax.ppermute(packed, "col", NEIGHBOURS)
    far = lower[-16:-15].astype(jnp.int32)
    lists = (block_row, block_col, far)

    sent = call(low_by_class, [((PEERS, 32, SN), BF16)], place, over_z(spread))
    low = over_core(over_peers(sent))
    part = call(
        mid_sums,
        [((PEERS, 2 * STRIP, SN), BF16)],
        place,
        *lists,
        low,
        blocks,
        lower,
        right,
        scratch=work,
    )
    upper, part = lax.optimization_barrier((blocks[0, SLOTS1:].reshape(-1, SN), part))
    upper = lax.ppermute(upper, "col", NEIGHBOURS)
    y_mid, spread = call(
        mid_forward,
        [((2 * STRIP, SN), BF16), ((Z, 2 * STRIP, SN), BF16)],
        place,
        over_peers(part),
        dinv,
    )
    mid = over_core(over_y(over_z_by_y(spread)))
    part = call(
        top_sums, [((PEERS, 16, SN), BF16)], *lists, low, mid, blocks, upper, scratch=work
    )
    x_top, spread = call(
        top_solve, [((16, SN), BF16), ((PEERS, 16, SN), BF16)], over_peers(part), right, dinv
    )
    low_part, keep, sent = call(
        top_carries,
        [
            ((LOWS, N, SN), F32),
            ((Y, 2 * STRIP, SN), F32),
            ((Y, 2 * STRIP, SN), BF16),
        ],
        place,
        *lists,
        over_peers(spread),
        blocks,
        upper,
        scratch=work,
    )
    both = call(pair_sum, [((Y, 2 * STRIP, SN), BF16)], keep, swap(sent))
    carry = over_z_by_y(over_y(both))
    spread = call(mid_backward, [((PEERS, 2 * STRIP, SN), BF16)], place, carry, y_mid, dinv)
    x_mid, keep, sent = call(
        low_carries,
        [((32, SN), BF16), ((PEERS, 32, SN), F32), ((PEERS, 32, SN), BF16)],
        place,
        *lists,
        over_peers(spread),
        low_part,
        blocks,
        lower,
        scratch=work,
    )
    both = call(pair_sum, [((PEERS, 32, SN), BF16)], keep, swap(sent))
    sent = call(low_by_row, [((Z, 64, SN), BF16)], place, over_peers(both))
    out = call(low_backward, [((W, OWN * SN), BF16)], over_z(sent), y_low, dinv, x_mid, x_top)
    return out.T


def solution(mesh):
    placed = (
        P("row", "col"),
        P("row", None, None),
        P("row", "col", None, None),
        P("row", "col"),
        P("row", "col"),
    )
    return jax.shard_map(
        on_device, mesh=mesh, in_specs=placed, out_specs=P("row", "col"), check_vma=False
    )
```

```python
import jax
import jax.numpy as jnp
from jax import lax
from jax.experimental import pallas as pl
from jax.experimental.pallas import tpu as pltpu
from jax.sharding import PartitionSpec as P

SN = 256
L0 = 8
L1 = 4
L2 = 2
MID = L0 + L1
OWN = L0 + L1 + L2
SLOTS1 = 8
SLOTS = 14
R = 16
C = 32
X = 4
Y = 8
Z = 8
HALVES = 2
PEERS = Y * HALVES
W = 8
STRIP = W * HALVES
N = W * PEERS
LOWS = 8
MIDS = 4
F32 = jnp.float32
BF16 = jnp.bfloat16
Z_GROUPS = [[2 * z + core for z in range(Z)] for core in range(2)]
CORE_GROUPS = [[2 * z, 2 * z + 1] for z in range(Z)]
Y_GROUPS = [[X * y + x for y in range(Y)] for x in range(X)]
PEER_GROUPS = [[2 * peer + (side + peer) % 2 for peer in range(PEERS)] for side in range(2)]
SWAP = [(r, r ^ 1) for r in range(R)]
NEIGHBOURS = [(c, c ^ 1) for c in range(C)]


def mid_groups():
    groups = []
    for core in range(2):
        for c in range(C):
            by_y = [0] * Y
            for z in range(Z):
                r = 2 * z + core
                column = [s % C for s in range(r * OWN + L0, r * OWN + MID) if s % X == c % X][0]
                by_y[column // X] = r * C + c
            groups.append(by_y)
    return groups


MID_GROUPS = mid_groups()


def dot_nt(left, right):
    return lax.dot_general(left, right, (((1,), (1,)), ((), ())), preferred_element_type=F32)


def dot_nn(left, right):
    return lax.dot_general(left, right, (((1,), (0,)), ((), ())), preferred_element_type=F32)


def low_panel(column):
    return column % (2 * OWN) // OWN * 4 + column % 2 * 2 + column % OWN // 4


def mid_panel(column):
    return column % (2 * OWN) // OWN * 2 + column % 2


def panel_of(column):
    return jnp.where(column % OWN < L0, low_panel(column), LOWS + mid_panel(column))


def join(pieces, out_ref, first=0):
    count = pieces.shape[1] // W
    wide = pieces.astype(F32).reshape(PEERS, count, W, SN)
    for i in range(count):
        out_ref[first + i] = wide[:, i].reshape(N, SN).astype(BF16)


def cut(panels, kind=BF16):
    parts = [p.reshape(PEERS, W, SN) for p in panels]
    return jnp.stack(parts, axis=1).reshape(PEERS, W * len(parts), SN).astype(kind)


def slots(row_ref, col_ref, far_ref, mine_ref, other_ref, first, final):
    for q in range(first, final):
        yield row_ref[0, q], col_ref[0, q], mine_ref[0, q]
    for q in range(first, final):
        tile = other_ref[(q - first) * SN : (q - first + 1) * SN]
        yield far_ref[0, q], far_ref[0, 128 + q], tile


def low_forward(
    rhs_ref, row_ref, col_ref, dinv_ref, blocks_ref, y_ref, spread_ref, sent_ref, factors, sems
):
    fetch = [pltpu.make_async_copy(dinv_ref.at[k], factors.at[k], sems.at[k]) for k in range(L0)]
    for copy in fetch:
        copy.start()
    pack = []
    for q in range(SLOTS1):
        target = sent_ref.at[pl.ds(q * SN, SN)]
        pack.append(pltpu.make_async_copy(blocks_ref.at[0, q], target, sems.at[L0 + q]))
    for copy in pack:
        copy.start()
    last = SLOTS1 * SN
    sent_ref[last:] = jnp.zeros((16, SN), BF16)
    sent_ref[last:, :SLOTS] = jnp.broadcast_to(row_ref[...].astype(F32), (16, SLOTS)).astype(BF16)
    sent_ref[last:, 128 : 128 + SLOTS] = jnp.broadcast_to(
        col_ref[...].astype(F32), (16, SLOTS)
    ).astype(BF16)
    rows = []
    for k in range(L0):
        fetch[k].wait()
        rows.append(dot_nt(rhs_ref[:, k * SN : (k + 1) * SN], factors[k]))
    y = jnp.concatenate(rows, axis=0).astype(BF16)
    y_ref[...] = y
    for z in range(Z):
        spread_ref[z] = y
    for copy in pack:
        copy.wait()


def low_by_class(place_ref, in_ref, out_ref):
    core = place_ref[0] % 2
    for c in range(C):
        halves = []
        for o in range(2):
            a = (c + 2 * core) % 4
            z = (7 * ((c - 14 * core - a - 4 * o + 64) // 4)) % Z
            tile = in_ref[z, 32 * o : 32 * o + 32].astype(F32)
            piece = jnp.where(a == 0, tile[0:8], tile[8:16])
            other = jnp.where(a == 2, tile[16:24], tile[24:32])
            halves.append(jnp.where(a < 2, piece, other))
        out_ref[c // 2, c % 2 * 16 : c % 2 * 16 + 16] = jnp.concatenate(halves, axis=0).astype(BF16)


def mid_sums(place_ref, row_ref, col_ref, far_ref, low_ref, mine_ref, other_ref, rhs_ref, out_ref, panels, acc):
    r = place_ref[0]
    own = pl.multiple_of(place_ref[1] // 2 * W, W)
    for p in range(2):
        join(low_ref[p], panels, 4 * p)
    acc[...] = jnp.zeros_like(acc)
    for i in range(L1):
        x = (r * OWN + L0 + i) % X
        acc[x, pl.ds(own, W)] = -rhs_ref[:, (L0 + i) * SN : (L0 + i + 1) * SN].astype(F32)
    for row, column, tile in slots(row_ref, col_ref, far_ref, mine_ref, other_ref, 0, SLOTS1):
        slot = jnp.where(row < OWN, (r * OWN + row) % X, X)
        source = jnp.minimum(panel_of(column), LOWS - 1)
        acc[slot] += dot_nt(panels[source], tile)
    for x in range(X):
        strips = acc[x].astype(BF16)
        for y in range(Y):
            out_ref[2 * y + x // 2, x % 2 * STRIP : x % 2 * STRIP + STRIP] = strips[y * STRIP :][:STRIP]


def mid_forward(place_ref, in_ref, dinv_ref, y_ref, spread_ref):
    right = -jnp.sum(in_ref[...].astype(F32), axis=0)
    rows = []
    for b in range(2):
        k = L0 + (place_ref[1] // 2 * 2 + b + 2 * place_ref[0]) % X
        rows.append(dot_nt(right[b * STRIP :][:STRIP].astype(BF16), dinv_ref[k]))
    y = jnp.concatenate(rows, axis=0).astype(BF16)
    y_ref[...] = y
    for z in range(Z):
        spread_ref[z] = y


def top_sums(row_ref, col_ref, far_ref, low_ref, mid_ref, mine_ref, other_ref, out_ref, panels, acc):
    for p in range(2):
        join(low_ref[p], panels, 4 * p)
        for b in range(2):
            for y in range(Y):
                strip = mid_ref[p, y, b * STRIP : (b + 1) * STRIP]
                panels[LOWS + 2 * p + b, y * STRIP : (y + 1) * STRIP] = strip
    acc[...] = jnp.zeros_like(acc)
    for row, column, tile in slots(row_ref, col_ref, far_ref, mine_ref, other_ref, SLOTS1, SLOTS):
        slot = jnp.where(row < OWN, row - MID, L2)
        source = panel_of(column)
        acc[slot] += dot_nt(panels[source], tile)
    out_ref[...] = cut([acc[i] for i in range(L2)])


def top_solve(in_ref, rhs_ref, dinv_ref, x_ref, spread_ref):
    sums = jnp.sum(in_ref[...].astype(F32), axis=0)
    rows = []
    for i in range(L2):
        k = MID + i
        right = rhs_ref[:, k * SN : (k + 1) * SN].astype(F32) - sums[i * W : (i + 1) * W]
        y = dot_nt(right.astype(BF16), dinv_ref[k]).astype(BF16)
        rows.append(dot_nn(y, dinv_ref[k]))
    x = jnp.concatenate(rows, axis=0).astype(BF16)
    x_ref[...] = x
    for peer in range(PEERS):
        spread_ref[peer] = x


def top_carries(
    place_ref, row_ref, col_ref, far_ref, in_ref, mine_ref, other_ref, low_ref, keep_ref, out_ref, known, acc
):
    core = place_ref[0] % 2
    join(in_ref[...], known)
    acc[...] = jnp.zeros_like(acc)
    for row, column, tile in slots(row_ref, col_ref, far_ref, mine_ref, other_ref, SLOTS1, SLOTS):
        source = jnp.clip(row - MID, 0, L2 - 1)
        slot = jnp.where(row < OWN, panel_of(column), LOWS + MIDS)
        acc[slot] += dot_nn(known[source], tile)
    for p in range(LOWS):
        low_ref[p] = acc[p]
    for b in range(2):
        keep = acc[LOWS + 2 * core + b]
        sent = acc[LOWS + 2 * (1 - core) + b].astype(BF16)
        for y in range(Y):
            keep_ref[y, b * STRIP : (b + 1) * STRIP] = keep[y * STRIP : (y + 1) * STRIP]
            out_ref[y, b * STRIP : (b + 1) * STRIP] = sent[y * STRIP : (y + 1) * STRIP]


def mid_backward(place_ref, in_ref, y_ref, dinv_ref, spread_ref):
    left = y_ref[...].astype(F32) - jnp.sum(in_ref[...].astype(F32), axis=0)
    rows = []
    for b in range(2):
        k = L0 + (place_ref[1] // 2 * 2 + b + 2 * place_ref[0]) % X
        rows.append(dot_nn(left[b * STRIP :][:STRIP].astype(BF16), dinv_ref[k]))
    x = jnp.concatenate(rows, axis=0).astype(BF16)
    for peer in range(PEERS):
        spread_ref[peer] = x


def low_carries(
    place_ref,
    row_ref,
    col_ref,
    far_ref,
    in_ref,
    part_ref,
    mine_ref,
    other_ref,
    x_ref,
    keep_ref,
    out_ref,
    known,
    acc,
):
    r = place_ref[0]
    peer = place_ref[1] // 2
    core = r % 2
    for x in range(X):
        for y in range(Y):
            strip = in_ref[2 * y + x // 2, x % 2 * STRIP : x % 2 * STRIP + STRIP]
            known[x, y * STRIP : (y + 1) * STRIP] = strip
    own = []
    for i in range(L1):
        x = (r * OWN + L0 + i) % X
        strips = in_ref[peer // 2 * 2 + x // 2].astype(F32)
        octet = jnp.where(x % 2 == 0, strips[:STRIP], strips[STRIP:])
        own.append(jnp.where(peer % 2 == 0, octet[:W], octet[W:]))
    x_ref[...] = jnp.concatenate(own, axis=0).astype(BF16)
    for p in range(LOWS):
        acc[p] = part_ref[p]
    acc[LOWS] = jnp.zeros((N, SN), F32)
    for row, column, tile in slots(row_ref, col_ref, far_ref, mine_ref, other_ref, 0, SLOTS1):
        source = (r * OWN + row) % X
        panel = jnp.minimum(panel_of(column), LOWS - 1)
        slot = jnp.where(row < OWN, panel, LOWS)
        acc[slot] += dot_nn(known[source], tile)
    keep_ref[...] = cut([acc[4 * core + i] for i in range(4)], F32)
    out_ref[...] = cut([acc[4 * (1 - core) + i] for i in range(4)])


def pair_sum(keep_ref, in_ref, out_ref):
    out_ref[...] = (keep_ref[...] + in_ref[...].astype(F32)).astype(BF16)


def low_by_row(place_ref, in_ref, out_ref):
    core = place_ref[0] % 2
    for z in range(Z):
        parts = []
        for k in range(L0):
            c = (28 * z + 14 * core + k) % C
            o = k // 4
            tile = in_ref[c // 2].astype(F32)
            parts.append(tile[(k % 2 * 2 + o) * W :][:W])
        out_ref[z] = jnp.concatenate(parts, axis=0).astype(BF16)


def low_backward(in_ref, y_ref, dinv_ref, mid_ref, top_ref, out_ref):
    carry = jnp.sum(in_ref[...].astype(F32), axis=0)
    left = (y_ref[...].astype(F32) - carry).reshape(L0, W, SN)
    for k in range(L0):
        out_ref[:, k * SN : (k + 1) * SN] = dot_nn(left[k].astype(BF16), dinv_ref[k]).astype(BF16)
    mid = mid_ref[...].astype(F32)
    for i in range(L1):
        out_ref[:, (L0 + i) * SN : (L0 + i + 1) * SN] = mid[i * W : (i + 1) * W].astype(BF16)
    top = top_ref[...].astype(F32)
    for i in range(L2):
        out_ref[:, (MID + i) * SN : (MID + i + 1) * SN] = top[i * W : (i + 1) * W].astype(BF16)


VM = pl.BlockSpec(memory_space=pltpu.VMEM)
SM = pl.BlockSpec(memory_space=pltpu.SMEM)


def call(kernel, outs, *args, scratch=()):
    single = len(outs) == 1
    shapes = [jax.ShapeDtypeStruct(shape, kind) for shape, kind in outs]
    return pl.pallas_call(
        kernel,
        out_shape=shapes[0] if single else shapes,
        in_specs=[SM if a.dtype == jnp.int32 else VM for a in args],
        out_specs=VM if single else [VM] * len(outs),
        scratch_shapes=list(scratch),
        compiler_params=pltpu.CompilerParams(vmem_limit_bytes=24 * 1024 * 1024),
    )(*args)


def over_peers(pieces):
    return lax.all_to_all(pieces, "col", 0, 0, tiled=True, axis_index_groups=PEER_GROUPS)


def over_y(pieces):
    return lax.all_to_all(pieces, "col", 0, 0, tiled=True, axis_index_groups=Y_GROUPS)


def over_z_by_y(pieces):
    return lax.all_to_all(pieces, ("row", "col"), 0, 0, tiled=True, axis_index_groups=MID_GROUPS)


def over_core(pieces):
    return lax.all_gather(pieces, "row", axis=0, axis_index_groups=CORE_GROUPS)


def swap(half):
    return lax.ppermute(half, "row", SWAP)


def over_z(pieces):
    return lax.all_to_all(pieces, "row", 0, 0, tiled=True, axis_index_groups=Z_GROUPS)


def on_device(rhs, dinv, blocks, block_row, block_col):
    place = jnp.stack([lax.axis_index("row"), lax.axis_index("col")]).astype(jnp.int32)
    right = rhs.T
    panels = pltpu.VMEM((LOWS + MIDS, N, SN), BF16)
    sums = pltpu.VMEM((LOWS + MIDS + 1, N, SN), F32)
    work = (panels, sums)
    whole = pl.BlockSpec(memory_space=pl.ANY)
    y_low, spread, packed = pl.pallas_call(
        low_forward,
        out_shape=[
            jax.ShapeDtypeStruct((64, SN), BF16),
            jax.ShapeDtypeStruct((Z, 64, SN), BF16),
            jax.ShapeDtypeStruct((SLOTS1 * SN + 16, SN), BF16),
        ],
        in_specs=[VM, VM, VM, whole, whole],
        out_specs=[VM, VM, VM],
        scratch_shapes=[
            pltpu.VMEM((L0, SN, SN), BF16),
            pltpu.SemaphoreType.DMA((L0 + SLOTS1,)),
        ],
        compiler_params=pltpu.CompilerParams(vmem_limit_bytes=62 * 1062 * 1062),
    )(right, block_row, block_col, dinv, blocks)
    lower = lax.ppermute(packed, "col", NEIGHBOURS)
    far = lower[-16:-15].astype(jnp.int32)
    lists = (block_row, block_col, far)

    sent = call(low_by_class, [((PEERS, 32, SN), BF16)], place, over_z(spread))
    low = over_core(over_peers(sent))
    part = call(
        mid_sums,
        [((PEERS, 2 * STRIP, SN), BF16)],
        place,
        *lists,
        low,
        blocks,
        lower,
        right,
        scratch=work,
    )
    upper, part = lax.optimization_barrier((blocks[0, SLOTS1:].reshape(-1, SN), part))
    upper = lax.ppermute(upper, "col", NEIGHBOURS)
    y_mid, spread = call(
        mid_forward,
        [((2 * STRIP, SN), BF16), ((Z, 2 * STRIP, SN), BF16)],
        place,
        over_peers(part),
        dinv,
    )
    mid = over_core(over_y(over_z_by_y(spread)))
    part = call(
        top_sums, [((PEERS, 16, SN), BF16)], *lists, low, mid, blocks, upper, scratch=work
    )
    x_top, spread = call(
        top_solve, [((16, SN), BF16), ((PEERS, 16, SN), BF16)], over_peers(part), right, dinv
    )
    low_part, keep, sent = call(
        top_carries,
        [
            ((LOWS, N, SN), F32),
            ((Y, 2 * STRIP, SN), F32),
            ((Y, 2 * STRIP, SN), BF16),
        ],
        place,
        *lists,
        over_peers(spread),
        blocks,
        upper,
        scratch=work,
    )
    both = call(pair_sum, [((Y, 2 * STRIP, SN), BF16)], keep, swap(sent))
    carry = over_z_by_y(over_y(both))
    spread = call(mid_backward, [((PEERS, 2 * STRIP, SN), BF16)], place, carry, y_mid, dinv)
    x_mid, keep, sent = call(
        low_carries,
        [((32, SN), BF16), ((PEERS, 32, SN), F32), ((PEERS, 32, SN), BF16)],
        place,
        *lists,
        over_peers(spread),
        low_part,
        blocks,
        lower,
        scratch=work,
    )
    both = call(pair_sum, [((PEERS, 32, SN), BF16)], keep, swap(sent))
    sent = call(low_by_row, [((Z, 64, SN), BF16)], place, over_peers(both))
    out = call(low_backward, [((W, OWN * SN), BF16)], over_z(sent), y_low, dinv, x_mid, x_top)
    return out.T


def solution(mesh):
    placed = (
        P("row", "col"),
        P("row", None, None),
        P("row", "col", None, None),
        P("row", "col"),
        P("row", "col"),
    )
    return jax.shard_map(
        on_device, mesh=mesh, in_specs=placed, out_specs=P("row", "col"), check_vma=False
    )
```

```python
import jax
import jax.numpy as jnp
from jax import lax
from jax.experimental import pallas as pl
from jax.experimental.pallas import tpu as pltpu
from jax.sharding import PartitionSpec as P

SN = 256
L0 = 8
L1 = 4
L2 = 2
MID = L0 + L1
OWN = L0 + L1 + L2
SLOTS1 = 8
SLOTS = 14
R = 16
C = 32
X = 4
Y = 8
Z = 8
HALVES = 2
PEERS = Y * HALVES
W = 8
STRIP = W * HALVES
N = W * PEERS
LOWS = 8
MIDS = 4
F32 = jnp.float32
BF16 = jnp.bfloat16
Z_GROUPS = [[2 * z + core for z in range(Z)] for core in range(2)]
CORE_GROUPS = [[2 * z, 2 * z + 1] for z in range(Z)]
Y_GROUPS = [[X * y + x for y in range(Y)] for x in range(X)]
PEER_GROUPS = [[2 * peer + (side + peer) % 2 for peer in range(PEERS)] for side in range(2)]
SWAP = [(r, r ^ 1) for r in range(R)]
NEIGHBOURS = [(c, c ^ 1) for c in range(C)]


def mid_groups():
    groups = []
    for core in range(2):
        for c in range(C):
            by_y = [0] * Y
            for z in range(Z):
                r = 2 * z + core
                column = [s % C for s in range(r * OWN + L0, r * OWN + MID) if s % X == c % X][0]
                by_y[column // X] = r * C + c
            groups.append(by_y)
    return groups


MID_GROUPS = mid_groups()


def dot_nt(left, right):
    return lax.dot_general(left, right, (((1,), (1,)), ((), ())), preferred_element_type=F32)


def dot_nn(left, right):
    return lax.dot_general(left, right, (((1,), (0,)), ((), ())), preferred_element_type=F32)


def low_panel(column):
    return column % (2 * OWN) // OWN * 4 + column % 2 * 2 + column % OWN // 4


def mid_panel(column):
    return column % (2 * OWN) // OWN * 2 + column % 2


def panel_of(column):
    return jnp.where(column % OWN < L0, low_panel(column), LOWS + mid_panel(column))


def join(pieces, out_ref, first=0):
    count = pieces.shape[1] // W
    wide = pieces.astype(F32).reshape(PEERS, count, W, SN)
    for i in range(count):
        out_ref[first + i] = wide[:, i].reshape(N, SN).astype(BF16)


def cut(panels, kind=BF16):
    parts = [p.reshape(PEERS, W, SN) for p in panels]
    return jnp.stack(parts, axis=1).reshape(PEERS, W * len(parts), SN).astype(kind)


def slots(row_ref, col_ref, far_ref, mine_ref, other_ref, first, final):
    for q in range(first, final):
        yield row_ref[0, q], col_ref[0, q], mine_ref[0, q]
    for q in range(first, final):
        tile = other_ref[(q - first) * SN : (q - first + 1) * SN]
        yield far_ref[0, q], far_ref[0, 128 + q], tile


def low_forward(rhs_ref, dinv_ref, y_ref, spread_ref, factors, sems):
    fetch = [pltpu.make_async_copy(dinv_ref.at[k], factors.at[k], sems.at[k]) for k in range(L0)]
    for copy in fetch:
        copy.start()
    rows = []
    for k in range(L0):
        fetch[k].wait()
        rows.append(dot_nt(rhs_ref[:, k * SN : (k + 1) * SN], factors[k]))
    y = jnp.concatenate(rows, axis=0).astype(BF16)
    y_ref[...] = y
    for z in range(Z):
        spread_ref[z] = y


def pack(row_ref, col_ref, blocks_ref, out_ref, sems):
    fetch = []
    for q in range(SLOTS1):
        target = out_ref.at[pl.ds(q * SN, SN)]
        fetch.append(pltpu.make_async_copy(blocks_ref.at[0, q], target, sems.at[q]))
    for copy in fetch:
        copy.start()
    last = SLOTS1 * SN
    out_ref[last:] = jnp.zeros((16, SN), BF16)
    out_ref[last:, :SLOTS] = jnp.broadcast_to(row_ref[...].astype(F32), (16, SLOTS)).astype(BF16)
    out_ref[last:, 128 : 128 + SLOTS] = jnp.broadcast_to(
        col_ref[...].astype(F32), (16, SLOTS)
    ).astype(BF16)
    for copy in fetch:
        copy.wait()


def low_by_class(place_ref, in_ref, out_ref):
    core = place_ref[0] % 2
    for c in range(C):
        halves = []
        for o in range(2):
            a = (c + 2 * core) % 4
            z = (7 * ((c - 14 * core - a - 4 * o + 64) // 4)) % Z
            tile = in_ref[z, 32 * o : 32 * o + 32].astype(F32)
            piece = jnp.where(a == 0, tile[0:8], tile[8:16])
            other = jnp.where(a == 2, tile[16:24], tile[24:32])
            halves.append(jnp.where(a < 2, piece, other))
        out_ref[c // 2, c % 2 * 16 : c % 2 * 16 + 16] = jnp.concatenate(halves, axis=0).astype(BF16)


def mid_sums(place_ref, row_ref, col_ref, far_ref, low_ref, mine_ref, other_ref, rhs_ref, out_ref, panels, acc):
    r = place_ref[0]
    own = pl.multiple_of(place_ref[1] // 2 * W, W)
    for p in range(2):
        join(low_ref[p], panels, 4 * p)
    acc[...] = jnp.zeros_like(acc)
    for i in range(L1):
        x = (r * OWN + L0 + i) % X
        acc[x, pl.ds(own, W)] = -rhs_ref[:, (L0 + i) * SN : (L0 + i + 1) * SN].astype(F32)
    for row, column, tile in slots(row_ref, col_ref, far_ref, mine_ref, other_ref, 0, SLOTS1):
        slot = jnp.where(row < OWN, (r * OWN + row) % X, X)
        source = jnp.minimum(panel_of(column), LOWS - 1)
        acc[slot] += dot_nt(panels[source], tile)
    for x in range(X):
        strips = acc[x].astype(BF16)
        for y in range(Y):
            out_ref[2 * y + x // 2, x % 2 * STRIP : x % 2 * STRIP + STRIP] = strips[y * STRIP :][:STRIP]


def mid_forward(place_ref, in_ref, dinv_ref, y_ref, spread_ref):
    right = -jnp.sum(in_ref[...].astype(F32), axis=0)
    rows = []
    for b in range(2):
        k = (place_ref[1] // 2 * 2 + b + 2 * place_ref[0]) % X
        rows.append(dot_nt(right[b * STRIP :][:STRIP].astype(BF16), dinv_ref[k]))
    y = jnp.concatenate(rows, axis=0).astype(BF16)
    y_ref[...] = y
    for z in range(Z):
        spread_ref[z] = y


def top_sums(row_ref, col_ref, far_ref, low_ref, mid_ref, mine_ref, other_ref, out_ref, panels, acc):
    for p in range(2):
        join(low_ref[p], panels, 4 * p)
        for b in range(2):
            for y in range(Y):
                strip = mid_ref[p, y, b * STRIP : (b + 1) * STRIP]
                panels[LOWS + 2 * p + b, y * STRIP : (y + 1) * STRIP] = strip
    acc[...] = jnp.zeros_like(acc)
    for row, column, tile in slots(row_ref, col_ref, far_ref, mine_ref, other_ref, SLOTS1, SLOTS):
        slot = jnp.where(row < OWN, row - MID, L2)
        source = panel_of(column)
        acc[slot] += dot_nt(panels[source], tile)
    out_ref[...] = cut([acc[i] for i in range(L2)])


def top_solve(in_ref, rhs_ref, dinv_ref, x_ref, spread_ref):
    sums = jnp.sum(in_ref[...].astype(F32), axis=0)
    rows = []
    for i in range(L2):
        k = MID + i
        right = rhs_ref[:, k * SN : (k + 1) * SN].astype(F32) - sums[i * W : (i + 1) * W]
        y = dot_nt(right.astype(BF16), dinv_ref[i]).astype(BF16)
        rows.append(dot_nn(y, dinv_ref[i]))
    x = jnp.concatenate(rows, axis=0).astype(BF16)
    x_ref[...] = x
    for peer in range(PEERS):
        spread_ref[peer] = x


def top_carries(
    place_ref, row_ref, col_ref, far_ref, in_ref, mine_ref, other_ref, low_ref, keep_ref, out_ref, known, acc
):
    core = place_ref[0] % 2
    join(in_ref[...], known)
    acc[...] = jnp.zeros_like(acc)
    for row, column, tile in slots(row_ref, col_ref, far_ref, mine_ref, other_ref, SLOTS1, SLOTS):
        source = jnp.clip(row - MID, 0, L2 - 1)
        slot = jnp.where(row < OWN, panel_of(column), LOWS + MIDS)
        acc[slot] += dot_nn(known[source], tile)
    for p in range(LOWS):
        low_ref[p] = acc[p]
    for b in range(2):
        keep = acc[LOWS + 2 * core + b]
        sent = acc[LOWS + 2 * (1 - core) + b].astype(BF16)
        for y in range(Y):
            keep_ref[y, b * STRIP : (b + 1) * STRIP] = keep[y * STRIP : (y + 1) * STRIP]
            out_ref[y, b * STRIP : (b + 1) * STRIP] = sent[y * STRIP : (y + 1) * STRIP]


def mid_backward(place_ref, in_ref, y_ref, dinv_ref, spread_ref):
    left = y_ref[...].astype(F32) - jnp.sum(in_ref[...].astype(F32), axis=0)
    rows = []
    for b in range(2):
        k = (place_ref[1] // 2 * 2 + b + 2 * place_ref[0]) % X
        rows.append(dot_nn(left[b * STRIP :][:STRIP].astype(BF16), dinv_ref[k]))
    x = jnp.concatenate(rows, axis=0).astype(BF16)
    for peer in range(PEERS):
        spread_ref[peer] = x


def low_carries(
    place_ref,
    row_ref,
    col_ref,
    far_ref,
    in_ref,
    part_ref,
    mine_ref,
    other_ref,
    x_ref,
    keep_ref,
    out_ref,
    known,
    acc,
):
    r = place_ref[0]
    peer = place_ref[1] // 2
    core = r % 2
    for x in range(X):
        for y in range(Y):
            strip = in_ref[2 * y + x // 2, x % 2 * STRIP : x % 2 * STRIP + STRIP]
            known[x, y * STRIP : (y + 1) * STRIP] = strip
    own = []
    for i in range(L1):
        x = (r * OWN + L0 + i) % X
        strips = in_ref[peer // 2 * 2 + x // 2].astype(F32)
        octet = jnp.where(x % 2 == 0, strips[:STRIP], strips[STRIP:])
        own.append(jnp.where(peer % 2 == 0, octet[:W], octet[W:]))
    x_ref[...] = jnp.concatenate(own, axis=0).astype(BF16)
    for p in range(LOWS):
        acc[p] = part_ref[p]
    acc[LOWS] = jnp.zeros((N, SN), F32)
    for row, column, tile in slots(row_ref, col_ref, far_ref, mine_ref, other_ref, 0, SLOTS1):
        source = (r * OWN + row) % X
        panel = jnp.minimum(panel_of(column), LOWS - 1)
        slot = jnp.where(row < OWN, panel, LOWS)
        acc[slot] += dot_nn(known[source], tile)
    keep_ref[...] = cut([acc[4 * core + i] for i in range(4)], F32)
    out_ref[...] = cut([acc[4 * (1 - core) + i] for i in range(4)])


def pair_sum(keep_ref, in_ref, out_ref):
    out_ref[...] = (keep_ref[...] + in_ref[...].astype(F32)).astype(BF16)


def low_by_row(place_ref, in_ref, out_ref):
    core = place_ref[0] % 2
    for z in range(Z):
        parts = []
        for k in range(L0):
            c = (28 * z + 14 * core + k) % C
            o = k // 4
            tile = in_ref[c // 2].astype(F32)
            parts.append(tile[(k % 2 * 2 + o) * W :][:W])
        out_ref[z] = jnp.concatenate(parts, axis=0).astype(BF16)


def low_backward(in_ref, y_ref, dinv_ref, mid_ref, top_ref, out_ref):
    carry = jnp.sum(in_ref[...].astype(F32), axis=0)
    left = (y_ref[...].astype(F32) - carry).reshape(L0, W, SN)
    for k in range(L0):
        out_ref[:, k * SN : (k + 1) * SN] = dot_nn(left[k].astype(BF16), dinv_ref[k]).astype(BF16)
    mid = mid_ref[...].astype(F32)
    for i in range(L1):
        out_ref[:, (L0 + i) * SN : (L0 + i + 1) * SN] = mid[i * W : (i + 1) * W].astype(BF16)
    top = top_ref[...].astype(F32)
    for i in range(L2):
        out_ref[:, (MID + i) * SN : (MID + i + 1) * SN] = top[i * W : (i + 1) * W].astype(BF16)


VM = pl.BlockSpec(memory_space=pltpu.VMEM)
SM = pl.BlockSpec(memory_space=pltpu.SMEM)


def call(kernel, outs, *args, scratch=()):
    single = len(outs) == 1
    shapes = [jax.ShapeDtypeStruct(shape, kind) for shape, kind in outs]
    return pl.pallas_call(
        kernel,
        out_shape=shapes[0] if single else shapes,
        in_specs=[SM if a.dtype == jnp.int32 else VM for a in args],
        out_specs=VM if single else [VM] * len(outs),
        scratch_shapes=list(scratch),
        compiler_params=pltpu.CompilerParams(vmem_limit_bytes=24 * 1024 * 1024),
    )(*args)


def over_peers(pieces):
    return lax.all_to_all(pieces, "col", 0, 0, tiled=True, axis_index_groups=PEER_GROUPS)


def over_y(pieces):
    return lax.all_to_all(pieces, "col", 0, 0, tiled=True, axis_index_groups=Y_GROUPS)


def over_z_by_y(pieces):
    return lax.all_to_all(pieces, ("row", "col"), 0, 0, tiled=True, axis_index_groups=MID_GROUPS)


def over_core(pieces):
    return lax.all_gather(pieces, "row", axis=0, axis_index_groups=CORE_GROUPS)


def swap(half):
    return lax.ppermute(half, "row", SWAP)


def over_z(pieces):
    return lax.all_to_all(pieces, "row", 0, 0, tiled=True, axis_index_groups=Z_GROUPS)


def on_device(rhs, dinv, blocks, block_row, block_col):
    place = jnp.stack([lax.axis_index("row"), lax.axis_index("col")]).astype(jnp.int32)
    right = rhs.T
    panels = pltpu.VMEM((LOWS + MIDS, N, SN), BF16)
    sums = pltpu.VMEM((LOWS + MIDS + 1, N, SN), F32)
    work = (panels, sums)
    whole = pl.BlockSpec(memory_space=pl.ANY)
    y_low, spread = pl.pallas_call(
        low_forward,
        out_shape=[
            jax.ShapeDtypeStruct((64, SN), BF16),
            jax.ShapeDtypeStruct((Z, 64, SN), BF16),
        ],
        in_specs=[VM, whole],
        out_specs=[VM, VM],
        scratch_shapes=[pltpu.VMEM((L0, SN, SN), BF16), pltpu.SemaphoreType.DMA((L0,))],
        compiler_params=pltpu.CompilerParams(vmem_limit_bytes=60 * 1024 * 1024),
    )(right, dinv)
    spread, given = lax.optimization_barrier((spread, blocks))
    packed = pl.pallas_call(
        pack,
        out_shape=jax.ShapeDtypeStruct((SLOTS1 * SN + 16, SN), BF16),
        in_specs=[VM, VM, whole],
        out_specs=VM,
        scratch_shapes=[pltpu.SemaphoreType.DMA((SLOTS1,))],
        compiler_params=pltpu.CompilerParams(vmem_limit_bytes=24 * 1024 * 1024),
    )(block_row, block_col, given)
    lower = lax.ppermute(packed, "col", NEIGHBOURS)
    far = lower[-16:-15].astype(jnp.int32)
    lists = (block_row, block_col, far)

    sent = call(low_by_class, [((PEERS, 32, SN), BF16)], place, over_z(spread))
    low = over_core(over_peers(sent))
    part = call(
        mid_sums,
        [((PEERS, 2 * STRIP, SN), BF16)],
        place,
        *lists,
        low,
        blocks,
        lower,
        right,
        scratch=work,
    )
    upper, part = lax.optimization_barrier((blocks[0, SLOTS1:].reshape(-1, SN), part))
    upper = lax.ppermute(upper, "col", NEIGHBOURS)
    y_mid, spread = call(
        mid_forward,
        [((2 * STRIP, SN), BF16), ((Z, 2 * STRIP, SN), BF16)],
        place,
        over_peers(part),
        dinv[L0:MID],
    )
    mid = over_core(over_y(over_z_by_y(spread)))
    part = call(
        top_sums, [((PEERS, 16, SN), BF16)], *lists, low, mid, blocks, upper, scratch=work
    )
    x_top, spread = call(
        top_solve, [((16, SN), BF16), ((PEERS, 16, SN), BF16)], over_peers(part), right, dinv[MID:]
    )
    low_part, keep, sent = call(
        top_carries,
        [
            ((LOWS, N, SN), F32),
            ((Y, 2 * STRIP, SN), F32),
            ((Y, 2 * STRIP, SN), BF16),
        ],
        place,
        *lists,
        over_peers(spread),
        blocks,
        upper,
        scratch=work,
    )
    both = call(pair_sum, [((Y, 2 * STRIP, SN), BF16)], keep, swap(sent))
    carry = over_z_by_y(over_y(both))
    spread = call(mid_backward, [((PEERS, 2 * STRIP, SN), BF16)], place, carry, y_mid, dinv[L0:MID])
    x_mid, keep, sent = call(
        low_carries,
        [((32, SN), BF16), ((PEERS, 32, SN), F32), ((PEERS, 32, SN), BF16)],
        place,
        *lists,
        over_peers(spread),
        low_part,
        blocks,
        lower,
        scratch=work,
    )
    both = call(pair_sum, [((PEERS, 32, SN), BF16)], keep, swap(sent))
    sent = call(low_by_row, [((Z, 64, SN), BF16)], place, over_peers(both))
    out = call(low_backward, [((W, OWN * SN), BF16)], over_z(sent), y_low, dinv[:L0], x_mid, x_top)
    return out.T


def solution(mesh):
    placed = (
        P("row", "col"),
        P("row", None, None),
        P("row", "col", None, None),
        P("row", "col"),
        P("row", "col"),
    )
    return jax.shard_map(
        on_device, mesh=mesh, in_specs=placed, out_specs=P("row", "col"), check_vma=False
    )
```

```python
import jax
import jax.numpy as jnp
from jax import lax
from jax.experimental import pallas as pl
from jax.experimental.pallas import tpu as pltpu
from jax.sharding import PartitionSpec as P

SN = 256
L0 = 8
L1 = 4
L2 = 2
MID = L0 + L1
OWN = L0 + L1 + L2
SLOTS1 = 8
SLOTS = 14
R = 16
C = 32
X = 4
Y = 8
Z = 8
HALVES = 2
PEERS = Y * HALVES
W = 8
STRIP = W * HALVES
N = W * PEERS
LOWS = 8
MIDS = 4
F32 = jnp.float32
BF16 = jnp.bfloat16
Z_GROUPS = [[2 * z + core for z in range(Z)] for core in range(2)]
CORE_GROUPS = [[2 * z, 2 * z + 1] for z in range(Z)]
Y_GROUPS = [[X * y + x for y in range(Y)] for x in range(X)]
PEER_GROUPS = [[2 * peer + (side + peer) % 2 for peer in range(PEERS)] for side in range(2)]
Y_CORE_GROUPS = [
    [(2 * z + core) * C + X * y + x for y in range(Y) for core in range(2)]
    for z in range(Z)
    for x in range(X)
]
SWAP = [(r, r ^ 1) for r in range(R)]
NEIGHBOURS = [(c, c ^ 1) for c in range(C)]


def mid_groups():
    groups = []
    for core in range(2):
        for c in range(C):
            by_y = [0] * Y
            for z in range(Z):
                r = 2 * z + core
                column = [s % C for s in range(r * OWN + L0, r * OWN + MID) if s % X == c % X][0]
                by_y[column // X] = r * C + c
            groups.append(by_y)
    return groups


MID_GROUPS = mid_groups()


def dot_nt(left, right):
    return lax.dot_general(left, right, (((1,), (1,)), ((), ())), preferred_element_type=F32)


def dot_nn(left, right):
    return lax.dot_general(left, right, (((1,), (0,)), ((), ())), preferred_element_type=F32)


def low_panel(column):
    return column % (2 * OWN) // OWN * 4 + column % 2 * 2 + column % OWN // 4


def mid_panel(column):
    return column % (2 * OWN) // OWN * 2 + column % 2


def panel_of(column):
    return jnp.where(column % OWN < L0, low_panel(column), LOWS + mid_panel(column))


def join(pieces, out_ref, first=0):
    count = pieces.shape[1] // W
    wide = pieces.astype(F32).reshape(PEERS, count, W, SN)
    for i in range(count):
        out_ref[first + i] = wide[:, i].reshape(N, SN).astype(BF16)


def cut(panels, kind=BF16):
    parts = [p.reshape(PEERS, W, SN) for p in panels]
    return jnp.stack(parts, axis=1).reshape(PEERS, W * len(parts), SN).astype(kind)


def slots(row_ref, col_ref, far_ref, mine_ref, other_ref, tiles, sem, first, final):
    rows = pl.ds(0, (final - first) * SN)
    copy = pltpu.make_async_copy(other_ref.at[rows], tiles.at[rows], sem)
    copy.start()
    for q in range(first, final):
        yield row_ref[0, q], col_ref[0, q], mine_ref[0, q]
    copy.wait()
    for q in range(first, final):
        tile = tiles[(q - first) * SN : (q - first + 1) * SN]
        yield far_ref[0, q], far_ref[0, 128 + q], tile


def low_forward(
    rhs_ref, row_ref, col_ref, dinv_ref, blocks_ref, y_ref, spread_ref, sent_ref, factors, sems
):
    fetch = [pltpu.make_async_copy(dinv_ref.at[k], factors.at[k], sems.at[k]) for k in range(L0)]
    for copy in fetch:
        copy.start()
    pack = []
    for q in range(SLOTS1):
        target = sent_ref.at[pl.ds(q * SN, SN)]
        pack.append(pltpu.make_async_copy(blocks_ref.at[0, q], target, sems.at[L0 + q]))
    for copy in pack:
        copy.start()
    last = SLOTS1 * SN
    sent_ref[last:] = jnp.zeros((16, SN), BF16)
    sent_ref[last:, :SLOTS] = jnp.broadcast_to(row_ref[...].astype(F32), (16, SLOTS)).astype(BF16)
    sent_ref[last:, 128 : 128 + SLOTS] = jnp.broadcast_to(
        col_ref[...].astype(F32), (16, SLOTS)
    ).astype(BF16)
    rows = []
    for k in range(L0):
        fetch[k].wait()
        rows.append(dot_nt(rhs_ref[:, k * SN : (k + 1) * SN], factors[k]))
    y = jnp.concatenate(rows, axis=0).astype(BF16)
    y_ref[...] = y
    for z in range(Z):
        spread_ref[z] = y
    for copy in pack:
        copy.wait()


def low_by_class(place_ref, in_ref, out_ref):
    core = place_ref[0] % 2
    for c in range(C):
        halves = []
        for o in range(2):
            a = (c + 2 * core) % 4
            z = (7 * ((c - 14 * core - a - 4 * o + 64) // 4)) % Z
            tile = in_ref[z, 32 * o : 32 * o + 32].astype(F32)
            piece = jnp.where(a == 0, tile[0:8], tile[8:16])
            other = jnp.where(a == 2, tile[16:24], tile[24:32])
            halves.append(jnp.where(a < 2, piece, other))
        out_ref[c // 2, c % 2 * 16 : c % 2 * 16 + 16] = jnp.concatenate(halves, axis=0).astype(BF16)


def mid_sums(place_ref, row_ref, col_ref, far_ref, low_ref, mine_ref, other_ref, rhs_ref, out_ref, panels, acc, tiles, sem):
    r = place_ref[0]
    own = pl.multiple_of(place_ref[1] // 2 * W, W)
    for p in range(2):
        join(low_ref[p], panels, 4 * p)
    acc[...] = jnp.zeros_like(acc)
    for i in range(L1):
        x = (r * OWN + L0 + i) % X
        acc[x, pl.ds(own, W)] = -rhs_ref[:, (L0 + i) * SN : (L0 + i + 1) * SN].astype(F32)
    for row, column, tile in slots(
        row_ref, col_ref, far_ref, mine_ref, other_ref, tiles, sem, 0, SLOTS1
    ):
        slot = jnp.where(row < OWN, (r * OWN + row) % X, X)
        source = jnp.minimum(panel_of(column), LOWS - 1)
        acc[slot] += dot_nt(panels[source], tile)
    for x in range(X):
        strips = acc[x].astype(BF16)
        for y in range(Y):
            out_ref[2 * y + x // 2, x % 2 * STRIP : x % 2 * STRIP + STRIP] = strips[y * STRIP :][:STRIP]


def mid_forward(place_ref, in_ref, dinv_ref, y_ref, spread_ref):
    right = -jnp.sum(in_ref[...].astype(F32), axis=0)
    rows = []
    for b in range(2):
        k = (place_ref[1] // 2 * 2 + b + 2 * place_ref[0]) % X
        rows.append(dot_nt(right[b * STRIP :][:STRIP].astype(BF16), dinv_ref[k]))
    y = jnp.concatenate(rows, axis=0).astype(BF16)
    y_ref[...] = y
    for z in range(Z):
        spread_ref[z] = y


def top_sums(row_ref, col_ref, far_ref, low_ref, mid_ref, mine_ref, other_ref, out_ref, panels, acc, tiles, sem):
    for p in range(2):
        join(low_ref[p], panels, 4 * p)
        for b in range(2):
            for y in range(Y):
                strip = mid_ref[p, y, b * STRIP : (b + 1) * STRIP]
                panels[LOWS + 2 * p + b, y * STRIP : (y + 1) * STRIP] = strip
    acc[...] = jnp.zeros_like(acc)
    for row, column, tile in slots(
        row_ref, col_ref, far_ref, mine_ref, other_ref, tiles, sem, SLOTS1, SLOTS
    ):
        slot = jnp.where(row < OWN, row - MID, L2)
        source = panel_of(column)
        acc[slot] += dot_nt(panels[source], tile)
    out_ref[...] = cut([acc[i] for i in range(L2)])


def top_solve(in_ref, rhs_ref, dinv_ref, x_ref, spread_ref):
    sums = jnp.sum(in_ref[...].astype(F32), axis=0)
    rows = []
    for i in range(L2):
        k = MID + i
        right = rhs_ref[:, k * SN : (k + 1) * SN].astype(F32) - sums[i * W : (i + 1) * W]
        y = dot_nt(right.astype(BF16), dinv_ref[k]).astype(BF16)
        rows.append(dot_nn(y, dinv_ref[k]))
    x = jnp.concatenate(rows, axis=0).astype(BF16)
    x_ref[...] = x
    for peer in range(PEERS):
        spread_ref[peer] = x


def top_carries(
    row_ref, col_ref, far_ref, in_ref, mine_ref, other_ref, low_ref, out_ref, known, acc, tiles, sem
):
    join(in_ref[...], known)
    acc[...] = jnp.zeros_like(acc)
    for row, column, tile in slots(
        row_ref, col_ref, far_ref, mine_ref, other_ref, tiles, sem, SLOTS1, SLOTS
    ):
        source = jnp.clip(row - MID, 0, L2 - 1)
        slot = jnp.where(row < OWN, panel_of(column), LOWS + MIDS)
        acc[slot] += dot_nn(known[source], tile)
    for p in range(LOWS):
        low_ref[p] = acc[p]
    for p in range(2):
        for b in range(2):
            strips = acc[LOWS + 2 * p + b].astype(BF16)
            for y in range(Y):
                strip = strips[y * STRIP : (y + 1) * STRIP]
                out_ref[2 * y + p, b * STRIP : (b + 1) * STRIP] = strip


def core_sum(in_ref, out_ref):
    for y in range(Y):
        out_ref[y] = (in_ref[2 * y].astype(F32) + in_ref[2 * y + 1].astype(F32)).astype(BF16)


def mid_backward(place_ref, in_ref, y_ref, dinv_ref, spread_ref):
    left = y_ref[...].astype(F32) - jnp.sum(in_ref[...].astype(F32), axis=0)
    rows = []
    for b in range(2):
        k = (place_ref[1] // 2 * 2 + b + 2 * place_ref[0]) % X
        rows.append(dot_nn(left[b * STRIP :][:STRIP].astype(BF16), dinv_ref[k]))
    x = jnp.concatenate(rows, axis=0).astype(BF16)
    for peer in range(PEERS):
        spread_ref[peer] = x


def low_carries(
    place_ref,
    row_ref,
    col_ref,
    far_ref,
    in_ref,
    part_ref,
    mine_ref,
    other_ref,
    x_ref,
    keep_ref,
    out_ref,
    known,
    acc,
    tiles,
    sem,
):
    r = place_ref[0]
    peer = place_ref[1] // 2
    core = r % 2
    for x in range(X):
        for y in range(Y):
            strip = in_ref[2 * y + x // 2, x % 2 * STRIP : x % 2 * STRIP + STRIP]
            known[x, y * STRIP : (y + 1) * STRIP] = strip
    own = []
    for i in range(L1):
        x = (r * OWN + L0 + i) % X
        strips = in_ref[peer // 2 * 2 + x // 2].astype(F32)
        octet = jnp.where(x % 2 == 0, strips[:STRIP], strips[STRIP:])
        own.append(jnp.where(peer % 2 == 0, octet[:W], octet[W:]))
    x_ref[...] = jnp.concatenate(own, axis=0).astype(BF16)
    for p in range(LOWS):
        acc[p] = part_ref[p]
    acc[LOWS] = jnp.zeros((N, SN), F32)
    for row, column, tile in slots(
        row_ref, col_ref, far_ref, mine_ref, other_ref, tiles, sem, 0, SLOTS1
    ):
        source = (r * OWN + row) % X
        panel = jnp.minimum(panel_of(column), LOWS - 1)
        slot = jnp.where(row < OWN, panel, LOWS)
        acc[slot] += dot_nn(known[source], tile)
    keep_ref[...] = cut([acc[4 * core + i] for i in range(4)], F32)
    out_ref[...] = cut([acc[4 * (1 - core) + i] for i in range(4)])


def pair_sum(keep_ref, in_ref, out_ref):
    out_ref[...] = (keep_ref[...] + in_ref[...].astype(F32)).astype(BF16)


def low_by_row(place_ref, in_ref, out_ref):
    core = place_ref[0] % 2
    for z in range(Z):
        parts = []
        for k in range(L0):
            c = (28 * z + 14 * core + k) % C
            o = k // 4
            tile = in_ref[c // 2].astype(F32)
            parts.append(tile[(k % 2 * 2 + o) * W :][:W])
        out_ref[z] = jnp.concatenate(parts, axis=0).astype(BF16)


def low_backward(in_ref, y_ref, dinv_ref, mid_ref, top_ref, out_ref):
    carry = jnp.sum(in_ref[...].astype(F32), axis=0)
    left = (y_ref[...].astype(F32) - carry).reshape(L0, W, SN)
    for k in range(L0):
        out_ref[:, k * SN : (k + 1) * SN] = dot_nn(left[k].astype(BF16), dinv_ref[k]).astype(BF16)
    mid = mid_ref[...].astype(F32)
    for i in range(L1):
        out_ref[:, (L0 + i) * SN : (L0 + i + 1) * SN] = mid[i * W : (i + 1) * W].astype(BF16)
    top = top_ref[...].astype(F32)
    for i in range(L2):
        out_ref[:, (MID + i) * SN : (MID + i + 1) * SN] = top[i * W : (i + 1) * W].astype(BF16)


VM = pl.BlockSpec(memory_space=pltpu.VMEM)
SM = pl.BlockSpec(memory_space=pltpu.SMEM)
ANY = pl.BlockSpec(memory_space=pl.ANY)


def call(kernel, outs, *args, scratch=(), far=None):
    single = len(outs) == 1
    shapes = [jax.ShapeDtypeStruct(shape, kind) for shape, kind in outs]
    return pl.pallas_call(
        kernel,
        out_shape=shapes[0] if single else shapes,
        in_specs=[ANY if a is far else SM if a.dtype == jnp.int32 else VM for a in args],
        out_specs=VM if single else [VM] * len(outs),
        scratch_shapes=list(scratch),
        compiler_params=pltpu.CompilerParams(vmem_limit_bytes=24 * 1024 * 1024),
    )(*args)


def over_peers(pieces):
    return lax.all_to_all(pieces, "col", 0, 0, tiled=True, axis_index_groups=PEER_GROUPS)


def over_y(pieces):
    return lax.all_to_all(pieces, "col", 0, 0, tiled=True, axis_index_groups=Y_GROUPS)


def over_y_and_core(pieces):
    return lax.all_to_all(pieces, ("row", "col"), 0, 0, tiled=True, axis_index_groups=Y_CORE_GROUPS)


def over_z_by_y(pieces):
    return lax.all_to_all(pieces, ("row", "col"), 0, 0, tiled=True, axis_index_groups=MID_GROUPS)


def over_core(pieces):
    return lax.all_gather(pieces, "row", axis=0, axis_index_groups=CORE_GROUPS)


def swap(half):
    return lax.ppermute(half, "row", SWAP)


def over_z(pieces):
    return lax.all_to_all(pieces, "row", 0, 0, tiled=True, axis_index_groups=Z_GROUPS)


def on_device(rhs, dinv, blocks, block_row, block_col):
    place = jnp.stack([lax.axis_index("row"), lax.axis_index("col")]).astype(jnp.int32)
    right = rhs.T
    panels = pltpu.VMEM((LOWS + MIDS, N, SN), BF16)
    sums = pltpu.VMEM((LOWS + MIDS + 1, N, SN), F32)
    work = (panels, sums, pltpu.VMEM((SLOTS1 * SN, SN), BF16), pltpu.SemaphoreType.DMA)
    y_low, spread, packed = pl.pallas_call(
        low_forward,
        out_shape=[
            jax.ShapeDtypeStruct((64, SN), BF16),
            jax.ShapeDtypeStruct((Z, 64, SN), BF16),
            jax.ShapeDtypeStruct((SLOTS1 * SN + 16, SN), BF16),
        ],
        in_specs=[VM, VM, VM, ANY, ANY],
        out_specs=[VM, VM, VM],
        scratch_shapes=[
            pltpu.VMEM((L0, SN, SN), BF16),
            pltpu.SemaphoreType.DMA((L0 + SLOTS1,)),
        ],
        compiler_params=pltpu.CompilerParams(vmem_limit_bytes=63 * 1024 * 1024),
    )(right, block_row, block_col, dinv, blocks)
    lower = lax.ppermute(packed, "col", NEIGHBOURS)
    far = lower[-16:-15].astype(jnp.int32)
    lists = (block_row, block_col, far)

    sent = call(low_by_class, [((PEERS, 32, SN), BF16)], place, over_z(spread))
    low = over_core(over_peers(sent))
    part = call(
        mid_sums,
        [((PEERS, 2 * STRIP, SN), BF16)],
        place,
        *lists,
        low,
        blocks,
        lower,
        right,
        scratch=work,
        far=lower,
    )
    upper, part = lax.optimization_barrier((blocks[0, SLOTS1:].reshape(-1, SN), part))
    upper = lax.ppermute(upper, "col", NEIGHBOURS)
    y_mid, spread = call(
        mid_forward,
        [((2 * STRIP, SN), BF16), ((Z, 2 * STRIP, SN), BF16)],
        place,
        over_peers(part),
        dinv[L0:MID],
    )
    mid = over_core(over_y(over_z_by_y(spread)))
    part = call(
        top_sums, [((PEERS, 16, SN), BF16)], *lists, low, mid, blocks, upper, scratch=work, far=upper
    )
    x_top, spread = call(
        top_solve, [((16, SN), BF16), ((PEERS, 16, SN), BF16)], over_peers(part), right, dinv
    )
    low_part, sent = call(
        top_carries,
        [((LOWS, N, SN), F32), ((R, 2 * STRIP, SN), BF16)],
        *lists,
        over_peers(spread),
        blocks,
        upper,
        scratch=work,
        far=upper,
    )
    both = call(core_sum, [((Y, 2 * STRIP, SN), BF16)], over_y_and_core(sent))
    carry = over_z_by_y(both)
    spread = call(mid_backward, [((PEERS, 2 * STRIP, SN), BF16)], place, carry, y_mid, dinv[L0:MID])
    x_mid, keep, sent = call(
        low_carries,
        [((32, SN), BF16), ((PEERS, 32, SN), F32), ((PEERS, 32, SN), BF16)],
        place,
        *lists,
        over_peers(spread),
        low_part,
        blocks,
        lower,
        scratch=work,
        far=lower,
    )
    both = call(pair_sum, [((PEERS, 32, SN), BF16)], keep, swap(sent))
    sent = call(low_by_row, [((Z, 64, SN), BF16)], place, over_peers(both))
    out = call(low_backward, [((W, OWN * SN), BF16)], over_z(sent), y_low, dinv, x_mid, x_top)
    return out.T


def solution(mesh):
    placed = (
        P("row", "col"),
        P("row", None, None),
        P("row", "col", None, None),
        P("row", "col"),
        P("row", "col"),
    )
    return jax.shard_map(
        on_device, mesh=mesh, in_specs=placed, out_specs=P("row", "col"), check_vma=False
    )
```

```python
import jax
import jax.numpy as jnp
from jax import lax
from jax.experimental import pallas as pl
from jax.experimental.pallas import tpu as pltpu
from jax.sharding import PartitionSpec as P

SN = 256
L0 = 8
L1 = 4
L2 = 2
MID = L0 + L1
OWN = L0 + L1 + L2
SLOTS1 = 8
SLOTS2 = 6
SLOTS = 14
R = 16
C = 32
X = 4
Y = 8
Z = 8
W = 8
N = W * Y
LOWS = 4 * X
MIDS = 2 * X
F32 = jnp.float32
BF16 = jnp.bfloat16
Z_GROUPS = [[2 * z + core for z in range(Z)] for core in range(2)]
CORE_GROUPS = [[2 * z, 2 * z + 1] for z in range(Z)]
Y_GROUPS = [[X * y + x for y in range(Y)] for x in range(X)]
SWAP = [(r, r ^ 1) for r in range(R)]


def dot_nt(left, right):
    return lax.dot_general(left, right, (((1,), (1,)), ((), ())), preferred_element_type=F32)


def dot_nn(left, right):
    return lax.dot_general(left, right, (((1,), (0,)), ((), ())), preferred_element_type=F32)


def low_panel(column):
    return column % (2 * OWN) // OWN * MIDS + column % X * 2 + column % OWN // 4


def mid_panel(column):
    return column % (2 * OWN) // OWN * X + column % X


def panel_of(column):
    return jnp.where(column % OWN < L0, low_panel(column), LOWS + mid_panel(column))


def join(pieces, out_ref, first=0):
    count = pieces.shape[1] // W
    wide = pieces.astype(F32).reshape(Y, count, W, SN)
    for i in range(count):
        out_ref[first + i] = wide[:, i].reshape(N, SN).astype(BF16)


def cut(panels, kind=BF16):
    parts = [p.reshape(Y, W, SN) for p in panels]
    return jnp.stack(parts, axis=1).reshape(Y, W * len(parts), SN).astype(kind)


def slots(code_ref, mine_ref, others, first, final):
    for place in range(X):
        for q in range(first, final):
            at = (q - first) * SN
            tile = mine_ref[0, q] if place == 0 else others[place - 1][at : at + SN]
            yield code_ref[place, q], code_ref[place, 128 + q], tile


def pack(row_ref, col_ref, blocks_ref, out_ref, sems):
    fetch = []
    for q in range(SLOTS1):
        target = out_ref.at[pl.ds(q * SN, SN)]
        fetch.append(pltpu.make_async_copy(blocks_ref.at[0, q], target, sems.at[q]))
    for copy in fetch:
        copy.start()
    last = SLOTS1 * SN
    out_ref[last:] = jnp.zeros((16, SN), BF16)
    out_ref[last:, :SLOTS] = jnp.broadcast_to(row_ref[...].astype(F32), (16, SLOTS)).astype(BF16)
    out_ref[last:, 128 : 128 + SLOTS] = jnp.broadcast_to(
        col_ref[...].astype(F32), (16, SLOTS)
    ).astype(BF16)
    for copy in fetch:
        copy.wait()


def low_forward(rhs_ref, dinv_ref, y_ref, spread_ref):
    rows = []
    for k in range(L0):
        rows.append(dot_nt(rhs_ref[:, k * SN : (k + 1) * SN], dinv_ref[k]))
    y = jnp.concatenate(rows, axis=0).astype(BF16)
    y_ref[...] = y
    for z in range(Z):
        spread_ref[z] = y


def low_by_class(place_ref, in_ref, out_ref):
    core = place_ref[0] % 2
    for c in range(C):
        halves = []
        for o in range(2):
            a = (c + 2 * core) % 4
            z = (7 * ((c - 14 * core - a - 4 * o + 64) // 4)) % Z
            tile = in_ref[z, 32 * o : 32 * o + 32].astype(F32)
            piece = jnp.where(a == 0, tile[0:8], tile[8:16])
            other = jnp.where(a == 2, tile[16:24], tile[24:32])
            halves.append(jnp.where(a < 2, piece, other))
        x = c % X * 2 * W
        out_ref[c // X, x : x + 2 * W] = jnp.concatenate(halves, axis=0).astype(BF16)


def mid_sums(code_ref, low_ref, mine_ref, before_ref, after_ref, far_ref, out_ref, panels, acc):
    for p in range(2):
        join(low_ref[p], panels, p * MIDS)
    for i in range(L1 + 1):
        acc[i] = jnp.zeros((N, SN), F32)
    for row, column, tile in slots(code_ref, mine_ref, (before_ref, after_ref, far_ref), 0, SLOTS1):
        slot = jnp.where(row < OWN, row - L0, L1)
        source = jnp.minimum(panel_of(column), LOWS - 1)
        acc[slot] += dot_nt(panels[source], tile)
    out_ref[...] = cut([acc[i] for i in range(L1)])


def mid_forward(in_ref, rhs_ref, dinv_ref, y_ref, spread_ref):
    sums = jnp.sum(in_ref[...].astype(F32), axis=0)
    rows = []
    for i in range(L1):
        k = L0 + i
        right = rhs_ref[:, k * SN : (k + 1) * SN].astype(F32) - sums[i * W : (i + 1) * W]
        rows.append(dot_nt(right.astype(BF16), dinv_ref[k]))
    y = jnp.concatenate(rows, axis=0).astype(BF16)
    y_ref[...] = y
    for z in range(Z):
        spread_ref[z] = y


def mid_by_class(place_ref, in_ref, out_ref):
    core = place_ref[0] % 2
    for y in range(Y):
        octets = []
        for x in range(X):
            i = (x + 2 * core) % 4
            z = (7 * ((X * y + x - 14 * core - L0 - i + 64) // 4)) % Z
            tile = in_ref[z].astype(F32)
            octets.append(jnp.where(core == 0, tile[x * W :][:W], tile[(x + 2) % 4 * W :][:W]))
        out_ref[y] = jnp.concatenate(octets, axis=0).astype(BF16)


def top_sums(
    place_ref,
    code_ref,
    low_ref,
    mid_ref,
    rhs_ref,
    mine_ref,
    before_ref,
    after_ref,
    far_ref,
    out_ref,
    panels,
    acc,
):
    own = pl.multiple_of(place_ref[1] // X * W, W)
    for p in range(2):
        join(low_ref[p], panels, p * MIDS)
        join(mid_ref[p], panels, LOWS + p * X)
    for i in range(L2 + 1):
        acc[i] = jnp.zeros((N, SN), F32)
    for i in range(L2):
        acc[i, pl.ds(own, W)] = -rhs_ref[:, (MID + i) * SN : (MID + i + 1) * SN].astype(F32)
    others = (before_ref, after_ref, far_ref)
    for row, column, tile in slots(code_ref, mine_ref, others, SLOTS1, SLOTS):
        slot = jnp.where(row < OWN, row - MID, L2)
        acc[slot] += dot_nt(panels[panel_of(column)], tile)
    for i in range(L2):
        total = acc[i].astype(BF16)
        for y in range(Y):
            out_ref[y, i * N : (i + 1) * N] = total


def top_carries(
    place_ref,
    code_ref,
    in_ref,
    dinv_ref,
    mine_ref,
    before_ref,
    after_ref,
    far_ref,
    x_ref,
    low_ref,
    keep_ref,
    out_ref,
    known,
    acc,
):
    core = place_ref[0] % 2
    own = place_ref[1] // X
    octets = []
    for i in range(L2):
        right = -jnp.sum(in_ref[:, i * N : (i + 1) * N].astype(F32), axis=0)
        y = dot_nt(right.astype(BF16), dinv_ref[MID + i]).astype(BF16)
        x = dot_nn(y, dinv_ref[MID + i])
        known[i] = x.astype(BF16)
        octet = x[:W]
        for part in range(1, Y):
            octet = jnp.where(own == part, x[part * W : (part + 1) * W], octet)
        octets.append(octet)
    x_ref[...] = jnp.concatenate(octets, axis=0).astype(BF16)
    acc[...] = jnp.zeros_like(acc)
    others = (before_ref, after_ref, far_ref)
    for row, column, tile in slots(code_ref, mine_ref, others, SLOTS1, SLOTS):
        source = jnp.clip(row - MID, 0, L2 - 1)
        slot = jnp.where(row < OWN, panel_of(column), LOWS + MIDS)
        acc[slot] += dot_nn(known[source], tile)
    for p in range(LOWS):
        low_ref[p] = acc[p]
    keep_ref[...] = cut([acc[LOWS + core * X + x] for x in range(X)], F32)
    out_ref[...] = cut([acc[LOWS + (1 - core) * X + x] for x in range(X)])


def mid_by_row(place_ref, in_ref, out_ref):
    core = place_ref[0] % 2
    for z in range(Z):
        octets = []
        for i in range(L1):
            y = (28 * z + 14 * core + L0 + i) % C // X
            tile = in_ref[y].astype(F32)
            octets.append(jnp.where(core == 0, tile[i * W :][:W], tile[(i + 2) % 4 * W :][:W]))
        out_ref[z] = jnp.concatenate(octets, axis=0).astype(BF16)


def mid_backward(in_ref, y_ref, dinv_ref, x_ref, spread_ref):
    carry = jnp.sum(in_ref[...].astype(F32), axis=0)
    left = (y_ref[...].astype(F32) - carry).reshape(L1, W, SN)
    rows = [dot_nn(left[i].astype(BF16), dinv_ref[L0 + i]) for i in range(L1)]
    x = jnp.concatenate(rows, axis=0).astype(BF16)
    x_ref[...] = x
    for y in range(Y):
        spread_ref[y] = x


def low_carries(
    place_ref,
    code_ref,
    in_ref,
    part_ref,
    mine_ref,
    before_ref,
    after_ref,
    far_ref,
    keep_ref,
    out_ref,
    known,
    acc,
):
    core = place_ref[0] % 2
    join(in_ref[...], known)
    for p in range(LOWS):
        acc[p] = part_ref[p]
    acc[LOWS] = jnp.zeros((N, SN), F32)
    for row, column, tile in slots(code_ref, mine_ref, (before_ref, after_ref, far_ref), 0, SLOTS1):
        source = jnp.clip(row - L0, 0, L1 - 1)
        slot = jnp.where(row < OWN, jnp.minimum(panel_of(column), LOWS - 1), LOWS)
        acc[slot] += dot_nn(known[source], tile)
    keep_ref[...] = cut([acc[core * MIDS + i] for i in range(MIDS)], F32)
    out_ref[...] = cut([acc[(1 - core) * MIDS + i] for i in range(MIDS)])


def pair_sum(keep_ref, in_ref, out_ref):
    out_ref[...] = (keep_ref[...] + in_ref[...].astype(F32)).astype(BF16)


def low_by_row(place_ref, in_ref, out_ref):
    core = place_ref[0] % 2
    for z in range(Z):
        parts = []
        for k in range(L0):
            c = (28 * z + 14 * core + k) % C
            o = k // 4
            tile = in_ref[c // X].astype(F32)
            even = tile[(k % X * 2 + o) * W :][:W]
            odd = tile[((k + 2) % X * 2 + o) * W :][:W]
            parts.append(jnp.where(core == 0, even, odd))
        out_ref[z] = jnp.concatenate(parts, axis=0).astype(BF16)


def low_backward(in_ref, y_ref, dinv_ref, mid_ref, top_ref, out_ref):
    carry = jnp.sum(in_ref[...].astype(F32), axis=0)
    left = (y_ref[...].astype(F32) - carry).reshape(L0, W, SN)
    for k in range(L0):
        out_ref[:, k * SN : (k + 1) * SN] = dot_nn(left[k].astype(BF16), dinv_ref[k]).astype(BF16)
    mid = mid_ref[...].astype(F32)
    for i in range(L1):
        out_ref[:, (L0 + i) * SN : (L0 + i + 1) * SN] = mid[i * W : (i + 1) * W].astype(BF16)
    top = top_ref[...].astype(F32)
    for i in range(L2):
        out_ref[:, (MID + i) * SN : (MID + i + 1) * SN] = top[i * W : (i + 1) * W].astype(BF16)


VM = pl.BlockSpec(memory_space=pltpu.VMEM)
SM = pl.BlockSpec(memory_space=pltpu.SMEM)


def call(kernel, outs, *args, scratch=()):
    single = len(outs) == 1
    shapes = [jax.ShapeDtypeStruct(shape, kind) for shape, kind in outs]
    return pl.pallas_call(
        kernel,
        out_shape=shapes[0] if single else shapes,
        in_specs=[SM if a.dtype == jnp.int32 else VM for a in args],
        out_specs=VM if single else [VM] * len(outs),
        scratch_shapes=list(scratch),
        compiler_params=pltpu.CompilerParams(vmem_limit_bytes=40 * 1024 * 1024),
    )(*args)


def over_y(pieces):
    return lax.all_to_all(pieces, "col", 0, 0, tiled=True, axis_index_groups=Y_GROUPS)


def over_z(pieces):
    return lax.all_to_all(pieces, "row", 0, 0, tiled=True, axis_index_groups=Z_GROUPS)


def over_core(pieces):
    return lax.all_gather(pieces, "row", axis=0, axis_index_groups=CORE_GROUPS)


def swap(half):
    return lax.ppermute(half, "row", SWAP)


def along_x(array, step):
    return lax.ppermute(array, "col", [(c, c // X * X + (c + step) % X) for c in range(C)])


def on_device(rhs, dinv, blocks, block_row, block_col):
    place = jnp.stack([lax.axis_index("row"), lax.axis_index("col")]).astype(jnp.int32)
    right = rhs.T
    panels = pltpu.VMEM((LOWS + MIDS, N, SN), BF16)
    sums = pltpu.VMEM((LOWS + MIDS + 1, N, SN), F32)
    work = (panels, sums)

    y_low, spread = call(low_forward, [((64, SN), BF16), ((Z, 64, SN), BF16)], right, dinv)
    spread, given = lax.optimization_barrier((spread, blocks))
    packed = pl.pallas_call(
        pack,
        out_shape=jax.ShapeDtypeStruct((SLOTS1 * SN + 16, SN), BF16),
        in_specs=[VM, VM, pl.BlockSpec(memory_space=pl.ANY)],
        out_specs=VM,
        scratch_shapes=[pltpu.SemaphoreType.DMA((SLOTS1,))],
        compiler_params=pltpu.CompilerParams(vmem_limit_bytes=24 * 1024 * 1024),
    )(block_row, block_col, given)
    lower = [along_x(packed, 2), along_x(packed, 1), along_x(packed, -1)]
    code = jnp.concatenate([a[-16:-15] for a in [packed, *lower]]).astype(jnp.int32)

    sent = call(low_by_class, [((Y, 64, SN), BF16)], place, over_z(spread))
    low = over_core(over_y(sent))
    part = call(mid_sums, [((Y, 32, SN), BF16)], code, low, blocks, *lower, scratch=work)
    upper, part = lax.optimization_barrier((blocks[0, SLOTS1:].reshape(-1, SN), part))
    upper = [along_x(upper, 2), along_x(upper, 1), along_x(upper, -1)]
    y_mid, spread = call(
        mid_forward, [((32, SN), BF16), ((Z, 32, SN), BF16)], over_y(part), right, dinv
    )
    sent = call(mid_by_class, [((Y, 32, SN), BF16)], place, over_z(spread))
    mid = over_core(over_y(sent))
    part = call(
        top_sums,
        [((Y, 2 * N, SN), BF16)],
        place,
        code,
        low,
        mid,
        right,
        blocks,
        *upper,
        scratch=work,
    )
    x_top, low_part, keep, sent = call(
        top_carries,
        [((16, SN), BF16), ((LOWS, N, SN), F32), ((Y, 32, SN), F32), ((Y, 32, SN), BF16)],
        place,
        code,
        over_y(part),
        dinv,
        blocks,
        *upper,
        scratch=work,
    )
    both = call(pair_sum, [((Y, 32, SN), BF16)], keep, swap(sent))
    sent = call(mid_by_row, [((Z, 32, SN), BF16)], place, over_y(both))
    x_mid, spread = call(
        mid_backward, [((32, SN), BF16), ((Y, 32, SN), BF16)], over_z(sent), y_mid, dinv
    )
    keep, sent = call(
        low_carries,
        [((Y, 64, SN), F32), ((Y, 64, SN), BF16)],
        place,
        code,
        over_y(spread),
        low_part,
        blocks,
        *lower,
        scratch=work,
    )
    both = call(pair_sum, [((Y, 64, SN), BF16)], keep, swap(sent))
    sent = call(low_by_row, [((Z, 64, SN), BF16)], place, over_y(both))
    out = call(low_backward, [((W, OWN * SN), BF16)], over_z(sent), y_low, dinv, x_mid, x_top)
    return out.T


def solution(mesh):
    placed = (
        P("row", "col"),
        P("row", None, None),
        P("row", "col", None, None),
        P("row", "col"),
        P("row", "col"),
    )
    return jax.shard_map(
        on_device, mesh=mesh, in_specs=placed, out_specs=P("row", "col"), check_vma=False
    )
```

```python
import jax
import jax.numpy as jnp
from jax import lax
from jax.experimental import pallas as pl
from jax.experimental.pallas import tpu as pltpu
from jax.sharding import PartitionSpec as P

SN = 256
L0 = 8
L1 = 4
L2 = 2
MID = L0 + L1
OWN = L0 + L1 + L2
SLOTS1 = 8
SLOTS2 = 6
SLOTS = 14
R = 16
C = 32
X = 4
Y = 8
Z = 8
W = 8
N = W * Y
LOWS = 4 * X
MIDS = 2 * X
F32 = jnp.float32
BF16 = jnp.bfloat16
Z_GROUPS = [[2 * z + core for z in range(Z)] for core in range(2)]
CORE_GROUPS = [[2 * z, 2 * z + 1] for z in range(Z)]
Y_GROUPS = [[X * y + x for y in range(Y)] for x in range(X)]
SWAP = [(r, r ^ 1) for r in range(R)]


def dot_nt(left, right):
    return lax.dot_general(left, right, (((1,), (1,)), ((), ())), preferred_element_type=F32)


def dot_nn(left, right):
    return lax.dot_general(left, right, (((1,), (0,)), ((), ())), preferred_element_type=F32)


def low_panel(column):
    return column % (2 * OWN) // OWN * MIDS + column % X * 2 + column % OWN // 4


def mid_panel(column):
    return column % (2 * OWN) // OWN * X + column % X


def panel_of(column):
    return jnp.where(column % OWN < L0, low_panel(column), LOWS + mid_panel(column))


def join(pieces, out_ref, first=0):
    count = pieces.shape[1] // W
    wide = pieces.astype(F32).reshape(Y, count, W, SN)
    for i in range(count):
        out_ref[first + i] = wide[:, i].reshape(N, SN).astype(BF16)


def cut(panels, kind=BF16):
    parts = [p.reshape(Y, W, SN) for p in panels]
    return jnp.stack(parts, axis=1).reshape(Y, W * len(parts), SN).astype(kind)


def slots(code_ref, mine_ref, others, first, final):
    for place in range(X):
        for q in range(first, final):
            at = (q - first) * SN
            tile = mine_ref[0, q] if place == 0 else others[place - 1][at : at + SN]
            yield code_ref[place, q], code_ref[place, 128 + q], tile


def pack(row_ref, col_ref, blocks_ref, out_ref, sems):
    fetch = []
    for q in range(SLOTS1):
        target = out_ref.at[pl.ds(q * SN, SN)]
        fetch.append(pltpu.make_async_copy(blocks_ref.at[0, q], target, sems.at[q]))
    for copy in fetch:
        copy.start()
    last = SLOTS1 * SN
    out_ref[last:] = jnp.zeros((16, SN), BF16)
    out_ref[last:, :SLOTS] = jnp.broadcast_to(row_ref[...].astype(F32), (16, SLOTS)).astype(BF16)
    out_ref[last:, 128 : 128 + SLOTS] = jnp.broadcast_to(
        col_ref[...].astype(F32), (16, SLOTS)
    ).astype(BF16)
    for copy in fetch:
        copy.wait()


def low_forward(rhs_ref, dinv_ref, y_ref, spread_ref):
    rows = []
    for k in range(L0):
        rows.append(dot_nt(rhs_ref[:, k * SN : (k + 1) * SN], dinv_ref[k]))
    y = jnp.concatenate(rows, axis=0).astype(BF16)
    y_ref[...] = y
    for z in range(Z):
        spread_ref[z] = y


def low_by_class(place_ref, in_ref, out_ref):
    core = place_ref[0] % 2
    for c in range(C):
        halves = []
        for o in range(2):
            a = (c + 2 * core) % 4
            z = (7 * ((c - 14 * core - a - 4 * o + 64) // 4)) % Z
            tile = in_ref[z, 32 * o : 32 * o + 32].astype(F32)
            piece = jnp.where(a == 0, tile[0:8], tile[8:16])
            other = jnp.where(a == 2, tile[16:24], tile[24:32])
            halves.append(jnp.where(a < 2, piece, other))
        x = c % X * 2 * W
        out_ref[c // X, x : x + 2 * W] = jnp.concatenate(halves, axis=0).astype(BF16)


def mid_sums(code_ref, low_ref, mine_ref, before_ref, after_ref, far_ref, out_ref, panels, acc):
    for p in range(2):
        join(low_ref[p], panels, p * MIDS)
    for i in range(L1 + 1):
        acc[i] = jnp.zeros((N, SN), F32)
    for row, column, tile in slots(code_ref, mine_ref, (before_ref, after_ref, far_ref), 0, SLOTS1):
        slot = jnp.where(row < OWN, row - L0, L1)
        source = jnp.minimum(panel_of(column), LOWS - 1)
        acc[slot] += dot_nt(panels[source], tile)
    out_ref[...] = cut([acc[i] for i in range(L1)])


def mid_forward(in_ref, rhs_ref, dinv_ref, y_ref, spread_ref):
    sums = jnp.sum(in_ref[...].astype(F32), axis=0)
    rows = []
    for i in range(L1):
        k = L0 + i
        right = rhs_ref[:, k * SN : (k + 1) * SN].astype(F32) - sums[i * W : (i + 1) * W]
        rows.append(dot_nt(right.astype(BF16), dinv_ref[k]))
    y = jnp.concatenate(rows, axis=0).astype(BF16)
    y_ref[...] = y
    for z in range(Z):
        spread_ref[z] = y


def mid_by_class(place_ref, in_ref, out_ref):
    core = place_ref[0] % 2
    for y in range(Y):
        octets = []
        for x in range(X):
            i = (x + 2 * core) % 4
            z = (7 * ((X * y + x - 14 * core - L0 - i + 64) // 4)) % Z
            tile = in_ref[z].astype(F32)
            octets.append(jnp.where(core == 0, tile[x * W :][:W], tile[(x + 2) % 4 * W :][:W]))
        out_ref[y] = jnp.concatenate(octets, axis=0).astype(BF16)


def top_sums(
    place_ref,
    code_ref,
    low_ref,
    mid_ref,
    rhs_ref,
    mine_ref,
    before_ref,
    after_ref,
    far_ref,
    out_ref,
    panels,
    acc,
):
    own = pl.multiple_of(place_ref[1] // X * W, W)
    for p in range(2):
        join(low_ref[p], panels, p * MIDS)
        join(mid_ref[p], panels, LOWS + p * X)
    for i in range(L2 + 1):
        acc[i] = jnp.zeros((N, SN), F32)
    for i in range(L2):
        acc[i, pl.ds(own, W)] = -rhs_ref[:, (MID + i) * SN : (MID + i + 1) * SN].astype(F32)
    others = (before_ref, after_ref, far_ref)
    for row, column, tile in slots(code_ref, mine_ref, others, SLOTS1, SLOTS):
        slot = jnp.where(row < OWN, row - MID, L2)
        acc[slot] += dot_nt(panels[panel_of(column)], tile)
    for i in range(L2):
        total = acc[i].astype(BF16)
        for y in range(Y):
            out_ref[y, i * N : (i + 1) * N] = total


def top_carries(
    place_ref,
    code_ref,
    in_ref,
    dinv_ref,
    mine_ref,
    before_ref,
    after_ref,
    far_ref,
    x_ref,
    low_ref,
    keep_ref,
    out_ref,
    known,
    acc,
):
    core = place_ref[0] % 2
    own = place_ref[1] // X
    octets = []
    for i in range(L2):
        right = -jnp.sum(in_ref[:, i * N : (i + 1) * N].astype(F32), axis=0)
        y = dot_nt(right.astype(BF16), dinv_ref[MID + i]).astype(BF16)
        x = dot_nn(y, dinv_ref[MID + i])
        known[i] = x.astype(BF16)
        octet = x[:W]
        for part in range(1, Y):
            octet = jnp.where(own == part, x[part * W : (part + 1) * W], octet)
        octets.append(octet)
    x_ref[...] = jnp.concatenate(octets, axis=0).astype(BF16)
    acc[...] = jnp.zeros_like(acc)
    others = (before_ref, after_ref, far_ref)
    for row, column, tile in slots(code_ref, mine_ref, others, SLOTS1, SLOTS):
        source = jnp.clip(row - MID, 0, L2 - 1)
        slot = jnp.where(row < OWN, panel_of(column), LOWS + MIDS)
        acc[slot] += dot_nn(known[source], tile)
    for p in range(LOWS):
        low_ref[p] = acc[p]
    keep_ref[...] = cut([acc[LOWS + core * X + x] for x in range(X)], F32)
    out_ref[...] = cut([acc[LOWS + (1 - core) * X + x] for x in range(X)])


def mid_by_row(place_ref, in_ref, out_ref):
    core = place_ref[0] % 2
    for z in range(Z):
        octets = []
        for i in range(L1):
            y = (28 * z + 14 * core + L0 + i) % C // X
            tile = in_ref[y].astype(F32)
            octets.append(jnp.where(core == 0, tile[i * W :][:W], tile[(i + 2) % 4 * W :][:W]))
        out_ref[z] = jnp.concatenate(octets, axis=0).astype(BF16)


def mid_backward(in_ref, y_ref, dinv_ref, x_ref, spread_ref):
    carry = jnp.sum(in_ref[...].astype(F32), axis=0)
    left = (y_ref[...].astype(F32) - carry).reshape(L1, W, SN)
    rows = [dot_nn(left[i].astype(BF16), dinv_ref[L0 + i]) for i in range(L1)]
    x = jnp.concatenate(rows, axis=0).astype(BF16)
    x_ref[...] = x
    for y in range(Y):
        spread_ref[y] = x


def low_carries(
    place_ref,
    code_ref,
    in_ref,
    part_ref,
    mine_ref,
    before_ref,
    after_ref,
    far_ref,
    keep_ref,
    out_ref,
    known,
    acc,
):
    core = place_ref[0] % 2
    join(in_ref[...], known)
    for p in range(LOWS):
        acc[p] = part_ref[p]
    acc[LOWS] = jnp.zeros((N, SN), F32)
    for row, column, tile in slots(code_ref, mine_ref, (before_ref, after_ref, far_ref), 0, SLOTS1):
        source = jnp.clip(row - L0, 0, L1 - 1)
        slot = jnp.where(row < OWN, jnp.minimum(panel_of(column), LOWS - 1), LOWS)
        acc[slot] += dot_nn(known[source], tile)
    keep_ref[...] = cut([acc[core * MIDS + i] for i in range(MIDS)], F32)
    out_ref[...] = cut([acc[(1 - core) * MIDS + i] for i in range(MIDS)])


def pair_sum(keep_ref, in_ref, out_ref):
    out_ref[...] = (keep_ref[...] + in_ref[...].astype(F32)).astype(BF16)


def low_by_row(place_ref, in_ref, out_ref):
    core = place_ref[0] % 2
    for z in range(Z):
        parts = []
        for k in range(L0):
            c = (28 * z + 14 * core + k) % C
            o = k // 4
            tile = in_ref[c // X].astype(F32)
            even = tile[(k % X * 2 + o) * W :][:W]
            odd = tile[((k + 2) % X * 2 + o) * W :][:W]
            parts.append(jnp.where(core == 0, even, odd))
        out_ref[z] = jnp.concatenate(parts, axis=0).astype(BF16)


def low_backward(in_ref, y_ref, dinv_ref, mid_ref, top_ref, out_ref):
    carry = jnp.sum(in_ref[...].astype(F32), axis=0)
    left = (y_ref[...].astype(F32) - carry).reshape(L0, W, SN)
    for k in range(L0):
        out_ref[:, k * SN : (k + 1) * SN] = dot_nn(left[k].astype(BF16), dinv_ref[k]).astype(BF16)
    mid = mid_ref[...].astype(F32)
    for i in range(L1):
        out_ref[:, (L0 + i) * SN : (L0 + i + 1) * SN] = mid[i * W : (i + 1) * W].astype(BF16)
    top = top_ref[...].astype(F32)
    for i in range(L2):
        out_ref[:, (MID + i) * SN : (MID + i + 1) * SN] = top[i * W : (i + 1) * W].astype(BF16)


VM = pl.BlockSpec(memory_space=pltpu.VMEM)
SM = pl.BlockSpec(memory_space=pltpu.SMEM)


def call(kernel, outs, *args, scratch=()):
    single = len(outs) == 1
    shapes = [jax.ShapeDtypeStruct(shape, kind) for shape, kind in outs]
    return pl.pallas_call(
        kernel,
        out_shape=shapes[0] if single else shapes,
        in_specs=[SM if a.dtype == jnp.int32 else VM for a in args],
        out_specs=VM if single else [VM] * len(outs),
        scratch_shapes=list(scratch),
        compiler_params=pltpu.CompilerParams(vmem_limit_bytes=40 * 1024 * 1024),
    )(*args)


def over_y(pieces):
    return lax.all_to_all(pieces, "col", 0, 0, tiled=True, axis_index_groups=Y_GROUPS)


def over_z(pieces):
    return lax.all_to_all(pieces, "row", 0, 0, tiled=True, axis_index_groups=Z_GROUPS)


def over_core(pieces):
    return lax.all_gather(pieces, "row", axis=0, axis_index_groups=CORE_GROUPS)


def swap(half):
    return lax.ppermute(half, "row", SWAP)


def along_x(array, step):
    return lax.ppermute(array, "col", [(c, c // X * X + (c + step) % X) for c in range(C)])


def on_device(rhs, dinv, blocks, block_row, block_col):
    place = jnp.stack([lax.axis_index("row"), lax.axis_index("col")]).astype(jnp.int32)
    right = rhs.T
    panels = pltpu.VMEM((LOWS + MIDS, N, SN), BF16)
    sums = pltpu.VMEM((LOWS + MIDS + 1, N, SN), F32)
    work = (panels, sums)

    y_low, spread = call(low_forward, [((64, SN), BF16), ((Z, 64, SN), BF16)], right, dinv)
    spread, given = lax.optimization_barrier((spread, blocks))
    packed = pl.pallas_call(
        pack,
        out_shape=jax.ShapeDtypeStruct((SLOTS1 * SN + 16, SN), BF16),
        in_specs=[VM, VM, pl.BlockSpec(memory_space=pl.ANY)],
        out_specs=VM,
        scratch_shapes=[pltpu.SemaphoreType.DMA((SLOTS1,))],
        compiler_params=pltpu.CompilerParams(vmem_limit_bytes=24 * 1024 * 1024),
    )(block_row, block_col, given)
    far = along_x(packed, 2)
    before = along_x(packed, 1)
    sent = call(low_by_class, [((Y, 64, SN), BF16)], place, over_z(spread))
    sent, given = lax.optimization_barrier((sent, packed))
    lower = [far, before, along_x(given, -1)]
    code = jnp.concatenate([a[-16:-15] for a in [packed, *lower]]).astype(jnp.int32)
    low = over_core(over_y(sent))
    part = call(mid_sums, [((Y, 32, SN), BF16)], code, low, blocks, *lower, scratch=work)
    rest = blocks[0, SLOTS1:].reshape(-1, SN)
    part, given = lax.optimization_barrier((part, rest))
    upper = [along_x(given, 2)]
    y_mid, spread = call(
        mid_forward, [((32, SN), BF16), ((Z, 32, SN), BF16)], over_y(part), right, dinv
    )
    spread, given = lax.optimization_barrier((spread, given))
    upper.append(along_x(given, 1))
    sent = call(mid_by_class, [((Y, 32, SN), BF16)], place, over_z(spread))
    sent, given = lax.optimization_barrier((sent, given))
    upper.append(along_x(given, -1))
    mid = over_core(over_y(sent))
    part = call(
        top_sums,
        [((Y, 2 * N, SN), BF16)],
        place,
        code,
        low,
        mid,
        right,
        blocks,
        *upper,
        scratch=work,
    )
    x_top, low_part, keep, sent = call(
        top_carries,
        [((16, SN), BF16), ((LOWS, N, SN), F32), ((Y, 32, SN), F32), ((Y, 32, SN), BF16)],
        place,
        code,
        over_y(part),
        dinv,
        blocks,
        *upper,
        scratch=work,
    )
    both = call(pair_sum, [((Y, 32, SN), BF16)], keep, swap(sent))
    sent = call(mid_by_row, [((Z, 32, SN), BF16)], place, over_y(both))
    x_mid, spread = call(
        mid_backward, [((32, SN), BF16), ((Y, 32, SN), BF16)], over_z(sent), y_mid, dinv
    )
    keep, sent = call(
        low_carries,
        [((Y, 64, SN), F32), ((Y, 64, SN), BF16)],
        place,
        code,
        over_y(spread),
        low_part,
        blocks,
        *lower,
        scratch=work,
    )
    both = call(pair_sum, [((Y, 64, SN), BF16)], keep, swap(sent))
    sent = call(low_by_row, [((Z, 64, SN), BF16)], place, over_y(both))
    out = call(low_backward, [((W, OWN * SN), BF16)], over_z(sent), y_low, dinv, x_mid, x_top)
    return out.T


def solution(mesh):
    placed = (
        P("row", "col"),
        P("row", None, None),
        P("row", "col", None, None),
        P("row", "col"),
        P("row", "col"),
    )
    return jax.shard_map(
        on_device, mesh=mesh, in_specs=placed, out_specs=P("row", "col"), check_vma=False
    )
```

```python
import jax
import jax.numpy as jnp
from jax import lax
from jax.experimental import pallas as pl
from jax.experimental.pallas import tpu as pltpu
from jax.sharding import PartitionSpec as P

SN = 256
L0 = 8
L1 = 4
L2 = 2
MID = L0 + L1
OWN = L0 + L1 + L2
SLOTS1 = 8
SLOTS = 14
R = 16
C = 32
X = 4
Y = 8
Z = 8
HALVES = 2
PEERS = Y * HALVES
W = 8
STRIP = W * HALVES
N = W * PEERS
LOWS = 8
MIDS = 4
F32 = jnp.float32
BF16 = jnp.bfloat16
Z_GROUPS = [[2 * z + core for z in range(Z)] for core in range(2)]
CORE_GROUPS = [[2 * z, 2 * z + 1] for z in range(Z)]
Y_GROUPS = [[X * y + x for y in range(Y)] for x in range(X)]
PEER_GROUPS = [[2 * peer + (side + peer) % 2 for peer in range(PEERS)] for side in range(2)]
SWAP = [(r, r ^ 1) for r in range(R)]
NEIGHBOURS = [(c, c ^ 1) for c in range(C)]


def mid_groups():
    groups = []
    for core in range(2):
        for c in range(C):
            by_y = [0] * Y
            for z in range(Z):
                r = 2 * z + core
                column = [s % C for s in range(r * OWN + L0, r * OWN + MID) if s % X == c % X][0]
                by_y[column // X] = r * C + c
            groups.append(by_y)
    return groups


MID_GROUPS = mid_groups()


def dot_nt(left, right):
    return lax.dot_general(left, right, (((1,), (1,)), ((), ())), preferred_element_type=F32)


def dot_nn(left, right):
    return lax.dot_general(left, right, (((1,), (0,)), ((), ())), preferred_element_type=F32)


def low_panel(column):
    return column % (2 * OWN) // OWN * 4 + column % 2 * 2 + column % OWN // 4


def mid_panel(column):
    return column % (2 * OWN) // OWN * 2 + column % 2


def panel_of(column):
    return jnp.where(column % OWN < L0, low_panel(column), LOWS + mid_panel(column))


def join(pieces, out_ref, first=0):
    count = pieces.shape[1] // W
    wide = pieces.astype(F32).reshape(PEERS, count, W, SN)
    for i in range(count):
        out_ref[first + i] = wide[:, i].reshape(N, SN).astype(BF16)


def cut(panels, kind=BF16):
    parts = [p.reshape(PEERS, W, SN) for p in panels]
    return jnp.stack(parts, axis=1).reshape(PEERS, W * len(parts), SN).astype(kind)


def slots(row_ref, col_ref, far_ref, mine_ref, other_ref, first, final):
    for q in range(first, final):
        yield row_ref[0, q], col_ref[0, q], mine_ref[0, q]
    for q in range(first, final):
        tile = other_ref[(q - first) * SN : (q - first + 1) * SN]
        yield far_ref[0, q], far_ref[0, 128 + q], tile


def low_forward(
    rhs_ref, row_ref, col_ref, dinv_ref, blocks_ref, y_ref, spread_ref, sent_ref, factors, sems
):
    fetch = [pltpu.make_async_copy(dinv_ref.at[k], factors.at[k], sems.at[k]) for k in range(L0)]
    for copy in fetch:
        copy.start()
    pack = []
    for q in range(SLOTS1):
        target = sent_ref.at[pl.ds(q * SN, SN)]
        pack.append(pltpu.make_async_copy(blocks_ref.at[0, q], target, sems.at[L0 + q]))
    for copy in pack:
        copy.start()
    last = SLOTS1 * SN
    sent_ref[last:] = jnp.zeros((16, SN), BF16)
    sent_ref[last:, :SLOTS] = jnp.broadcast_to(row_ref[...].astype(F32), (16, SLOTS)).astype(BF16)
    sent_ref[last:, 128 : 128 + SLOTS] = jnp.broadcast_to(
        col_ref[...].astype(F32), (16, SLOTS)
    ).astype(BF16)
    rows = []
    for k in range(L0):
        fetch[k].wait()
        rows.append(dot_nt(rhs_ref[:, k * SN : (k + 1) * SN], factors[k]))
    y = jnp.concatenate(rows, axis=0).astype(BF16)
    y_ref[...] = y
    for z in range(Z):
        spread_ref[z] = y
    for copy in pack:
        copy.wait()


def low_by_class(place_ref, in_ref, out_ref):
    core = place_ref[0] % 2
    for c in range(C):
        halves = []
        for o in range(2):
            a = (c + 2 * core) % 4
            z = (7 * ((c - 14 * core - a - 4 * o + 64) // 4)) % Z
            tile = in_ref[z, 32 * o : 32 * o + 32].astype(F32)
            piece = jnp.where(a == 0, tile[0:8], tile[8:16])
            other = jnp.where(a == 2, tile[16:24], tile[24:32])
            halves.append(jnp.where(a < 2, piece, other))
        out_ref[c // 2, c % 2 * 16 : c % 2 * 16 + 16] = jnp.concatenate(halves, axis=0).astype(BF16)


def mid_sums(place_ref, row_ref, col_ref, far_ref, low_ref, mine_ref, other_ref, rhs_ref, out_ref, panels, acc):
    r = place_ref[0]
    own = pl.multiple_of(place_ref[1] // 2 * W, W)
    for p in range(2):
        join(low_ref[p], panels, 4 * p)
    acc[...] = jnp.zeros_like(acc)
    for i in range(L1):
        x = (r * OWN + L0 + i) % X
        acc[x, pl.ds(own, W)] = -rhs_ref[:, (L0 + i) * SN : (L0 + i + 1) * SN].astype(F32)
    for row, column, tile in slots(row_ref, col_ref, far_ref, mine_ref, other_ref, 0, SLOTS1):
        slot = jnp.where(row < OWN, (r * OWN + row) % X, X)
        source = jnp.minimum(panel_of(column), LOWS - 1)
        acc[slot] += dot_nt(panels[source], tile)
    for x in range(X):
        strips = acc[x].astype(BF16)
        for y in range(Y):
            out_ref[2 * y + x // 2, x % 2 * STRIP : x % 2 * STRIP + STRIP] = strips[y * STRIP :][:STRIP]


def mid_forward(place_ref, in_ref, dinv_ref, y_ref, spread_ref):
    right = -jnp.sum(in_ref[...].astype(F32), axis=0)
    rows = []
    for b in range(2):
        k = L0 + (place_ref[1] // 2 * 2 + b + 2 * place_ref[0]) % X
        rows.append(dot_nt(right[b * STRIP :][:STRIP].astype(BF16), dinv_ref[k]))
    y = jnp.concatenate(rows, axis=0).astype(BF16)
    y_ref[...] = y
    for z in range(Z):
        spread_ref[z] = y


def top_sums(row_ref, col_ref, far_ref, low_ref, mid_ref, mine_ref, other_ref, out_ref, panels, acc):
    for p in range(2):
        join(low_ref[p], panels, 4 * p)
        for b in range(2):
            for y in range(Y):
                strip = mid_ref[p, y, b * STRIP : (b + 1) * STRIP]
                panels[LOWS + 2 * p + b, y * STRIP : (y + 1) * STRIP] = strip
    acc[...] = jnp.zeros_like(acc)
    for row, column, tile in slots(row_ref, col_ref, far_ref, mine_ref, other_ref, SLOTS1, SLOTS):
        slot = jnp.where(row < OWN, row - MID, L2)
        source = panel_of(column)
        acc[slot] += dot_nt(panels[source], tile)
    out_ref[...] = cut([acc[i] for i in range(L2)])


def top_solve(in_ref, rhs_ref, dinv_ref, x_ref, spread_ref):
    sums = jnp.sum(in_ref[...].astype(F32), axis=0)
    rows = []
    for i in range(L2):
        k = MID + i
        right = rhs_ref[:, k * SN : (k + 1) * SN].astype(F32) - sums[i * W : (i + 1) * W]
        y = dot_nt(right.astype(BF16), dinv_ref[k]).astype(BF16)
        rows.append(dot_nn(y, dinv_ref[k]))
    x = jnp.concatenate(rows, axis=0).astype(BF16)
    x_ref[...] = x
    for peer in range(PEERS):
        spread_ref[peer] = x


def top_carries(
    place_ref, row_ref, col_ref, far_ref, in_ref, mine_ref, other_ref, low_ref, keep_ref, out_ref, known, acc
):
    core = place_ref[0] % 2
    join(in_ref[...], known)
    acc[...] = jnp.zeros_like(acc)
    for row, column, tile in slots(row_ref, col_ref, far_ref, mine_ref, other_ref, SLOTS1, SLOTS):
        source = jnp.clip(row - MID, 0, L2 - 1)
        slot = jnp.where(row < OWN, panel_of(column), LOWS + MIDS)
        acc[slot] += dot_nn(known[source], tile)
    for p in range(LOWS):
        low_ref[p] = acc[p]
    for b in range(2):
        keep = acc[LOWS + 2 * core + b]
        sent = acc[LOWS + 2 * (1 - core) + b].astype(BF16)
        for y in range(Y):
            keep_ref[y, b * STRIP : (b + 1) * STRIP] = keep[y * STRIP : (y + 1) * STRIP]
            out_ref[y, b * STRIP : (b + 1) * STRIP] = sent[y * STRIP : (y + 1) * STRIP]


def mid_backward(place_ref, in_ref, y_ref, dinv_ref, spread_ref):
    left = y_ref[...].astype(F32) - jnp.sum(in_ref[...].astype(F32), axis=0)
    rows = []
    for b in range(2):
        k = L0 + (place_ref[1] // 2 * 2 + b + 2 * place_ref[0]) % X
        rows.append(dot_nn(left[b * STRIP :][:STRIP].astype(BF16), dinv_ref[k]))
    x = jnp.concatenate(rows, axis=0).astype(BF16)
    for peer in range(PEERS):
        spread_ref[peer] = x


def low_carries(
    place_ref,
    row_ref,
    col_ref,
    far_ref,
    in_ref,
    part_ref,
    mine_ref,
    other_ref,
    x_ref,
    keep_ref,
    out_ref,
    known,
    acc,
):
    r = place_ref[0]
    peer = place_ref[1] // 2
    core = r % 2
    for x in range(X):
        for y in range(Y):
            strip = in_ref[2 * y + x // 2, x % 2 * STRIP : x % 2 * STRIP + STRIP]
            known[x, y * STRIP : (y + 1) * STRIP] = strip
    own = []
    for i in range(L1):
        x = (r * OWN + L0 + i) % X
        strips = in_ref[peer // 2 * 2 + x // 2].astype(F32)
        octet = jnp.where(x % 2 == 0, strips[:STRIP], strips[STRIP:])
        own.append(jnp.where(peer % 2 == 0, octet[:W], octet[W:]))
    x_ref[...] = jnp.concatenate(own, axis=0).astype(BF16)
    for p in range(LOWS):
        acc[p] = part_ref[p]
    acc[LOWS] = jnp.zeros((N, SN), F32)
    for row, column, tile in slots(row_ref, col_ref, far_ref, mine_ref, other_ref, 0, SLOTS1):
        source = (r * OWN + row) % X
        panel = jnp.minimum(panel_of(column), LOWS - 1)
        slot = jnp.where(row < OWN, panel, LOWS)
        acc[slot] += dot_nn(known[source], tile)
    keep_ref[...] = cut([acc[4 * core + i] for i in range(4)], F32)
    out_ref[...] = cut([acc[4 * (1 - core) + i] for i in range(4)])


def pair_sum(keep_ref, in_ref, out_ref):
    out_ref[...] = (keep_ref[...] + in_ref[...].astype(F32)).astype(BF16)


def low_by_row(place_ref, in_ref, out_ref):
    core = place_ref[0] % 2
    for z in range(Z):
        parts = []
        for k in range(L0):
            c = (28 * z + 14 * core + k) % C
            o = k // 4
            tile = in_ref[c // 2].astype(F32)
            parts.append(tile[(k % 2 * 2 + o) * W :][:W])
        out_ref[z] = jnp.concatenate(parts, axis=0).astype(BF16)


def low_backward(in_ref, y_ref, dinv_ref, mid_ref, top_ref, out_ref):
    carry = jnp.sum(in_ref[...].astype(F32), axis=0)
    left = (y_ref[...].astype(F32) - carry).reshape(L0, W, SN)
    for k in range(L0):
        out_ref[:, k * SN : (k + 1) * SN] = dot_nn(left[k].astype(BF16), dinv_ref[k]).astype(BF16)
    mid = mid_ref[...].astype(F32)
    for i in range(L1):
        out_ref[:, (L0 + i) * SN : (L0 + i + 1) * SN] = mid[i * W : (i + 1) * W].astype(BF16)
    top = top_ref[...].astype(F32)
    for i in range(L2):
        out_ref[:, (MID + i) * SN : (MID + i + 1) * SN] = top[i * W : (i + 1) * W].astype(BF16)


VM = pl.BlockSpec(memory_space=pltpu.VMEM)
SM = pl.BlockSpec(memory_space=pltpu.SMEM)


def call(kernel, outs, *args, scratch=()):
    single = len(outs) == 1
    shapes = [jax.ShapeDtypeStruct(shape, kind) for shape, kind in outs]
    return pl.pallas_call(
        kernel,
        out_shape=shapes[0] if single else shapes,
        in_specs=[SM if a.dtype == jnp.int32 else VM for a in args],
        out_specs=VM if single else [VM] * len(outs),
        scratch_shapes=list(scratch),
        compiler_params=pltpu.CompilerParams(vmem_limit_bytes=24 * 1024 * 1024),
    )(*args)


def over_peers(pieces):
    return lax.all_to_all(pieces, "col", 0, 0, tiled=True, axis_index_groups=PEER_GROUPS)


def over_y(pieces):
    return lax.all_to_all(pieces, "col", 0, 0, tiled=True, axis_index_groups=Y_GROUPS)


def over_z_by_y(pieces):
    return lax.all_to_all(pieces, ("row", "col"), 0, 0, tiled=True, axis_index_groups=MID_GROUPS)


def over_core(pieces):
    return lax.all_gather(pieces, "row", axis=0, axis_index_groups=CORE_GROUPS)


def swap(half):
    return lax.ppermute(half, "row", SWAP)


def over_z(pieces):
    return lax.all_to_all(pieces, "row", 0, 0, tiled=True, axis_index_groups=Z_GROUPS)


def on_device(rhs, dinv, blocks, block_row, block_col):
    place = jnp.stack([lax.axis_index("row"), lax.axis_index("col")]).astype(jnp.int32)
    right = rhs.T
    panels = pltpu.VMEM((LOWS + MIDS, N, SN), BF16)
    sums = pltpu.VMEM((LOWS + MIDS + 1, N, SN), F32)
    work = (panels, sums)
    whole = pl.BlockSpec(memory_space=pl.ANY)
    y_low, spread, packed = pl.pallas_call(
        low_forward,
        out_shape=[
            jax.ShapeDtypeStruct((64, SN), BF16),
            jax.ShapeDtypeStruct((Z, 64, SN), BF16),
            jax.ShapeDtypeStruct((SLOTS1 * SN + 16, SN), BF16),
        ],
        in_specs=[VM, VM, VM, whole, whole],
        out_specs=[VM, VM, VM],
        scratch_shapes=[
            pltpu.VMEM((L0, SN, SN), BF16),
            pltpu.SemaphoreType.DMA((L0 + SLOTS1,)),
        ],
        compiler_params=pltpu.CompilerParams(vmem_limit_bytes=63 * 1024 * 1024),
    )(right, block_row, block_col, dinv, blocks)
    lower = lax.ppermute(packed, "col", NEIGHBOURS)
    far = lower[-16:-15].astype(jnp.int32)
    lists = (block_row, block_col, far)

    sent = call(low_by_class, [((PEERS, 32, SN), BF16)], place, over_z(spread))
    low = over_core(over_peers(sent))
    part = call(
        mid_sums,
        [((PEERS, 2 * STRIP, SN), BF16)],
        place,
        *lists,
        low,
        blocks,
        lower,
        right,
        scratch=work,
    )
    y_mid, spread = call(
        mid_forward,
        [((2 * STRIP, SN), BF16), ((Z, 2 * STRIP, SN), BF16)],
        place,
        over_peers(part),
        dinv,
    )
    upper, spread = lax.optimization_barrier((blocks[0, SLOTS1:].reshape(-1, SN), spread))
    upper = lax.ppermute(upper, "col", NEIGHBOURS)
    mid = over_core(over_y(over_z_by_y(spread)))
    part = call(
        top_sums, [((PEERS, 16, SN), BF16)], *lists, low, mid, blocks, upper, scratch=work
    )
    x_top, spread = call(
        top_solve, [((16, SN), BF16), ((PEERS, 16, SN), BF16)], over_peers(part), right, dinv
    )
    low_part, keep, sent = call(
        top_carries,
        [
            ((LOWS, N, SN), F32),
            ((Y, 2 * STRIP, SN), F32),
            ((Y, 2 * STRIP, SN), BF16),
        ],
        place,
        *lists,
        over_peers(spread),
        blocks,
        upper,
        scratch=work,
    )
    both = call(pair_sum, [((Y, 2 * STRIP, SN), BF16)], keep, swap(sent))
    carry = over_z_by_y(over_y(both))
    spread = call(mid_backward, [((PEERS, 2 * STRIP, SN), BF16)], place, carry, y_mid, dinv)
    x_mid, keep, sent = call(
        low_carries,
        [((32, SN), BF16), ((PEERS, 32, SN), F32), ((PEERS, 32, SN), BF16)],
        place,
        *lists,
        over_peers(spread),
        low_part,
        blocks,
        lower,
        scratch=work,
    )
    both = call(pair_sum, [((PEERS, 32, SN), BF16)], keep, swap(sent))
    sent = call(low_by_row, [((Z, 64, SN), BF16)], place, over_peers(both))
    out = call(low_backward, [((W, OWN * SN), BF16)], over_z(sent), y_low, dinv, x_mid, x_top)
    return out.T


def solution(mesh):
    placed = (
        P("row", "col"),
        P("row", None, None),
        P("row", "col", None, None),
        P("row", "col"),
        P("row", "col"),
    )
    return jax.shard_map(
        on_device, mesh=mesh, in_specs=placed, out_specs=P("row", "col"), check_vma=False
    )
```

```python
import jax
import jax.numpy as jnp
from jax import lax
from jax.experimental import pallas as pl
from jax.experimental.pallas import tpu as pltpu
from jax.sharding import PartitionSpec as P

SN = 256
L0 = 8
L1 = 4
L2 = 2
MID = L0 + L1
OWN = L0 + L1 + L2
SLOTS1 = 8
SLOTS = 14
R = 16
C = 32
X = 4
Y = 8
Z = 8
HALVES = 2
PEERS = Y * HALVES
W = 8
STRIP = W * HALVES
N = W * PEERS
LOWS = 8
MIDS = 4
F32 = jnp.float32
BF16 = jnp.bfloat16
Z_GROUPS = [[2 * z + core for z in range(Z)] for core in range(2)]
CORE_GROUPS = [[2 * z, 2 * z + 1] for z in range(Z)]
Y_GROUPS = [[X * y + x for y in range(Y)] for x in range(X)]
PEER_GROUPS = [[2 * peer + (side + peer) % 2 for peer in range(PEERS)] for side in range(2)]
SWAP = [(r, r ^ 1) for r in range(R)]
NEIGHBOURS = [(c, c ^ 1) for c in range(C)]


def mid_groups():
    groups = []
    for core in range(2):
        for c in range(C):
            by_y = [0] * Y
            for z in range(Z):
                r = 2 * z + core
                column = [s % C for s in range(r * OWN + L0, r * OWN + MID) if s % X == c % X][0]
                by_y[column // X] = r * C + c
            groups.append(by_y)
    return groups


MID_GROUPS = mid_groups()


def dot_nt(left, right):
    return lax.dot_general(left, right, (((1,), (1,)), ((), ())), preferred_element_type=F32)


def dot_nn(left, right):
    return lax.dot_general(left, right, (((1,), (0,)), ((), ())), preferred_element_type=F32)


def low_panel(column):
    return column % (2 * OWN) // OWN * 4 + column % 2 * 2 + column % OWN // 4


def mid_panel(column):
    return column % (2 * OWN) // OWN * 2 + column % 2


def panel_of(column):
    return jnp.where(column % OWN < L0, low_panel(column), LOWS + mid_panel(column))


def join(pieces, out_ref, first=0):
    count = pieces.shape[1] // W
    wide = pieces.astype(F32).reshape(PEERS, count, W, SN)
    for i in range(count):
        out_ref[first + i] = wide[:, i].reshape(N, SN).astype(BF16)


def cut(panels, kind=BF16):
    parts = [p.reshape(PEERS, W, SN) for p in panels]
    return jnp.stack(parts, axis=1).reshape(PEERS, W * len(parts), SN).astype(kind)


def slots(row_ref, col_ref, far_ref, mine_ref, other_ref, first, final):
    for q in range(first, final):
        yield row_ref[0, q], col_ref[0, q], mine_ref[0, q]
    for q in range(first, final):
        tile = other_ref[(q - first) * SN : (q - first + 1) * SN]
        yield far_ref[0, q], far_ref[0, 128 + q], tile


def low_forward(
    rhs_ref, row_ref, col_ref, dinv_ref, blocks_ref, y_ref, spread_ref, sent_ref, factors, sems
):
    fetch = [pltpu.make_async_copy(dinv_ref.at[k], factors.at[k], sems.at[k]) for k in range(L0)]
    for copy in fetch:
        copy.start()
    pack = []
    for q in range(SLOTS1):
        target = sent_ref.at[pl.ds(q * SN, SN)]
        pack.append(pltpu.make_async_copy(blocks_ref.at[0, q], target, sems.at[L0 + q]))
    for copy in pack:
        copy.start()
    last = SLOTS1 * SN
    sent_ref[last:] = jnp.zeros((16, SN), BF16)
    sent_ref[last:, :SLOTS] = jnp.broadcast_to(row_ref[...].astype(F32), (16, SLOTS)).astype(BF16)
    sent_ref[last:, 128 : 128 + SLOTS] = jnp.broadcast_to(
        col_ref[...].astype(F32), (16, SLOTS)
    ).astype(BF16)
    rows = []
    for k in range(L0):
        fetch[k].wait()
        rows.append(dot_nt(rhs_ref[:, k * SN : (k + 1) * SN], factors[k]))
    y = jnp.concatenate(rows, axis=0).astype(BF16)
    y_ref[...] = y
    for z in range(Z):
        spread_ref[z] = y
    for copy in pack:
        copy.wait()


def low_by_class(place_ref, in_ref, out_ref):
    core = place_ref[0] % 2
    for c in range(C):
        halves = []
        for o in range(2):
            a = (c + 2 * core) % 4
            z = (7 * ((c - 14 * core - a - 4 * o + 64) // 4)) % Z
            tile = in_ref[z, 32 * o : 32 * o + 32].astype(F32)
            piece = jnp.where(a == 0, tile[0:8], tile[8:16])
            other = jnp.where(a == 2, tile[16:24], tile[24:32])
            halves.append(jnp.where(a < 2, piece, other))
        out_ref[c // 2, c % 2 * 16 : c % 2 * 16 + 16] = jnp.concatenate(halves, axis=0).astype(BF16)


def mid_sums(place_ref, row_ref, col_ref, far_ref, low_ref, mine_ref, other_ref, rhs_ref, out_ref, panels, acc):
    r = place_ref[0]
    own = pl.multiple_of(place_ref[1] // 2 * W, W)
    for p in range(2):
        join(low_ref[p], panels, 4 * p)
    acc[...] = jnp.zeros_like(acc)
    for i in range(L1):
        x = (r * OWN + L0 + i) % X
        acc[x, pl.ds(own, W)] = -rhs_ref[:, (L0 + i) * SN : (L0 + i + 1) * SN].astype(F32)
    for row, column, tile in slots(row_ref, col_ref, far_ref, mine_ref, other_ref, 0, SLOTS1):
        slot = jnp.where(row < OWN, (r * OWN + row) % X, X)
        source = jnp.minimum(panel_of(column), LOWS - 1)
        acc[slot] += dot_nt(panels[source], tile)
    for x in range(X):
        strips = acc[x].astype(BF16)
        for y in range(Y):
            out_ref[2 * y + x // 2, x % 2 * STRIP : x % 2 * STRIP + STRIP] = strips[y * STRIP :][:STRIP]


def mid_forward(place_ref, in_ref, dinv_ref, y_ref, spread_ref):
    right = -jnp.sum(in_ref[...].astype(F32), axis=0)
    rows = []
    for b in range(2):
        k = L0 + (place_ref[1] // 2 * 2 + b + 2 * place_ref[0]) % X
        rows.append(dot_nt(right[b * STRIP :][:STRIP].astype(BF16), dinv_ref[k]))
    y = jnp.concatenate(rows, axis=0).astype(BF16)
    y_ref[...] = y
    for z in range(Z):
        spread_ref[z] = y


def top_sums(row_ref, col_ref, far_ref, low_ref, mid_ref, mine_ref, other_ref, out_ref, panels, acc):
    for p in range(2):
        join(low_ref[p], panels, 4 * p)
        for b in range(2):
            for y in range(Y):
                strip = mid_ref[p, y, b * STRIP : (b + 1) * STRIP]
                panels[LOWS + 2 * p + b, y * STRIP : (y + 1) * STRIP] = strip
    acc[...] = jnp.zeros_like(acc)
    for row, column, tile in slots(row_ref, col_ref, far_ref, mine_ref, other_ref, SLOTS1, SLOTS):
        slot = jnp.where(row < OWN, row - MID, L2)
        source = panel_of(column)
        acc[slot] += dot_nt(panels[source], tile)
    out_ref[...] = cut([acc[i] for i in range(L2)])


def top_solve(in_ref, rhs_ref, dinv_ref, x_ref, spread_ref):
    sums = jnp.sum(in_ref[...].astype(F32), axis=0)
    rows = []
    for i in range(L2):
        k = MID + i
        right = rhs_ref[:, k * SN : (k + 1) * SN].astype(F32) - sums[i * W : (i + 1) * W]
        y = dot_nt(right.astype(BF16), dinv_ref[k]).astype(BF16)
        rows.append(dot_nn(y, dinv_ref[k]))
    x = jnp.concatenate(rows, axis=0).astype(BF16)
    x_ref[...] = x
    for peer in range(PEERS):
        spread_ref[peer] = x


def top_carries(
    place_ref, row_ref, col_ref, far_ref, in_ref, mine_ref, other_ref, low_ref, keep_ref, out_ref, known, acc
):
    core = place_ref[0] % 2
    join(in_ref[...], known)
    acc[...] = jnp.zeros_like(acc)
    for row, column, tile in slots(row_ref, col_ref, far_ref, mine_ref, other_ref, SLOTS1, SLOTS):
        source = jnp.clip(row - MID, 0, L2 - 1)
        slot = jnp.where(row < OWN, panel_of(column), LOWS + MIDS)
        acc[slot] += dot_nn(known[source], tile)
    for p in range(LOWS):
        low_ref[p] = acc[p]
    for b in range(2):
        keep = acc[LOWS + 2 * core + b]
        sent = acc[LOWS + 2 * (1 - core) + b].astype(BF16)
        for y in range(Y):
            keep_ref[y, b * STRIP : (b + 1) * STRIP] = keep[y * STRIP : (y + 1) * STRIP]
            out_ref[y, b * STRIP : (b + 1) * STRIP] = sent[y * STRIP : (y + 1) * STRIP]


def mid_backward(place_ref, in_ref, y_ref, dinv_ref, spread_ref):
    left = y_ref[...].astype(F32) - jnp.sum(in_ref[...].astype(F32), axis=0)
    rows = []
    for b in range(2):
        k = L0 + (place_ref[1] // 2 * 2 + b + 2 * place_ref[0]) % X
        rows.append(dot_nn(left[b * STRIP :][:STRIP].astype(BF16), dinv_ref[k]))
    x = jnp.concatenate(rows, axis=0).astype(BF16)
    for peer in range(PEERS):
        spread_ref[peer] = x


def low_carries(
    place_ref,
    row_ref,
    col_ref,
    far_ref,
    in_ref,
    part_ref,
    mine_ref,
    other_ref,
    x_ref,
    keep_ref,
    out_ref,
    known,
    acc,
):
    r = place_ref[0]
    peer = place_ref[1] // 2
    core = r % 2
    for x in range(X):
        for y in range(Y):
            strip = in_ref[2 * y + x // 2, x % 2 * STRIP : x % 2 * STRIP + STRIP]
            known[x, y * STRIP : (y + 1) * STRIP] = strip
    own = []
    for i in range(L1):
        x = (r * OWN + L0 + i) % X
        strips = in_ref[peer // 2 * 2 + x // 2].astype(F32)
        octet = jnp.where(x % 2 == 0, strips[:STRIP], strips[STRIP:])
        own.append(jnp.where(peer % 2 == 0, octet[:W], octet[W:]))
    x_ref[...] = jnp.concatenate(own, axis=0).astype(BF16)
    for p in range(LOWS):
        acc[p] = part_ref[p]
    acc[LOWS] = jnp.zeros((N, SN), F32)
    for row, column, tile in slots(row_ref, col_ref, far_ref, mine_ref, other_ref, 0, SLOTS1):
        source = (r * OWN + row) % X
        panel = jnp.minimum(panel_of(column), LOWS - 1)
        slot = jnp.where(row < OWN, panel, LOWS)
        acc[slot] += dot_nn(known[source], tile)
    keep_ref[...] = cut([acc[4 * core + i] for i in range(4)], F32)
    out_ref[...] = cut([acc[4 * (1 - core) + i] for i in range(4)])


def pair_sum(keep_ref, in_ref, out_ref):
    out_ref[...] = (keep_ref[...] + in_ref[...].astype(F32)).astype(BF16)


def low_by_row(place_ref, in_ref, out_ref):
    core = place_ref[0] % 2
    for z in range(Z):
        parts = []
        for k in range(L0):
            c = (28 * z + 14 * core + k) % C
            o = k // 4
            tile = in_ref[c // 2].astype(F32)
            parts.append(tile[(k % 2 * 2 + o) * W :][:W])
        out_ref[z] = jnp.concatenate(parts, axis=0).astype(BF16)


def low_backward(in_ref, y_ref, dinv_ref, mid_ref, top_ref, out_ref):
    carry = jnp.sum(in_ref[...].astype(F32), axis=0)
    left = (y_ref[...].astype(F32) - carry).reshape(L0, W, SN)
    for k in range(L0):
        out_ref[:, k * SN : (k + 1) * SN] = dot_nn(left[k].astype(BF16), dinv_ref[k]).astype(BF16)
    mid = mid_ref[...].astype(F32)
    for i in range(L1):
        out_ref[:, (L0 + i) * SN : (L0 + i + 1) * SN] = mid[i * W : (i + 1) * W].astype(BF16)
    top = top_ref[...].astype(F32)
    for i in range(L2):
        out_ref[:, (MID + i) * SN : (MID + i + 1) * SN] = top[i * W : (i + 1) * W].astype(BF16)


VM = pl.BlockSpec(memory_space=pltpu.VMEM)
SM = pl.BlockSpec(memory_space=pltpu.SMEM)


def call(kernel, outs, *args, scratch=()):
    single = len(outs) == 1
    shapes = [jax.ShapeDtypeStruct(shape, kind) for shape, kind in outs]
    return pl.pallas_call(
        kernel,
        out_shape=shapes[0] if single else shapes,
        in_specs=[SM if a.dtype == jnp.int32 else VM for a in args],
        out_specs=VM if single else [VM] * len(outs),
        scratch_shapes=list(scratch),
        compiler_params=pltpu.CompilerParams(vmem_limit_bytes=24 * 1024 * 1024),
    )(*args)


def over_peers(pieces):
    return lax.all_to_all(pieces, "col", 0, 0, tiled=True, axis_index_groups=PEER_GROUPS)


def over_y(pieces):
    return lax.all_to_all(pieces, "col", 0, 0, tiled=True, axis_index_groups=Y_GROUPS)


def over_z_by_y(pieces):
    return lax.all_to_all(pieces, ("row", "col"), 0, 0, tiled=True, axis_index_groups=MID_GROUPS)


def over_core(pieces):
    return lax.all_gather(pieces, "row", axis=0, axis_index_groups=CORE_GROUPS)


def swap(half):
    return lax.ppermute(half, "row", SWAP)


def over_z(pieces):
    return lax.all_to_all(pieces, "row", 0, 0, tiled=True, axis_index_groups=Z_GROUPS)


def on_device(rhs, dinv, blocks, block_row, block_col):
    place = jnp.stack([lax.axis_index("row"), lax.axis_index("col")]).astype(jnp.int32)
    right = rhs.T
    panels = pltpu.VMEM((LOWS + MIDS, N, SN), BF16)
    sums = pltpu.VMEM((LOWS + MIDS + 1, N, SN), F32)
    work = (panels, sums)
    whole = pl.BlockSpec(memory_space=pl.ANY)
    y_low, spread, packed = pl.pallas_call(
        low_forward,
        out_shape=[
            jax.ShapeDtypeStruct((64, SN), BF16),
            jax.ShapeDtypeStruct((Z, 64, SN), BF16),
            jax.ShapeDtypeStruct((SLOTS1 * SN + 16, SN), BF16),
        ],
        in_specs=[VM, VM, VM, whole, whole],
        out_specs=[VM, VM, VM],
        scratch_shapes=[
            pltpu.VMEM((L0, SN, SN), BF16),
            pltpu.SemaphoreType.DMA((L0 + SLOTS1,)),
        ],
        compiler_params=pltpu.CompilerParams(vmem_limit_bytes=63 * 1024 * 1024),
    )(right, block_row, block_col, dinv, blocks)
    lower = lax.ppermute(packed, "col", NEIGHBOURS)
    far = lower[-16:-15].astype(jnp.int32)
    lists = (block_row, block_col, far)

    held, rest = lax.optimization_barrier((over_z(spread), blocks[0, SLOTS1:].reshape(-1, SN)))
    sent = call(low_by_class, [((PEERS, 32, SN), BF16)], place, held)
    low = over_core(over_peers(sent))
    part = call(
        mid_sums,
        [((PEERS, 2 * STRIP, SN), BF16)],
        place,
        *lists,
        low,
        blocks,
        lower,
        right,
        scratch=work,
    )
    y_mid, spread = call(
        mid_forward,
        [((2 * STRIP, SN), BF16), ((Z, 2 * STRIP, SN), BF16)],
        place,
        over_peers(part),
        dinv,
    )
    upper, spread = lax.optimization_barrier((rest, spread))
    upper = lax.ppermute(upper, "col", NEIGHBOURS)
    mid = over_core(over_y(over_z_by_y(spread)))
    part = call(
        top_sums, [((PEERS, 16, SN), BF16)], *lists, low, mid, blocks, upper, scratch=work
    )
    x_top, spread = call(
        top_solve, [((16, SN), BF16), ((PEERS, 16, SN), BF16)], over_peers(part), right, dinv
    )
    low_part, keep, sent = call(
        top_carries,
        [
            ((LOWS, N, SN), F32),
            ((Y, 2 * STRIP, SN), F32),
            ((Y, 2 * STRIP, SN), BF16),
        ],
        place,
        *lists,
        over_peers(spread),
        blocks,
        upper,
        scratch=work,
    )
    both = call(pair_sum, [((Y, 2 * STRIP, SN), BF16)], keep, swap(sent))
    carry = over_z_by_y(over_y(both))
    spread = call(mid_backward, [((PEERS, 2 * STRIP, SN), BF16)], place, carry, y_mid, dinv)
    x_mid, keep, sent = call(
        low_carries,
        [((32, SN), BF16), ((PEERS, 32, SN), F32), ((PEERS, 32, SN), BF16)],
        place,
        *lists,
        over_peers(spread),
        low_part,
        blocks,
        lower,
        scratch=work,
    )
    both = call(pair_sum, [((PEERS, 32, SN), BF16)], keep, swap(sent))
    sent = call(low_by_row, [((Z, 64, SN), BF16)], place, over_peers(both))
    out = call(low_backward, [((W, OWN * SN), BF16)], over_z(sent), y_low, dinv, x_mid, x_top)
    return out.T


def solution(mesh):
    placed = (
        P("row", "col"),
        P("row", None, None),
        P("row", "col", None, None),
        P("row", "col"),
        P("row", "col"),
    )
    return jax.shard_map(
        on_device, mesh=mesh, in_specs=placed, out_specs=P("row", "col"), check_vma=False
    )
```

```python
import jax
import jax.numpy as jnp
from jax import lax
from jax.experimental import pallas as pl
from jax.experimental.pallas import tpu as pltpu
from jax.sharding import PartitionSpec as P

SN = 256
L0 = 8
L1 = 4
L2 = 2
MID = L0 + L1
OWN = L0 + L1 + L2
SLOTS1 = 8
SLOTS = 14
R = 16
C = 32
X = 4
Y = 8
Z = 8
HALVES = 2
PEERS = Y * HALVES
W = 8
STRIP = W * HALVES
N = W * PEERS
LOWS = 8
MIDS = 4
F32 = jnp.float32
BF16 = jnp.bfloat16
Z_GROUPS = [[2 * z + core for z in range(Z)] for core in range(2)]
CORE_GROUPS = [[2 * z, 2 * z + 1] for z in range(Z)]
Y_GROUPS = [[X * y + x for y in range(Y)] for x in range(X)]
PEER_GROUPS = [[2 * peer + (side + peer) % 2 for peer in range(PEERS)] for side in range(2)]
SWAP = [(r, r ^ 1) for r in range(R)]
NEIGHBOURS = [(c, c ^ 1) for c in range(C)]


def mid_groups():
    groups = []
    for core in range(2):
        for c in range(C):
            by_y = [0] * Y
            for z in range(Z):
                r = 2 * z + core
                column = [s % C for s in range(r * OWN + L0, r * OWN + MID) if s % X == c % X][0]
                by_y[column // X] = r * C + c
            groups.append(by_y)
    return groups


MID_GROUPS = mid_groups()


def dot_nt(left, right):
    return lax.dot_general(left, right, (((1,), (1,)), ((), ())), preferred_element_type=F32)


def dot_nn(left, right):
    return lax.dot_general(left, right, (((1,), (0,)), ((), ())), preferred_element_type=F32)


def low_panel(column):
    return column % (2 * OWN) // OWN * 4 + column % 2 * 2 + column % OWN // 4


def mid_panel(column):
    return column % (2 * OWN) // OWN * 2 + column % 2


def panel_of(column):
    return jnp.where(column % OWN < L0, low_panel(column), LOWS + mid_panel(column))


def join(pieces, out_ref, first=0):
    count = pieces.shape[1] // W
    wide = pieces.astype(F32).reshape(PEERS, count, W, SN)
    for i in range(count):
        out_ref[first + i] = wide[:, i].reshape(N, SN).astype(BF16)


def cut(panels, kind=BF16):
    parts = [p.reshape(PEERS, W, SN) for p in panels]
    return jnp.stack(parts, axis=1).reshape(PEERS, W * len(parts), SN).astype(kind)


def slots(row_ref, col_ref, far_ref, mine_ref, other_ref, first, final):
    for q in range(first, final):
        yield row_ref[0, q], col_ref[0, q], mine_ref[0, q]
    for q in range(first, final):
        tile = other_ref[(q - first) * SN : (q - first + 1) * SN]
        yield far_ref[0, q], far_ref[0, 128 + q], tile


def low_forward(
    rhs_ref, row_ref, col_ref, dinv_ref, blocks_ref, y_ref, spread_ref, sent_ref, factors, sems
):
    fetch = [pltpu.make_async_copy(dinv_ref.at[k], factors.at[k], sems.at[k]) for k in range(L0)]
    for copy in fetch:
        copy.start()
    pack = []
    for q in range(SLOTS1):
        target = sent_ref.at[pl.ds(q * SN, SN)]
        pack.append(pltpu.make_async_copy(blocks_ref.at[0, q], target, sems.at[L0 + q]))
    for copy in pack:
        copy.start()
    last = SLOTS1 * SN
    sent_ref[last:] = jnp.zeros((16, SN), BF16)
    sent_ref[last:, :SLOTS] = jnp.broadcast_to(row_ref[...].astype(F32), (16, SLOTS)).astype(BF16)
    sent_ref[last:, 128 : 128 + SLOTS] = jnp.broadcast_to(
        col_ref[...].astype(F32), (16, SLOTS)
    ).astype(BF16)
    rows = []
    for k in range(L0):
        fetch[k].wait()
        rows.append(dot_nt(rhs_ref[:, k * SN : (k + 1) * SN], factors[k]))
    y = jnp.concatenate(rows, axis=0).astype(BF16)
    y_ref[...] = y
    for z in range(Z):
        spread_ref[z] = y
    for copy in pack:
        copy.wait()


def low_by_class(place_ref, in_ref, out_ref):
    core = place_ref[0] % 2
    for c in range(C):
        halves = []
        for o in range(2):
            a = (c + 2 * core) % 4
            z = (7 * ((c - 14 * core - a - 4 * o + 64) // 4)) % Z
            tile = in_ref[z, 32 * o : 32 * o + 32].astype(F32)
            piece = jnp.where(a == 0, tile[0:8], tile[8:16])
            other = jnp.where(a == 2, tile[16:24], tile[24:32])
            halves.append(jnp.where(a < 2, piece, other))
        out_ref[c // 2, c % 2 * 16 : c % 2 * 16 + 16] = jnp.concatenate(halves, axis=0).astype(BF16)


def mid_sums(place_ref, row_ref, col_ref, far_ref, low_ref, mine_ref, other_ref, rhs_ref, out_ref, panels, acc):
    r = place_ref[0]
    own = pl.multiple_of(place_ref[1] // 2 * W, W)
    for p in range(2):
        join(low_ref[p], panels, 4 * p)
    acc[...] = jnp.zeros_like(acc)
    for i in range(L1):
        x = (r * OWN + L0 + i) % X
        acc[x, pl.ds(own, W)] = -rhs_ref[:, (L0 + i) * SN : (L0 + i + 1) * SN].astype(F32)
    for row, column, tile in slots(row_ref, col_ref, far_ref, mine_ref, other_ref, 0, SLOTS1):
        slot = jnp.where(row < OWN, (r * OWN + row) % X, X)
        source = jnp.minimum(panel_of(column), LOWS - 1)
        acc[slot] += dot_nt(panels[source], tile)
    for x in range(X):
        strips = acc[x].astype(BF16)
        for y in range(Y):
            out_ref[2 * y + x // 2, x % 2 * STRIP : x % 2 * STRIP + STRIP] = strips[y * STRIP :][:STRIP]


def mid_forward(place_ref, in_ref, dinv_ref, y_ref, spread_ref):
    right = -jnp.sum(in_ref[...].astype(F32), axis=0)
    rows = []
    for b in range(2):
        k = L0 + (place_ref[1] // 2 * 2 + b + 2 * place_ref[0]) % X
        rows.append(dot_nt(right[b * STRIP :][:STRIP].astype(BF16), dinv_ref[k]))
    y = jnp.concatenate(rows, axis=0).astype(BF16)
    y_ref[...] = y
    for z in range(Z):
        spread_ref[z] = y


def top_sums(row_ref, col_ref, far_ref, low_ref, mid_ref, mine_ref, other_ref, out_ref, panels, acc):
    for p in range(2):
        join(low_ref[p], panels, 4 * p)
        for b in range(2):
            for y in range(Y):
                strip = mid_ref[p, y, b * STRIP : (b + 1) * STRIP]
                panels[LOWS + 2 * p + b, y * STRIP : (y + 1) * STRIP] = strip
    acc[...] = jnp.zeros_like(acc)
    for row, column, tile in slots(row_ref, col_ref, far_ref, mine_ref, other_ref, SLOTS1, SLOTS):
        slot = jnp.where(row < OWN, row - MID, L2)
        source = panel_of(column)
        acc[slot] += dot_nt(panels[source], tile)
    out_ref[...] = cut([acc[i] for i in range(L2)])


def top_solve(in_ref, rhs_ref, dinv_ref, x_ref, spread_ref):
    sums = jnp.sum(in_ref[...].astype(F32), axis=0)
    rows = []
    for i in range(L2):
        k = MID + i
        right = rhs_ref[:, k * SN : (k + 1) * SN].astype(F32) - sums[i * W : (i + 1) * W]
        y = dot_nt(right.astype(BF16), dinv_ref[k]).astype(BF16)
        rows.append(dot_nn(y, dinv_ref[k]))
    x = jnp.concatenate(rows, axis=0).astype(BF16)
    x_ref[...] = x
    for peer in range(PEERS):
        spread_ref[peer] = x


def top_carries(
    place_ref, row_ref, col_ref, far_ref, in_ref, mine_ref, other_ref, low_ref, keep_ref, out_ref, known, acc
):
    core = place_ref[0] % 2
    join(in_ref[...], known)
    acc[...] = jnp.zeros_like(acc)
    for row, column, tile in slots(row_ref, col_ref, far_ref, mine_ref, other_ref, SLOTS1, SLOTS):
        source = jnp.clip(row - MID, 0, L2 - 1)
        slot = jnp.where(row < OWN, panel_of(column), LOWS + MIDS)
        acc[slot] += dot_nn(known[source], tile)
    for p in range(LOWS):
        low_ref[p] = acc[p]
    for b in range(2):
        keep = acc[LOWS + 2 * core + b]
        sent = acc[LOWS + 2 * (1 - core) + b].astype(BF16)
        for y in range(Y):
            keep_ref[y, b * STRIP : (b + 1) * STRIP] = keep[y * STRIP : (y + 1) * STRIP]
            out_ref[y, b * STRIP : (b + 1) * STRIP] = sent[y * STRIP : (y + 1) * STRIP]


def mid_backward(place_ref, in_ref, y_ref, dinv_ref, spread_ref):
    left = y_ref[...].astype(F32) - jnp.sum(in_ref[...].astype(F32), axis=0)
    rows = []
    for b in range(2):
        k = L0 + (place_ref[1] // 2 * 2 + b + 2 * place_ref[0]) % X
        rows.append(dot_nn(left[b * STRIP :][:STRIP].astype(BF16), dinv_ref[k]))
    x = jnp.concatenate(rows, axis=0).astype(BF16)
    for peer in range(PEERS):
        spread_ref[peer] = x


def low_carries(
    place_ref,
    row_ref,
    col_ref,
    far_ref,
    in_ref,
    part_ref,
    mine_ref,
    other_ref,
    x_ref,
    keep_ref,
    out_ref,
    known,
    acc,
):
    r = place_ref[0]
    peer = place_ref[1] // 2
    core = r % 2
    for x in range(X):
        for y in range(Y):
            strip = in_ref[2 * y + x // 2, x % 2 * STRIP : x % 2 * STRIP + STRIP]
            known[x, y * STRIP : (y + 1) * STRIP] = strip
    own = []
    for i in range(L1):
        x = (r * OWN + L0 + i) % X
        strips = in_ref[peer // 2 * 2 + x // 2].astype(F32)
        octet = jnp.where(x % 2 == 0, strips[:STRIP], strips[STRIP:])
        own.append(jnp.where(peer % 2 == 0, octet[:W], octet[W:]))
    x_ref[...] = jnp.concatenate(own, axis=0).astype(BF16)
    for p in range(LOWS):
        acc[p] = part_ref[p]
    acc[LOWS] = jnp.zeros((N, SN), F32)
    for row, column, tile in slots(row_ref, col_ref, far_ref, mine_ref, other_ref, 0, SLOTS1):
        source = (r * OWN + row) % X
        panel = jnp.minimum(panel_of(column), LOWS - 1)
        slot = jnp.where(row < OWN, panel, LOWS)
        acc[slot] += dot_nn(known[source], tile)
    keep_ref[...] = cut([acc[4 * core + i] for i in range(4)], F32)
    out_ref[...] = cut([acc[4 * (1 - core) + i] for i in range(4)])


def pair_sum(keep_ref, in_ref, out_ref):
    out_ref[...] = (keep_ref[...] + in_ref[...].astype(F32)).astype(BF16)


def low_by_row(place_ref, in_ref, out_ref):
    core = place_ref[0] % 2
    for z in range(Z):
        parts = []
        for k in range(L0):
            c = (28 * z + 14 * core + k) % C
            o = k // 4
            tile = in_ref[c // 2].astype(F32)
            parts.append(tile[(k % 2 * 2 + o) * W :][:W])
        out_ref[z] = jnp.concatenate(parts, axis=0).astype(BF16)


def low_backward(in_ref, y_ref, dinv_ref, mid_ref, top_ref, out_ref):
    carry = jnp.sum(in_ref[...].astype(F32), axis=0)
    left = (y_ref[...].astype(F32) - carry).reshape(L0, W, SN)
    for k in range(L0):
        out_ref[:, k * SN : (k + 1) * SN] = dot_nn(left[k].astype(BF16), dinv_ref[k]).astype(BF16)
    mid = mid_ref[...].astype(F32)
    for i in range(L1):
        out_ref[:, (L0 + i) * SN : (L0 + i + 1) * SN] = mid[i * W : (i + 1) * W].astype(BF16)
    top = top_ref[...].astype(F32)
    for i in range(L2):
        out_ref[:, (MID + i) * SN : (MID + i + 1) * SN] = top[i * W : (i + 1) * W].astype(BF16)


VM = pl.BlockSpec(memory_space=pltpu.VMEM)
SM = pl.BlockSpec(memory_space=pltpu.SMEM)


def call(kernel, outs, *args, scratch=()):
    single = len(outs) == 1
    shapes = [jax.ShapeDtypeStruct(shape, kind) for shape, kind in outs]
    return pl.pallas_call(
        kernel,
        out_shape=shapes[0] if single else shapes,
        in_specs=[SM if a.dtype == jnp.int32 else VM for a in args],
        out_specs=VM if single else [VM] * len(outs),
        scratch_shapes=list(scratch),
        compiler_params=pltpu.CompilerParams(vmem_limit_bytes=24 * 1024 * 1024),
    )(*args)


def over_peers(pieces):
    return lax.all_to_all(pieces, "col", 0, 0, tiled=True, axis_index_groups=PEER_GROUPS)


def over_y(pieces):
    return lax.all_to_all(pieces, "col", 0, 0, tiled=True, axis_index_groups=Y_GROUPS)


def over_z_by_y(pieces):
    return lax.all_to_all(pieces, ("row", "col"), 0, 0, tiled=True, axis_index_groups=MID_GROUPS)


def over_core(pieces):
    return lax.all_gather(pieces, "row", axis=0, axis_index_groups=CORE_GROUPS)


def swap(half):
    return lax.ppermute(half, "row", SWAP)


def over_z(pieces):
    return lax.all_to_all(pieces, "row", 0, 0, tiled=True, axis_index_groups=Z_GROUPS)


def on_device(rhs, dinv, blocks, block_row, block_col):
    place = jnp.stack([lax.axis_index("row"), lax.axis_index("col")]).astype(jnp.int32)
    right = rhs.T
    panels = pltpu.VMEM((LOWS + MIDS, N, SN), BF16)
    sums = pltpu.VMEM((LOWS + MIDS + 1, N, SN), F32)
    work = (panels, sums)
    whole = pl.BlockSpec(memory_space=pl.ANY)
    y_low, spread, packed = pl.pallas_call(
        low_forward,
        out_shape=[
            jax.ShapeDtypeStruct((64, SN), BF16),
            jax.ShapeDtypeStruct((Z, 64, SN), BF16),
            jax.ShapeDtypeStruct((SLOTS1 * SN + 16, SN), BF16),
        ],
        in_specs=[VM, VM, VM, whole, whole],
        out_specs=[VM, VM, VM],
        scratch_shapes=[
            pltpu.VMEM((L0, SN, SN), BF16),
            pltpu.SemaphoreType.DMA((L0 + SLOTS1,)),
        ],
        compiler_params=pltpu.CompilerParams(vmem_limit_bytes=63 * 1024 * 1024),
    )(right, block_row, block_col, dinv, blocks)
    lower = lax.ppermute(packed, "col", NEIGHBOURS)
    far = lower[-16:-15].astype(jnp.int32)
    lists = (block_row, block_col, far)

    held, rest = lax.optimization_barrier((over_z(spread), blocks[0, SLOTS1:].reshape(-1, SN)))
    sent = call(low_by_class, [((PEERS, 32, SN), BF16)], place, held)
    upper = lax.ppermute(rest, "col", NEIGHBOURS)
    low = over_core(over_peers(sent))
    part = call(
        mid_sums,
        [((PEERS, 2 * STRIP, SN), BF16)],
        place,
        *lists,
        low,
        blocks,
        lower,
        right,
        scratch=work,
    )
    y_mid, spread = call(
        mid_forward,
        [((2 * STRIP, SN), BF16), ((Z, 2 * STRIP, SN), BF16)],
        place,
        over_peers(part),
        dinv,
    )
    mid = over_core(over_y(over_z_by_y(spread)))
    part = call(
        top_sums, [((PEERS, 16, SN), BF16)], *lists, low, mid, blocks, upper, scratch=work
    )
    x_top, spread = call(
        top_solve, [((16, SN), BF16), ((PEERS, 16, SN), BF16)], over_peers(part), right, dinv
    )
    low_part, keep, sent = call(
        top_carries,
        [
            ((LOWS, N, SN), F32),
            ((Y, 2 * STRIP, SN), F32),
            ((Y, 2 * STRIP, SN), BF16),
        ],
        place,
        *lists,
        over_peers(spread),
        blocks,
        upper,
        scratch=work,
    )
    both = call(pair_sum, [((Y, 2 * STRIP, SN), BF16)], keep, swap(sent))
    carry = over_z_by_y(over_y(both))
    spread = call(mid_backward, [((PEERS, 2 * STRIP, SN), BF16)], place, carry, y_mid, dinv)
    x_mid, keep, sent = call(
        low_carries,
        [((32, SN), BF16), ((PEERS, 32, SN), F32), ((PEERS, 32, SN), BF16)],
        place,
        *lists,
        over_peers(spread),
        low_part,
        blocks,
        lower,
        scratch=work,
    )
    both = call(pair_sum, [((PEERS, 32, SN), BF16)], keep, swap(sent))
    sent = call(low_by_row, [((Z, 64, SN), BF16)], place, over_peers(both))
    out = call(low_backward, [((W, OWN * SN), BF16)], over_z(sent), y_low, dinv, x_mid, x_top)
    return out.T


def solution(mesh):
    placed = (
        P("row", "col"),
        P("row", None, None),
        P("row", "col", None, None),
        P("row", "col"),
        P("row", "col"),
    )
    return jax.shard_map(
        on_device, mesh=mesh, in_specs=placed, out_specs=P("row", "col"), check_vma=False
    )
```
